32 devices in a mesh: blocks: 8 (over y, x, core), group: 4 (over z).
Axes of the slice: x: 2, y: 2, z: 4, core: 2. Of those that a mesh axis runs over, the one named last changes fastest.
Arguments:
- ocean_state: float32 [36, 4, 64, 512], P(None, None, 'blocks', 'group'), may hold values from -6 to 6
- surface_height: float32 [64, 512], P('blocks', 'group'), may hold values from -6 to 6
- surface_damping: float32 [64, 512], P('blocks', 'group'), may hold values from 0.05 to 1
- land_mask: int32 [64, 512], P('blocks', 'group'), may hold values from 0 to 1, as said below
Outputs:
- new_state: float32 [36, 4, 64, 512], P(None, None, 'blocks', 'group')
- surface: float32 [64, 512], P('blocks', 'group')
The draws below stay inside these ranges and needn't reach their ends.
Inputs may be any that keep to these rules, and one draw needn't show every extreme that they name: `land_mask`: 1 marks an ocean cell.
All inputs are finite; a program needn't handle non-finite values.
Results may differ from the reference program's by a relative error of at most 0.0003.
Values sent between devices are 32-bit elements; how exact they have to be, the bound alone decides.
No kernel may reach another device: no remote copies, remote signals or barrier semaphores. Data moves between devices by JAX's collectives and lax.ppermute only.
A program may use at most 64 MiB of HBM per device.

```python
import math
import jax
import jax.numpy as jnp
from jax import lax

LEV = 36
ITERS = 3
NX = 64
NY = 512


def draw_ocean_state(key, part):
    shape = (LEV, 4, NX, NY)
    return jnp.clip(jax.random.normal(key, shape, jnp.float32), -4.0, 4.0)


def draw_land_mask(key, part):
    rows = jnp.arange(NX, dtype=jnp.int32)[:, None]
    limit = 256 + 768 * rows // NX
    picked = jax.random.randint(key, (NX, NY), 0, 1024, dtype=jnp.int32)
    return (picked < limit).astype(jnp.int32)


def shard_levels(stream_key, extent, cuts, low, high):
    level = 1.0
    for axis_at, shards_of in cuts:
        draws = jax.random.uniform(jax.random.fold_in(jax.random.fold_in(stream_key, 6), axis_at), (shards_of,), jnp.float32, low / len(cuts), high / len(cuts))
        level = level * jnp.repeat(jnp.exp(draws), extent[axis_at] // shards_of).reshape((-1,) + (1,) * (len(extent) - 1 - axis_at))
    return level


def bell_draw(rng, dims, scale, most, split=(), kind=jnp.bfloat16):
    loudness = shard_levels(rng, dims, split, -0.22, 0.18) if split else 1.0
    result = jax.random.normal(rng, dims, jnp.float32) * scale * loudness
    return jnp.minimum(jnp.maximum(result, -most), most).astype(kind)


def setup_inputs(seed: int = 0) -> dict:
    arg_keys = jax.random.split(jax.random.key(seed), 5)
    return {
        "ocean_state": draw_ocean_state(jax.random.fold_in(arg_keys[4], 71), 0),
        "surface_height": bell_draw(arg_keys[1], (NX, NY), 1.0, 6.0, ((0, 8), (1, 4)), jnp.float32),
        "surface_damping": jnp.clip(jnp.exp(math.log(1.0) - 2.9957323 * jax.random.uniform(arg_keys[2], (NX, NY), jnp.float32) ** shard_levels(arg_keys[2], (NX, NY), ((0, 8), (1, 4)), -0.2, 0.2)), 0.05, 1.0),
        "land_mask": draw_land_mask(jax.random.fold_in(arg_keys[4], 71), 0),
    }


time_step = 0.25
hyper_visc = 0.025
mixing = 0.2
gravity = 4.0
rotation = 0.2


def laplace(padded):
    return (padded[..., 2:, 1:-1] + padded[..., :-2, 1:-1] + padded[..., 1:-1, 2:] + padded[..., 1:-1, :-2]) - 4.0 * padded[..., 1:-1, 1:-1]


def pad_plane(values):
    return jnp.pad(values, [(0, 0)] * (values.ndim - 2) + [(1, 1), (1, 1)])


def level_update(level_now, level_above, level_below, sea_mask, coriolis):
    padded = pad_plane(level_now)
    lap_once = laplace(padded)
    biharm = laplace(pad_plane(lap_once))
    slope_east = 0.5 * (padded[:, 2:, 1:-1] - padded[:, :-2, 1:-1])
    slope_north = 0.5 * (padded[:, 1:-1, 2:] - padded[:, 1:-1, :-2])
    east_flow = level_now[2:3]
    north_flow = level_now[3:4]
    advect = east_flow * slope_east + north_flow * slope_north
    vertical = level_above + level_below - 2.0 * level_now
    zeros_two = jnp.zeros_like(level_now[0:2])
    rotated = jnp.concatenate([zeros_two, coriolis * north_flow, -coriolis * east_flow], axis=0)
    updated = level_now + time_step * (rotated - advect) - hyper_visc * biharm + mixing * vertical
    return sea_mask * updated


def surface_operator(surface_field, damping, sea_mask):
    padded = jnp.pad(surface_field, 1)
    beside = padded[2:, 1:-1] + padded[:-2, 1:-1] + padded[1:-1, 2:] + padded[1:-1, :-2]
    return sea_mask * ((4.0 + damping) * surface_field - beside)


def reference(ocean_state, surface_height, surface_damping, land_mask):
    sea_mask = land_mask.astype(jnp.float32)
    masked = ocean_state * sea_mask
    coriolis = rotation * (2.0 * (jnp.arange(NY).astype(jnp.float32) + 0.5) / NY - 1.0)

    def one_level(level):
        above = jnp.maximum(level - 1, 0).astype(jnp.int32)
        below = jnp.minimum(level + 1, LEV - 1).astype(jnp.int32)
        return level_update(masked[level], masked[above], masked[below], sea_mask, coriolis)

    new_state = lax.map(one_level, jnp.arange(LEV, dtype=jnp.int32))
    transport = jnp.sum(new_state[:, 2:4], axis=0) / LEV
    padded = pad_plane(transport)
    divergence = 0.5 * (padded[0, 2:, 1:-1] - padded[0, :-2, 1:-1] + padded[1, 1:-1, 2:] - padded[1, 1:-1, :-2])
    right_side = sea_mask * (surface_damping * surface_height - gravity * divergence)
    solution = jnp.zeros_like(right_side)
    residual = right_side
    direction = right_side
    norm_now = jnp.sum(residual * residual)
    for iteration in range(ITERS):
        applied = surface_operator(direction, surface_damping, sea_mask)
        step_size = norm_now / jnp.sum(direction * applied)
        solution = solution + step_size * direction
        residual = residual - step_size * applied
        norm_next = jnp.sum(residual * residual)
        direction = residual + (norm_next / norm_now) * direction
        norm_now = norm_next
    return new_state, solution
```

```python
import jax
import jax.numpy as jnp
from jax import lax
from jax.experimental import pallas as pl
from jax.experimental.pallas import tpu as pltpu
from jax.sharding import PartitionSpec as P

ITERS = 3

time_step = 0.25
hyper_visc = 0.025
mixing = 0.2
gravity = 4.0
rotation = 0.2

COMPS = 4
ROWS = 8
LANES = 128
SLOT = 8
PER = LANES // SLOT
EXT = 12
F32 = jnp.float32
VMEM = pl.BlockSpec(memory_space=pltpu.VMEM)


def iota(axis):
    return lax.broadcasted_iota(jnp.int32, (ROWS, LANES), axis)


def roll(x, shift, axis):
    return pltpu.roll(x, shift % x.shape[axis], axis)


def swap_pairs(mesh_shape, along):
    nb, ng = mesh_shape
    first, second = [], []
    for b in range(nb):
        for g in range(ng):
            me = b * ng + g
            if along == "blocks":
                one = (b ^ 1, g)
                two = ((b - 1) ^ 1) + 1
                two = (two, g) if 0 <= two < nb else (b, g ^ 1)
            else:
                one = (b, g ^ 1)
                two = ((g - 1) ^ 1) + 1
                two = (b, two) if 0 <= two < ng else (b ^ 1, g)
            first.append((me, one[0] * ng + one[1]))
            second.append((me, two[0] * ng + two[1]))
    return first, second


def pack_kernel(state_ref, mask_ref, m_ref, pack_ref):
    sea = mask_ref[...].astype(F32)
    slot = iota(1) // SLOT
    tiles = state_ref.shape[0] // ROWS
    for p in range(tiles // PER):
        acc = jnp.zeros((ROWS, LANES), F32)
        for q in range(PER):
            at = pl.ds((p * PER + q) * ROWS, ROWS)
            x = state_ref[at, :] * sea
            m_ref[at, :] = x
            acc = jnp.where(slot == q, roll(x, SLOT * q + SLOT // 2, 1), acc)
        pack_ref[pl.ds(p * ROWS, ROWS), :] = acc


def edge_kernel(m_ref, pack_ref, first_ref, second_ref, delta_ref, one_ref, two_ref):
    g = lax.axis_index("group")
    ng = lax.axis_size("group")
    geven = lax.rem(g, 2) == 0
    beven = lax.rem(lax.axis_index("blocks"), 2) == 0
    half = lax.rem(iota(1), SLOT) < SLOT // 2
    has_left = (g > 0).astype(F32)
    has_right = (g < ng - 1).astype(F32)
    packs = pack_ref.shape[0] // ROWS
    eights = m_ref.shape[0] // 64
    base = one_ref.shape[0] - 2 * ROWS
    for p in range(packs):
        at = pl.ds(p * ROWS, ROWS)
        first, second = first_ref[at, :], second_ref[at, :]
        from_left = jnp.where(geven, second, first) * has_left
        from_right = jnp.where(geven, first, second) * has_right
        delta_ref[at, :] = jnp.where(half, from_left, from_right) - pack_ref[at, :]

    def fill(low_ref, high_ref):
        for r in range(2):
            for s in range(eights):
                at = pl.ds((r * eights + s) * ROWS, ROWS)
                low_ref[at, :] = m_ref[pl.ds(64 * s + r, ROWS, stride=ROWS), :]
                high_ref[at, :] = m_ref[pl.ds(64 * s + 6 + r, ROWS, stride=ROWS), :]
        for p in range(packs):
            low_ref[pl.ds(base + p, 1), :] = delta_ref[pl.ds(ROWS * p, 1), :]
            high_ref[pl.ds(base + p, 1), :] = delta_ref[pl.ds(ROWS * p + ROWS - 1, 1), :]

    pl.when(beven)(lambda: fill(two_ref, one_ref))
    pl.when(jnp.logical_not(beven))(lambda: fill(one_ref, two_ref))


def step_kernel(
    m_ref, pack_ref, delta_ref, one_ref, two_ref, mask_ref, height_ref, damp_ref, new_ref, field_ref, ext_ref, corr_ref
):
    b, nb = lax.axis_index("blocks"), lax.axis_size("blocks")
    g, ng = lax.axis_index("group"), lax.axis_size("group")
    even = lax.rem(b, 2) == 0
    has_up = (b > 0).astype(F32)
    has_down = (b < nb - 1).astype(F32)
    row, lane = iota(0), iota(1)
    tiles = m_ref.shape[0] // ROWS
    levels = tiles // COMPS
    eights = tiles // ROWS
    packs = tiles // PER
    base = one_ref.shape[0] - 2 * ROWS

    for t in range(tiles):
        ext_ref[pl.ds(EXT * t + 2, ROWS), :] = m_ref[pl.ds(ROWS * t, ROWS), :]
    for r in range(2):
        for s in range(eights):
            at = pl.ds((r * eights + s) * ROWS, ROWS)
            one, two = one_ref[at, :], two_ref[at, :]
            up = jnp.where(even, two, one) * has_up
            down = jnp.where(even, one, two) * has_down
            ext_ref[pl.ds(EXT * ROWS * s + r, ROWS, stride=EXT), :] = up
            ext_ref[pl.ds(EXT * ROWS * s + 10 + r, ROWS, stride=EXT), :] = down

    in_slot = lax.rem(lane, SLOT)
    left_half = in_slot < SLOT // 2
    comp = lax.rem(lane // SLOT, COMPS)
    near = (in_slot == 3) | (in_slot == 4)
    far = (in_slot >= 2) & (in_slot <= 5)
    sign = jnp.where(in_slot == 3, -0.5 * time_step, jnp.where(in_slot == 4, 0.5 * time_step, 0.0))
    for p in range(packs):
        at = pl.ds(p * ROWS, ROWS)
        d = delta_ref[at, :]
        one, two = one_ref[pl.ds(base + p, 1), :], two_ref[pl.ds(base + p, 1), :]
        up = jnp.where(even, two, one) * has_up
        down = jnp.where(even, one, two) * has_down
        dv = jnp.where(row == 0, up, roll(d, 1, 0)) + jnp.where(row == ROWS - 1, down, roll(d, -1, 0))
        x2 = jnp.where(left_half, roll(d, -2, 1), roll(d, 2, 1))
        x1 = jnp.where(left_half, roll(d, -1, 1), roll(d, 1, 1))
        y = 2.0 * dv - 8.0 * d
        y1 = jnp.where(left_half, roll(y, -1, 1), roll(y, 1, 1))
        own = pack_ref[at, :]
        v = own
        for c in range(3):
            v = jnp.where(comp == c, roll(own, -SLOT * (3 - c), 1), v)
        corr_ref[at, :] = (
            jnp.where(far, -hyper_visc * x2, 0.0) + jnp.where(near, -hyper_visc * y1, 0.0) + sign * v * x1
        )

    sea = mask_ref[...].astype(F32)
    edge_rows = jnp.where((row == 0) & (b == 0), 1.0, 0.0) + jnp.where((row == ROWS - 1) & (b == nb - 1), 1.0, 0.0)
    edge_cols = jnp.where((lane == 0) & (g == 0), 1.0, 0.0) + jnp.where((lane == LANES - 1) & (g == ng - 1), 1.0, 0.0)
    centre = 1.0 - 2.0 * mixing + hyper_visc * (edge_rows + edge_cols)
    col = (lane + g * LANES).astype(F32)
    coriolis = time_step * rotation * (2.0 * (col + 0.5) / (ng * LANES) - 1.0)
    border = (lane < SLOT // 2) | (lane >= LANES - SLOT // 2)
    sums = [jnp.zeros((ROWS, LANES), F32) for _ in range(2)]

    def own(level, c):
        level = min(max(level, 0), levels - 1)
        return m_ref[pl.ds(ROWS * (COMPS * level + c), ROWS), :]

    for k in range(levels):
        u, v = own(k, 2), own(k, 3)
        for c in range(COMPS):
            t = COMPS * k + c
            x = own(k, c)
            up2 = ext_ref[pl.ds(EXT * t, ROWS), :]
            up1 = ext_ref[pl.ds(EXT * t + 1, ROWS), :]
            dn1 = ext_ref[pl.ds(EXT * t + 3, ROWS), :]
            dn2 = ext_ref[pl.ds(EXT * t + 4, ROWS), :]
            left, right = roll(x, 1, 1), roll(x, -1, 1)
            near1 = up1 + dn1
            q = (left + right) + 2.0 * near1 - 6.0 * x
            biharm = (roll(q, 1, 1) + roll(q, -1, 1)) - 2.0 * q + (up2 + dn2) - 4.0 * near1 + 6.0 * x
            advect = u * (dn1 - up1) + v * (right - left)
            out = centre * x - hyper_visc * biharm - 0.5 * time_step * advect + mixing * (own(k - 1, c) + own(k + 1, c))
            if c == 2:
                out = out + coriolis * v
            if c == 3:
                out = out - coriolis * u
            p, s = divmod(t, PER)
            fix = roll(corr_ref[pl.ds(p * ROWS, ROWS), :], -(SLOT * s + SLOT // 2), 1)
            out = sea * (out + jnp.where(border, fix, 0.0))
            new_ref[pl.ds(ROWS * t, ROWS), :] = out
            if c >= 2:
                sums[c - 2] = sums[c - 2] + out
    field_ref[0:8, :] = sums[0] / levels
    field_ref[8:16, :] = sums[1] / levels
    field_ref[16:24, :] = sea * damp_ref[...] * height_ref[...]
    field_ref[24:32, :] = sea * (4.0 + damp_ref[...])


def call(kernel, outs, *args, scratch=(), flops=0):
    return pl.pallas_call(
        kernel,
        out_shape=[jax.ShapeDtypeStruct(s, F32) for s in outs],
        in_specs=[VMEM] * len(args),
        out_specs=[VMEM] * len(outs),
        scratch_shapes=[pltpu.VMEM(s, F32) for s in scratch],
        compiler_params=pltpu.CompilerParams(vmem_limit_bytes=32 * 1024 * 1024),
        cost_estimate=pl.CostEstimate(flops=flops, bytes_accessed=0, transcendentals=0),
    )(*args)


def on_device(ocean_state, surface_height, surface_damping, land_mask, *, shape):
    nb, ng = shape
    axes = ("blocks", "group")
    levels = ocean_state.shape[0]
    tiles = levels * COMPS
    state = ocean_state.reshape(tiles * ROWS, LANES)
    g_one, g_two = swap_pairs(shape, "group")
    b_one, b_two = swap_pairs(shape, "blocks")
    packs = tiles // PER

    m, pack = call(pack_kernel, [state.shape, (packs * ROWS, LANES)], state, land_mask)
    first = lax.ppermute(pack, axes, g_one)
    second = lax.ppermute(pack, axes, g_two)
    message = (tiles * 2 + 2 * ROWS, LANES)
    delta, one, two = call(edge_kernel, [pack.shape, message, message], m, pack, first, second)
    one = lax.ppermute(one, axes, b_one)
    two = lax.ppermute(two, axes, b_two)
    new_state, fields = call(
        step_kernel,
        [state.shape, (4 * ROWS, LANES)],
        m,
        pack,
        delta,
        one,
        two,
        land_mask,
        surface_height,
        surface_damping,
        scratch=[(tiles * EXT, LANES), pack.shape],
    )
    whole = lax.all_to_all(jnp.broadcast_to(fields[None], (nb * ng,) + fields.shape), axes, 0, 0)
    whole = whole.reshape(nb, ng, 4, ROWS, LANES).transpose(2, 0, 3, 1, 4).reshape(4, nb * ROWS, ng * LANES)
    east, north, forced, diagonal = whole[0], whole[1], whole[2], whole[3]
    sea = (diagonal > 0).astype(F32)

    def shifts(f):
        f = jnp.pad(f, 1)
        return f[2:, 1:-1], f[:-2, 1:-1], f[1:-1, 2:], f[1:-1, :-2]

    e, n = shifts(east), shifts(north)
    direction = forced - gravity * sea * (0.5 * (e[0] - e[1] + n[2] - n[3]))
    residual = direction
    total = jnp.zeros_like(direction)
    norm = jnp.sum(residual * residual)
    for iteration in range(ITERS):
        image = diagonal * direction - sea * sum(shifts(direction))
        alpha = norm / jnp.sum(direction * image)
        total = total + alpha * direction
        residual = residual - alpha * image
        following = jnp.sum(residual * residual)
        direction = residual + following / norm * direction
        norm = following
    b, g = lax.axis_index("blocks"), lax.axis_index("group")
    surface = lax.dynamic_slice(total, (b * ROWS, g * LANES), (ROWS, LANES))
    return new_state.reshape(ocean_state.shape), surface


def solution(mesh):
    placed = (
        P(None, None, "blocks", "group"),
        P("blocks", "group"),
        P("blocks", "group"),
        P("blocks", "group"),
    )
    shape = (mesh.shape["blocks"], mesh.shape["group"])

    def body(*args):
        return on_device(*args, shape=shape)

    return jax.shard_map(
        body,
        mesh=mesh,
        in_specs=placed,
        out_specs=(P(None, None, "blocks", "group"), P("blocks", "group")),
        check_vma=False,
    )
```

```python
import jax
import jax.numpy as jnp
from jax import lax
from jax.experimental import pallas as pl
from jax.experimental.pallas import tpu as pltpu
from jax.sharding import PartitionSpec as P

ITERS = 3

time_step = 0.25
hyper_visc = 0.025
mixing = 0.2
gravity = 4.0
rotation = 0.2

COMPS = 4
ROWS = 8
LANES = 128
SLOT = 8
PER = LANES // SLOT
EXT = 12
FLAT = 6
STRIP = 16
SHIFT = 4.5
F32 = jnp.float32
VMEM = pl.BlockSpec(memory_space=pltpu.VMEM)
HBM = pl.BlockSpec(memory_space=pltpu.HBM)


def iota(axis, rows=ROWS, lanes=LANES):
    return lax.broadcasted_iota(jnp.int32, (rows, lanes), axis)


def roll(x, shift, axis):
    return pltpu.roll(x, shift % x.shape[axis], axis)


def tile(k):
    return pl.ds(k * ROWS, ROWS)


def swap_pairs(mesh_shape, along):
    nb, ng = mesh_shape
    first, second = [], []
    for b in range(nb):
        for g in range(ng):
            me = b * ng + g
            if along == "blocks":
                one = (b ^ 1, g)
                two = ((b - 1) ^ 1) + 1
                two = (two, g) if 0 <= two < nb else (b, g ^ 1)
            else:
                one = (b, g ^ 1)
                two = ((g - 1) ^ 1) + 1
                two = (b, two) if 0 <= two < ng else (b ^ 1, g)
            first.append((me, one[0] * ng + one[1]))
            second.append((me, two[0] * ng + two[1]))
    return first, second


class Layout:
    def __init__(self, tiles):
        self.tiles = tiles
        self.levels = tiles // COMPS
        self.packs = tiles // PER
        self.eights = tiles // ROWS
        self.pad = -(-self.packs // ROWS) * ROWS
        self.edge = 2 * tiles
        self.delta = self.edge + self.pad
        self.flat = self.delta + self.pad
        self.strip = self.flat + FLAT * ROWS
        self.rows = self.strip + ROWS


class Place:
    def __init__(self):
        self.b, self.nb = lax.axis_index("blocks"), lax.axis_size("blocks")
        self.g, self.ng = lax.axis_index("group"), lax.axis_size("group")
        self.b_even = lax.rem(self.b, 2) == 0
        self.g_even = lax.rem(self.g, 2) == 0
        self.up = (self.b > 0).astype(F32)
        self.down = (self.b < self.nb - 1).astype(F32)
        self.left = (self.g > 0).astype(F32)
        self.right = (self.g < self.ng - 1).astype(F32)

    def from_up(self, one, two):
        return jnp.where(self.b_even, two, one) * self.up

    def from_down(self, one, two):
        return jnp.where(self.b_even, one, two) * self.down


def pack_kernel(
    state_hbm, mask_hbm, height_hbm, damp_hbm, m_ref, pack_ref, flat_ref, state_ref, mask_ref, height_ref, damp_ref, sems
):
    lay = Layout(m_ref.shape[0] // ROWS)
    chunk = PER * ROWS
    small = [(mask_hbm, mask_ref), (height_hbm, height_ref), (damp_hbm, damp_ref)]
    copies = [pltpu.make_async_copy(a, b, sems.at[k]) for k, (a, b) in enumerate(small)]
    for p in range(lay.packs):
        at = pl.ds(p * chunk, chunk)
        copies.append(pltpu.make_async_copy(state_hbm.at[at], state_ref.at[at], sems.at[3 + p]))
    for copy in copies:
        copy.start()
    for copy in copies[:3]:
        copy.wait()
    sea = mask_ref[...].astype(F32)
    row, lane = iota(0), iota(1)
    slot = lane // SLOT
    sums = [jnp.zeros((ROWS, LANES), F32) for _ in range(4)]
    for p in range(lay.packs):
        copies[3 + p].wait()
        acc = jnp.zeros((ROWS, LANES), F32)
        for k in range(PER // COMPS):
            x = []
            for c in range(COMPS):
                q = COMPS * k + c
                x.append(state_ref[tile(p * PER + q), :] * sea)
                m_ref[tile(p * PER + q), :] = x[c]
                acc = jnp.where(slot == q, roll(x[c], SLOT * q + SLOT // 2, 1), acc)
            u_up, u_down = jnp.where(row == 0, 0.0, x[2]), jnp.where(row == ROWS - 1, 0.0, x[2])
            v_left, v_right = jnp.where(lane == 0, 0.0, x[3]), jnp.where(lane == LANES - 1, 0.0, x[3])
            for f in range(2):
                y = x[2 + f]
                sums[f] = sums[f] + y
                sums[2 + f] = sums[2 + f] + (
                    (u_down * roll(y, -1, 0) - u_up * roll(y, 1, 0))
                    + (v_right * roll(y, -1, 1) - v_left * roll(y, 1, 1))
                )
        pack_ref[tile(p), :] = acc
    damp = damp_ref[...]
    flat = [sums[0], sums[1], 0.5 * sums[2], 0.5 * sums[3], sea * damp * height_ref[...], sea * (4.0 + damp)]
    acc = jnp.zeros((ROWS, LANES), F32)
    for f in range(FLAT):
        flat_ref[tile(f), :] = flat[f]
        acc = jnp.where(lane // STRIP == f, roll(flat[f], STRIP * f + STRIP // 2, 1), acc)
    pack_ref[tile(lay.packs), :] = acc


def spread(x, of):
    comp = lax.rem(lax.broadcasted_iota(jnp.int32, x.shape, 1) // SLOT, COMPS)
    out = x
    for c in range(COMPS):
        if c != of:
            out = jnp.where(comp == c, roll(x, SLOT * (c - of), 1), out)
    return out


def across(x):
    half = lax.rem(lax.broadcasted_iota(jnp.int32, x.shape, 1), SLOT) < SLOT // 2
    return jnp.where(half, roll(x, -1, 1), roll(x, 1, 1))


def fold(x):
    step = SLOT * COMPS
    while step < LANES:
        x = x + roll(x, step, 1)
        step *= 2
    return x


def edge_kernel(m_ref, pack_ref, flat_ref, first_ref, second_ref, own_ref, near_ref, delta_ref, one_ref, two_ref):
    lay = Layout(m_ref.shape[0] // ROWS)
    at = Place()
    lane = iota(1)
    in_slot = lax.rem(lane, SLOT)
    half = in_slot < SLOT // 2
    sign = jnp.where(in_slot == SLOT // 2 - 1, 0.5, jnp.where(in_slot == SLOT // 2, -0.5, 0.0))

    def beyond(p, low):
        first, second = first_ref[tile(p), :], second_ref[tile(p), :]
        from_left = jnp.where(at.g_even, second, first) * at.left
        from_right = jnp.where(at.g_even, first, second) * at.right
        return jnp.where(low, from_left, from_right)

    near_ref[...] = jnp.zeros(near_ref.shape, F32)
    inner = jnp.zeros((ROWS, LANES), F32)
    outer = jnp.zeros((ROWS, LANES), F32)
    for p in range(lay.packs):
        own, far = pack_ref[tile(p), :], beyond(p, half)
        delta_ref[tile(p), :] = far - own
        near_ref[p : p + 1, :] = far[0:1]
        near_ref[lay.pad + p : lay.pad + p + 1, :] = far[ROWS - 1 : ROWS]
        inner = inner + spread(own, 3) * across(far)
        outer = outer + spread(far, 3) * across(own)
    inner, outer = fold(sign * inner), fold(sign * outer)
    strip = beyond(lay.packs, lax.rem(lane, STRIP) < STRIP // 2)
    for f in range(FLAT):
        value = flat_ref[tile(f), :]
        if 2 <= f <= 3:
            border = (lane == 0) | (lane == LANES - 1)
            value = value + jnp.where(border, roll(inner, -(SLOT * f + SLOT // 2), 1), 0.0)
            mid = STRIP * f + STRIP // 2
            border = (lane == mid - 1) | (lane == mid)
            strip = strip + jnp.where(border, roll(outer, mid - (SLOT * f + SLOT // 2), 1), 0.0)
        own_ref[tile(f), :] = value
    own_ref[tile(FLAT), :] = strip

    def fill(low_ref, high_ref):
        for r in range(2):
            for s in range(lay.eights):
                to = tile(r * lay.eights + s)
                low_ref[to, :] = m_ref[pl.ds(ROWS * ROWS * s + r, ROWS, stride=ROWS), :]
                high_ref[to, :] = m_ref[pl.ds(ROWS * ROWS * s + ROWS - 2 + r, ROWS, stride=ROWS), :]
        low_ref[pl.ds(lay.edge, lay.pad), :] = near_ref[0 : lay.pad, :]
        high_ref[pl.ds(lay.edge, lay.pad), :] = near_ref[lay.pad :, :]
        for ref in (low_ref, high_ref):
            ref[pl.ds(lay.delta, lay.pad), :] = jnp.zeros((lay.pad, LANES), F32)
            ref[pl.ds(lay.flat, (FLAT + 1) * ROWS), :] = own_ref[...]
        for p in range(lay.packs):
            low_ref[pl.ds(lay.delta + p, 1), :] = delta_ref[pl.ds(ROWS * p, 1), :]
            high_ref[pl.ds(lay.delta + p, 1), :] = delta_ref[pl.ds(ROWS * p + ROWS - 1, 1), :]

    pl.when(at.b_even)(lambda: fill(two_ref, one_ref))
    pl.when(jnp.logical_not(at.b_even))(lambda: fill(one_ref, two_ref))


def moment_kernel(m_ref, own_ref, near_ref, one_ref, two_ref, basis_ref, send_ref, wide_ref):
    lay = Layout(m_ref.shape[0] // ROWS)
    at = Place()
    row, lane = iota(0), iota(1)
    outside = (lane < STRIP // 2) | (lane >= LANES - STRIP // 2)
    rows = 3 * ROWS

    def neighbours(where):
        return at.from_up(one_ref[where, :], two_ref[where, :]), at.from_down(one_ref[where, :], two_ref[where, :])

    strips = neighbours(pl.ds(lay.strip, ROWS))
    strips = (strips[0], own_ref[tile(FLAT), :], strips[1])
    for f in range(FLAT):
        fields = neighbours(pl.ds(lay.flat + f * ROWS, ROWS))
        fields = (fields[0], own_ref[tile(f), :], fields[1])
        for k in range(3):
            to = pl.ds(f * rows + k * ROWS, ROWS)
            wide_ref[to, 0:LANES] = fields[k]
            side = roll(strips[k], -(STRIP * f + STRIP // 2), 1)
            wide_ref[to, LANES : 2 * LANES] = jnp.where(outside, side, 0.0)

    comp = lax.rem(row, COMPS)
    cross = [jnp.zeros((ROWS, LANES), F32) for _ in range(4)]
    for s in range(lay.eights):
        above = neighbours(tile(lay.eights + s))[0]
        below = neighbours(tile(s))[1]
        top = m_ref[pl.ds(ROWS * ROWS * s, ROWS, stride=ROWS), :]
        bottom = m_ref[pl.ds(ROWS * ROWS * s + ROWS - 1, ROWS, stride=ROWS), :]

        def flow(x):
            return jnp.where(comp == 3, roll(x, 1, 0), x)

        cross[0] = cross[0] + flow(above) * top
        cross[1] = cross[1] - flow(top) * above
        cross[2] = cross[2] + flow(bottom) * below
        cross[3] = cross[3] - flow(below) * bottom
    cross = [0.5 * (x + roll(x, COMPS, 0)) for x in cross]
    above, below = neighbours(pl.ds(lay.edge, lay.pad))
    top, bottom = near_ref[0 : lay.pad, :], near_ref[lay.pad :, :]

    def flow_packed(x):
        return roll(x, SLOT, 1)

    def corner(a, b):
        comp = lax.rem(iota(1, lay.pad) // SLOT, COMPS)
        x = jnp.where(comp == 3, flow_packed(a), a) * b
        return 0.5 * fold(jnp.sum(x, axis=0, keepdims=True))

    corners = [corner(above, top), -corner(top, above), corner(bottom, below), -corner(below, bottom)]
    border = (iota(1, 1) < SLOT // 2) | (iota(1, 1) >= LANES - SLOT // 2)
    for f in (2, 3):
        for k, at_row in enumerate((ROWS - 1, ROWS, 2 * ROWS - 1, 2 * ROWS)):
            to = pl.ds(f * rows + at_row, 1)
            wide_ref[to, 0:LANES] = wide_ref[to, 0:LANES] + cross[k][f : f + 1]
            side = roll(corners[k], -(SLOT * f + SLOT // 2), 1)
            wide_ref[to, LANES : 2 * LANES] = wide_ref[to, LANES : 2 * LANES] + jnp.where(border, side, 0.0)

    sum_u, sum_v, adv_u, adv_v, forcing, diagonal = [wide_ref[pl.ds(f * rows, rows), :] for f in range(FLAT)]
    sea = jnp.where(diagonal > 0.0, 1.0, 0.0)
    shape = (rows, 2 * LANES)
    i = iota(0, *shape) - ROWS + at.b * ROWS
    j = iota(1, *shape)
    j = jnp.where(j < LANES + LANES // 2, j, j - 2 * LANES) + at.g * LANES
    total_rows, total_cols = at.nb * ROWS, at.ng * LANES
    edges = (
        jnp.where(i == 0, 1.0, 0.0)
        + jnp.where(i == total_rows - 1, 1.0, 0.0)
        + jnp.where(j == 0, 1.0, 0.0)
        + jnp.where(j == total_cols - 1, 1.0, 0.0)
    )
    coriolis = rotation * (2.0 * (j.astype(F32) + 0.5) / total_cols - 1.0)

    def both(x, n, axis):
        return roll(x, n, axis) + roll(x, -n, axis)

    def transport(x, turn, adv):
        near = both(x, 1, 0)
        linear = (
            (1.0 - hyper_visc * (20.0 - edges)) * x
            + 8.0 * hyper_visc * near
            - hyper_visc * (both(x, 2, 0) + both(x, 2, 1))
            + both(8.0 * hyper_visc * x - 2.0 * hyper_visc * near, 1, 1)
        )
        return sea * (linear + time_step * (turn - adv)) / lay.levels

    east = transport(sum_u, coriolis * sum_v, adv_u)
    north = transport(sum_v, -coriolis * sum_u, adv_v)
    divergence = 0.5 * (roll(east, -1, 0) - roll(east, 1, 0) + roll(north, -1, 1) - roll(north, 1, 1))
    v = [forcing - gravity * sea * divergence]
    own_diagonal = diagonal - SHIFT
    for _ in range(ITERS):
        x = v[-1]
        v.append(own_diagonal * x - sea * (both(x, 1, 0) + both(x, 1, 1)))
    v = [x[ROWS : 2 * ROWS, 0:LANES] for x in v]
    for k in range(ITERS):
        basis_ref[tile(k), :] = v[k]
    line = jnp.zeros((ROWS, LANES), F32)
    for k in range(2 * ITERS):
        part = jnp.sum(v[k // 2] * v[k - k // 2], axis=0, keepdims=True)
        line = jnp.where(row == k, part, line)
    line = jnp.sum(line, axis=1, keepdims=True)
    line = jnp.sum(jnp.where(row == lane, line, 0.0), axis=0, keepdims=True)
    send_ref[...] = jnp.broadcast_to(line, send_ref.shape)


def solve_kernel(got_ref, basis_ref, out_ref):
    line = jnp.sum(got_ref[...], axis=0, keepdims=True)
    lane = iota(1, 1)
    moment = [jnp.sum(jnp.where(lane == k, line, 0.0), axis=1, keepdims=True) for k in range(2 * ITERS)]

    def dot(a, b):
        total = None
        for k in range(len(a) + len(b) - 1):
            weight = sum(a[n] * b[k - n] for n in range(len(a)) if 0 <= k - n < len(b))
            total = weight * moment[k] if total is None else total + weight * moment[k]
        return total

    def add(a, scale, b):
        out = list(a) + [0.0] * (len(b) - len(a))
        return [x + scale * b[n] if n < len(b) else x for n, x in enumerate(out)]

    def image(a):
        return [SHIFT * (a[n] if n < len(a) else 0.0) + (a[n - 1] if n else 0.0) for n in range(len(a) + 1)]

    one = jnp.ones((1, 1), F32)
    residual, direction, surface = [one], [one], []
    norm = dot(residual, residual)
    for iteration in range(ITERS):
        applied = image(direction)
        alpha = norm / dot(direction, applied)
        surface = add(surface, alpha, direction)
        if iteration + 1 < ITERS:
            residual = add(residual, -alpha, applied)
            following = dot(residual, residual)
            direction = add(residual, following / norm, direction)
            norm = following
    out = surface[0] * basis_ref[tile(0), :]
    for k in range(1, ITERS):
        out = out + surface[k] * basis_ref[tile(k), :]
    out_ref[...] = out


def step_kernel(m_ref, pack_ref, delta_ref, one_ref, two_ref, mask_ref, new_ref, ext_ref, corr_ref):
    lay = Layout(m_ref.shape[0] // ROWS)
    at = Place()
    row, lane = iota(0), iota(1)
    for t in range(lay.tiles):
        ext_ref[pl.ds(EXT * t + 2, ROWS), :] = m_ref[tile(t), :]
    for r in range(2):
        for s in range(lay.eights):
            one, two = one_ref[tile(r * lay.eights + s), :], two_ref[tile(r * lay.eights + s), :]
            ext_ref[pl.ds(EXT * ROWS * s + r, ROWS, stride=EXT), :] = at.from_up(one, two)
            ext_ref[pl.ds(EXT * ROWS * s + ROWS + 2 + r, ROWS, stride=EXT), :] = at.from_down(one, two)

    in_slot = lax.rem(lane, SLOT)
    half = in_slot < SLOT // 2
    near = (in_slot == 3) | (in_slot == 4)
    far = (in_slot >= 2) & (in_slot <= 5)
    sign = jnp.where(in_slot == 3, -0.5 * time_step, jnp.where(in_slot == 4, 0.5 * time_step, 0.0))
    for p in range(lay.packs):
        d = delta_ref[tile(p), :]
        one, two = one_ref[pl.ds(lay.delta + p, 1), :], two_ref[pl.ds(lay.delta + p, 1), :]
        dv = jnp.where(row == 0, at.from_up(one, two), roll(d, 1, 0)) + jnp.where(
            row == ROWS - 1, at.from_down(one, two), roll(d, -1, 0)
        )
        second = jnp.where(half, roll(d, -2, 1), roll(d, 2, 1))
        corr_ref[tile(p), :] = (
            jnp.where(far, -hyper_visc * second, 0.0)
            + jnp.where(near, across(hyper_visc * (8.0 * d - 2.0 * dv)), 0.0)
            + sign * spread(pack_ref[tile(p), :], 3) * across(d)
        )

    sea = mask_ref[...].astype(F32)
    edges = (
        jnp.where((row == 0) & (at.b == 0), 1.0, 0.0)
        + jnp.where((row == ROWS - 1) & (at.b == at.nb - 1), 1.0, 0.0)
        + jnp.where((lane == 0) & (at.g == 0), 1.0, 0.0)
        + jnp.where((lane == LANES - 1) & (at.g == at.ng - 1), 1.0, 0.0)
    )
    centre = 1.0 - 2.0 * mixing - hyper_visc * (20.0 - edges)
    col = (lane + at.g * LANES).astype(F32)
    coriolis = time_step * rotation * (2.0 * (col + 0.5) / (at.ng * LANES) - 1.0)
    border = (lane < SLOT // 2) | (lane >= LANES - SLOT // 2)

    def own(level, c):
        return m_ref[tile(COMPS * min(max(level, 0), lay.levels - 1) + c), :]

    for k in range(lay.levels):
        u, v = own(k, 2), own(k, 3)
        half_u, half_v = 0.5 * time_step * u, 0.5 * time_step * v
        for c in range(COMPS):
            t = COMPS * k + c
            x = own(k, c)
            up2, up1, dn1, dn2 = [ext_ref[pl.ds(EXT * t + n, ROWS), :] for n in (0, 1, 3, 4)]
            left, right = roll(x, 1, 1), roll(x, -1, 1)
            near1 = up1 + dn1
            q = 8.0 * hyper_visc * x - 2.0 * hyper_visc * near1
            out = (
                centre * x
                + (roll(q, 1, 1) + roll(q, -1, 1))
                + 8.0 * hyper_visc * near1
                - hyper_visc * ((up2 + dn2) + (roll(x, 2, 1) + roll(x, -2, 1)))
                - (half_u * (dn1 - up1) + half_v * (right - left))
                + mixing * (own(k - 1, c) + own(k + 1, c))
            )
            if c == 2:
                out = out + coriolis * v
            if c == 3:
                out = out - coriolis * u
            p, s = divmod(t, PER)
            fix = roll(corr_ref[tile(p), :], -(SLOT * s + SLOT // 2), 1)
            new_ref[tile(t), :] = sea * (out + jnp.where(border, fix, 0.0))


def call(kernel, outs, *args, scratch=(), specs=None, flops=0):
    return pl.pallas_call(
        kernel,
        out_shape=[jax.ShapeDtypeStruct(s, F32) for s in outs],
        in_specs=specs or [VMEM] * len(args),
        out_specs=[VMEM] * len(outs),
        scratch_shapes=[pltpu.VMEM(s, F32) if isinstance(s, tuple) else s for s in scratch],
        compiler_params=pltpu.CompilerParams(vmem_limit_bytes=32 * 1024 * 1024),
        cost_estimate=pl.CostEstimate(flops=flops, bytes_accessed=0, transcendentals=0),
    )(*args)


def on_device(ocean_state, surface_height, surface_damping, land_mask, *, shape):
    nb, ng = shape
    axes = ("blocks", "group")
    state = ocean_state.reshape(-1, LANES)
    lay = Layout(state.shape[0] // ROWS)
    g_one, g_two = swap_pairs(shape, "group")
    b_one, b_two = swap_pairs(shape, "blocks")
    one_tile = (ROWS, LANES)
    packed = (lay.packs * ROWS, LANES)
    flats = (FLAT * ROWS, LANES)

    m, pack, flat = call(
        pack_kernel,
        [state.shape, (packed[0] + ROWS, LANES), flats],
        state,
        land_mask,
        surface_height,
        surface_damping,
        specs=[HBM] * 4,
        scratch=[
            state.shape,
            pltpu.VMEM(one_tile, land_mask.dtype),
            one_tile,
            one_tile,
            pltpu.SemaphoreType.DMA((3 + lay.packs,)),
        ],
    )
    first = lax.ppermute(pack, axes, g_one)
    second = lax.ppermute(pack, axes, g_two)
    message = (lay.rows, LANES)
    own, near, delta, one, two = call(
        edge_kernel,
        [(flats[0] + ROWS, LANES), (2 * lay.pad, LANES), packed, message, message],
        m,
        pack,
        flat,
        first,
        second,
    )
    one = lax.ppermute(one, axes, b_one)
    two = lax.ppermute(two, axes, b_two)
    basis, sent = call(
        moment_kernel,
        [(ITERS * ROWS, LANES), (nb * ng, LANES)],
        m,
        own,
        near,
        one,
        two,
        scratch=[(FLAT * 3 * ROWS, 2 * LANES)],
    )
    got = lax.all_to_all(sent, axes, 0, 0, tiled=True)
    (new_state,) = call(
        step_kernel, [state.shape], m, pack, delta, one, two, land_mask, scratch=[(lay.tiles * EXT, LANES), packed],
        flops=20_000_000,
    )
    (surface,) = call(solve_kernel, [one_tile], got, basis)
    return new_state.reshape(ocean_state.shape), surface


def solution(mesh):
    placed = (
        P(None, None, "blocks", "group"),
        P("blocks", "group"),
        P("blocks", "group"),
        P("blocks", "group"),
    )
    shape = (mesh.shape["blocks"], mesh.shape["group"])

    def body(*args):
        return on_device(*args, shape=shape)

    return jax.shard_map(
        body,
        mesh=mesh,
        in_specs=placed,
        out_specs=(P(None, None, "blocks", "group"), P("blocks", "group")),
        check_vma=False,
    )
```

```python
import jax
import jax.numpy as jnp
from jax import lax
from jax.experimental import pallas as pl
from jax.experimental.pallas import tpu as pltpu
from jax.sharding import PartitionSpec as P

ITERS = 3

time_step = 0.25
hyper_visc = 0.025
mixing = 0.2
gravity = 4.0
rotation = 0.2

COMPS = 4
ROWS = 8
LANES = 128
SLOT = 8
PER = LANES // SLOT
EXT = 12
FLAT = 6
STRIP = 16
FL_A = 10**9
FL_B = 10**9
SHIFT = 4.5
F32 = jnp.float32
VMEM = pl.BlockSpec(memory_space=pltpu.VMEM)
HBM = pl.BlockSpec(memory_space=pltpu.HBM)


def iota(axis, rows=ROWS, lanes=LANES):
    return lax.broadcasted_iota(jnp.int32, (rows, lanes), axis)


def roll(x, shift, axis):
    return pltpu.roll(x, shift % x.shape[axis], axis)


def tile(k):
    return pl.ds(k * ROWS, ROWS)


def swap_pairs(mesh_shape, along):
    nb, ng = mesh_shape
    first, second = [], []
    for b in range(nb):
        for g in range(ng):
            me = b * ng + g
            if along == "blocks":
                one = (b ^ 1, g)
                two = ((b - 1) ^ 1) + 1
                two = (two, g) if 0 <= two < nb else (b, g ^ 1)
            else:
                one = (b, g ^ 1)
                two = ((g - 1) ^ 1) + 1
                two = (b, two) if 0 <= two < ng else (b ^ 1, g)
            first.append((me, one[0] * ng + one[1]))
            second.append((me, two[0] * ng + two[1]))
    return first, second


class Layout:
    def __init__(self, tiles):
        self.tiles = tiles
        self.levels = tiles // COMPS
        self.packs = tiles // PER
        self.eights = tiles // ROWS
        self.pad = -(-self.packs // ROWS) * ROWS
        self.flow = -(-self.levels // ROWS) * ROWS
        self.edge = 2 * self.flow
        self.flat = self.edge + self.pad
        self.strip = self.flat + FLAT * ROWS
        self.first = self.strip + ROWS
        self.delta = 2 * tiles
        self.second = self.delta + self.pad

    def level_rows(self, m_ref, comp, row):
        step = COMPS * ROWS
        parts = []
        for start in range(0, self.levels, ROWS):
            count = min(ROWS, self.levels - start)
            x = m_ref[pl.ds(start * step + comp * ROWS + row, count, stride=step), :]
            if count < ROWS:
                x = jnp.concatenate([x, jnp.zeros((ROWS - count, LANES), F32)], axis=0)
            parts.append(x)
        return parts


class Place:
    def __init__(self):
        self.b, self.nb = lax.axis_index("blocks"), lax.axis_size("blocks")
        self.g, self.ng = lax.axis_index("group"), lax.axis_size("group")
        self.b_even = lax.rem(self.b, 2) == 0
        self.g_even = lax.rem(self.g, 2) == 0
        self.up = (self.b > 0).astype(F32)
        self.down = (self.b < self.nb - 1).astype(F32)
        self.left = (self.g > 0).astype(F32)
        self.right = (self.g < self.ng - 1).astype(F32)

    def from_up(self, one, two):
        return jnp.where(self.b_even, two, one) * self.up

    def from_down(self, one, two):
        return jnp.where(self.b_even, one, two) * self.down


def pack_kernel(
    state_hbm, mask_hbm, height_hbm, damp_hbm, m_ref, pack_ref, flat_ref, state_ref, mask_ref, height_ref, damp_ref, sems
):
    lay = Layout(m_ref.shape[0] // ROWS)
    chunk = PER * ROWS
    small = [(mask_hbm, mask_ref), (height_hbm, height_ref), (damp_hbm, damp_ref)]
    copies = [pltpu.make_async_copy(a, b, sems.at[k]) for k, (a, b) in enumerate(small)]
    for p in range(lay.packs):
        at = pl.ds(p * chunk, chunk)
        copies.append(pltpu.make_async_copy(state_hbm.at[at], state_ref.at[at], sems.at[3 + p]))
    for copy in copies:
        copy.start()
    for copy in copies[: 3 + lay.packs // 2]:
        copy.wait()
    sea = mask_ref[...].astype(F32)
    row, lane = iota(0), iota(1)
    slot = lane // SLOT
    sum_u = sum_v = uu = uv = vu = zero = jnp.zeros((ROWS, LANES), F32)
    across_u = across_v = across_vu = zero
    for p in range(lay.packs):
        if p == lay.packs // 2:
            for copy in copies[3 + p :]:
                copy.wait()
        acc = zero
        for k in range(PER // COMPS):
            x = []
            for c in range(COMPS):
                q = COMPS * k + c
                x.append(state_ref[tile(p * PER + q), :] * sea)
                m_ref[tile(p * PER + q), :] = x[c]
                acc = jnp.where(slot == q, roll(x[c], SLOT * q + SLOT // 2, 1), acc)
            u, v = x[2:]
            below_u, below_v = roll(u, -1, 0), roll(v, -1, 0)
            right_u, right_v = roll(u, -1, 1), roll(v, -1, 1)
            sum_u, sum_v = sum_u + u, sum_v + v
            uu, uv, vu = uu + u * below_u, uv + u * below_v, vu + v * below_u
            across_u, across_v, across_vu = across_u + v * right_u, across_v + v * right_v, across_vu + u * right_v
        pack_ref[tile(p), :] = acc

    def step_down(ahead, back):
        inner = row < ROWS - 1
        return jnp.where(inner, ahead, 0.0) - roll(jnp.where(inner, back, 0.0), 1, 0)

    def step_right(ahead, back):
        inner = lane < LANES - 1
        return jnp.where(inner, ahead, 0.0) - roll(jnp.where(inner, back, 0.0), 1, 1)

    advect_u = 0.5 * (step_down(uu, uu) + step_right(across_u, across_vu))
    advect_v = 0.5 * (step_down(uv, vu) + step_right(across_v, across_v))
    damp = damp_ref[...]
    flat = [sum_u, sum_v, advect_u, advect_v, sea * damp * height_ref[...], sea * (4.0 + damp)]
    acc = jnp.zeros((ROWS, LANES), F32)
    for f in range(FLAT):
        flat_ref[tile(f), :] = flat[f]
        acc = jnp.where(lane // STRIP == f, roll(flat[f], STRIP * f + STRIP // 2, 1), acc)
    pack_ref[tile(lay.packs), :] = acc


def spread(x, of):
    comp = lax.rem(lax.broadcasted_iota(jnp.int32, x.shape, 1) // SLOT, COMPS)
    out = x
    for c in range(COMPS):
        if c != of:
            out = jnp.where(comp == c, roll(x, SLOT * (c - of), 1), out)
    return out


def across(x):
    half = lax.rem(lax.broadcasted_iota(jnp.int32, x.shape, 1), SLOT) < SLOT // 2
    return jnp.where(half, roll(x, -1, 1), roll(x, 1, 1))


def fold(x):
    step = SLOT * COMPS
    while step < LANES:
        x = x + roll(x, step, 1)
        step *= 2
    return x


def edge_kernel(
    m_ref, pack_ref, flat_ref, first_ref, second_ref, own_ref, near_ref, delta_ref, one_ref, two_ref
):
    lay = Layout(m_ref.shape[0] // ROWS)
    at = Place()
    lane = iota(1)
    in_slot = lax.rem(lane, SLOT)
    half = in_slot < SLOT // 2
    sign = jnp.where(in_slot == SLOT // 2 - 1, 0.5, jnp.where(in_slot == SLOT // 2, -0.5, 0.0))

    def beyond(p, low):
        first, second = first_ref[tile(p), :], second_ref[tile(p), :]
        from_left = jnp.where(at.g_even, second, first) * at.left
        from_right = jnp.where(at.g_even, first, second) * at.right
        return jnp.where(low, from_left, from_right)

    near_ref[...] = jnp.zeros(near_ref.shape, F32)
    inner = jnp.zeros((ROWS, LANES), F32)
    outer = jnp.zeros((ROWS, LANES), F32)
    for p in range(lay.packs):
        own, far = pack_ref[tile(p), :], beyond(p, half)
        delta_ref[tile(p), :] = far - own
        near_ref[p : p + 1, :] = far[0:1]
        near_ref[lay.pad + p : lay.pad + p + 1, :] = far[ROWS - 1 : ROWS]
        inner = inner + spread(own, 3) * across(far)
        outer = outer + spread(far, 3) * across(own)
    inner, outer = fold(sign * inner), fold(sign * outer)
    strip = beyond(lay.packs, lax.rem(lane, STRIP) < STRIP // 2)
    for f in range(FLAT):
        value = flat_ref[tile(f), :]
        if 2 <= f <= 3:
            border = (lane == 0) | (lane == LANES - 1)
            value = value + jnp.where(border, roll(inner, -(SLOT * f + SLOT // 2), 1), 0.0)
            mid = STRIP * f + STRIP // 2
            border = (lane == mid - 1) | (lane == mid)
            strip = strip + jnp.where(border, roll(outer, mid - (SLOT * f + SLOT // 2), 1), 0.0)
        own_ref[tile(f), :] = value
    own_ref[tile(FLAT), :] = strip

    def fill(low_ref, high_ref):
        for ref, row, rows in ((low_ref, 0, slice(0, lay.pad)), (high_ref, ROWS - 1, slice(lay.pad, 2 * lay.pad))):
            for c in (2, 3):
                for n, x in enumerate(lay.level_rows(m_ref, c, row)):
                    ref[pl.ds((c - 2) * lay.flow + n * ROWS, ROWS), :] = x
            ref[pl.ds(lay.edge, lay.pad), :] = near_ref[rows, :]
            ref[pl.ds(lay.flat, (FLAT + 1) * ROWS), :] = own_ref[...]

    pl.when(at.b_even)(lambda: fill(two_ref, one_ref))
    pl.when(jnp.logical_not(at.b_even))(lambda: fill(one_ref, two_ref))


def rest_kernel(m_ref, delta_ref, one_ref, two_ref):
    lay = Layout(m_ref.shape[0] // ROWS)
    at = Place()

    def fill(low_ref, high_ref):
        for ref, row in ((low_ref, 0), (high_ref, ROWS - 1)):
            for r in range(2):
                for s in range(lay.eights):
                    start = ROWS * ROWS * s + (row - 1 if row else 0) + r
                    ref[tile(r * lay.eights + s), :] = m_ref[pl.ds(start, ROWS, stride=ROWS), :]
            ref[pl.ds(lay.delta, lay.pad), :] = jnp.zeros((lay.pad, LANES), F32)
            for p in range(lay.packs):
                ref[pl.ds(lay.delta + p, 1), :] = delta_ref[pl.ds(ROWS * p + row, 1), :]

    pl.when(at.b_even)(lambda: fill(two_ref, one_ref))
    pl.when(jnp.logical_not(at.b_even))(lambda: fill(one_ref, two_ref))


def moment_kernel(m_ref, own_ref, near_ref, one_ref, two_ref, basis_ref, send_ref, wide_ref):
    lay = Layout(m_ref.shape[0] // ROWS)
    at = Place()
    row, lane = iota(0), iota(1)
    outside = (lane < STRIP // 2) | (lane >= LANES - STRIP // 2)
    rows = 3 * ROWS

    def neighbours(where):
        return at.from_up(one_ref[where, :], two_ref[where, :]), at.from_down(one_ref[where, :], two_ref[where, :])

    strips = neighbours(pl.ds(lay.strip, ROWS))
    strips = (strips[0], own_ref[tile(FLAT), :], strips[1])
    for f in range(FLAT):
        fields = neighbours(pl.ds(lay.flat + f * ROWS, ROWS))
        fields = (fields[0], own_ref[tile(f), :], fields[1])
        for k in range(3):
            to = pl.ds(f * rows + k * ROWS, ROWS)
            wide_ref[to, 0:LANES] = fields[k]
            side = roll(strips[k], -(STRIP * f + STRIP // 2), 1)
            wide_ref[to, LANES : 2 * LANES] = jnp.where(outside, side, 0.0)

    own_rows = [[lay.level_rows(m_ref, c, r) for c in (2, 3)] for r in (0, ROWS - 1)]
    cross = []
    for f in range(2):
        total = [jnp.zeros((ROWS, LANES), F32) for _ in range(4)]
        for n in range(lay.flow // ROWS):
            flow = neighbours(tile(n))
            carried = neighbours(pl.ds(f * lay.flow + n * ROWS, ROWS))
            total[0] = total[0] + flow[0] * own_rows[0][f][n]
            total[1] = total[1] - own_rows[0][0][n] * carried[0]
            total[2] = total[2] + own_rows[1][0][n] * carried[1]
            total[3] = total[3] - flow[1] * own_rows[1][f][n]
        cross.append([0.5 * jnp.sum(x, axis=0, keepdims=True) for x in total])
    above, below = neighbours(pl.ds(lay.edge, lay.pad))
    top, bottom = near_ref[0 : lay.pad, :], near_ref[lay.pad :, :]

    def flow_packed(x):
        return roll(x, SLOT, 1)

    def corner(a, b):
        comp = lax.rem(iota(1, lay.pad) // SLOT, COMPS)
        x = jnp.where(comp == 3, flow_packed(a), a) * b
        return 0.5 * fold(jnp.sum(x, axis=0, keepdims=True))

    corners = [corner(above, top), -corner(top, above), corner(bottom, below), -corner(below, bottom)]
    border = (iota(1, 1) < SLOT // 2) | (iota(1, 1) >= LANES - SLOT // 2)
    for f in (2, 3):
        for k, at_row in enumerate((ROWS - 1, ROWS, 2 * ROWS - 1, 2 * ROWS)):
            to = pl.ds(f * rows + at_row, 1)
            wide_ref[to, 0:LANES] = wide_ref[to, 0:LANES] + cross[f - 2][k]
            side = roll(corners[k], -(SLOT * f + SLOT // 2), 1)
            wide_ref[to, LANES : 2 * LANES] = wide_ref[to, LANES : 2 * LANES] + jnp.where(border, side, 0.0)

    sum_u, sum_v, adv_u, adv_v, forcing, diagonal = [wide_ref[pl.ds(f * rows, rows), :] for f in range(FLAT)]
    sea = jnp.where(diagonal > 0.0, 1.0, 0.0)
    shape = (rows, 2 * LANES)
    i = iota(0, *shape) - ROWS + at.b * ROWS
    j = iota(1, *shape)
    j = jnp.where(j < LANES + LANES // 2, j, j - 2 * LANES) + at.g * LANES
    total_rows, total_cols = at.nb * ROWS, at.ng * LANES
    edges = (
        jnp.where(i == 0, 1.0, 0.0)
        + jnp.where(i == total_rows - 1, 1.0, 0.0)
        + jnp.where(j == 0, 1.0, 0.0)
        + jnp.where(j == total_cols - 1, 1.0, 0.0)
    )
    coriolis = rotation * (2.0 * (j.astype(F32) + 0.5) / total_cols - 1.0)

    def both(x, n, axis):
        return roll(x, n, axis) + roll(x, -n, axis)

    def transport(x, turn, adv):
        near = both(x, 1, 0)
        linear = (
            (1.0 - hyper_visc * (20.0 - edges)) * x
            + 8.0 * hyper_visc * near
            - hyper_visc * (both(x, 2, 0) + both(x, 2, 1))
            + both(8.0 * hyper_visc * x - 2.0 * hyper_visc * near, 1, 1)
        )
        return sea * (linear + time_step * (turn - adv)) / lay.levels

    east = transport(sum_u, coriolis * sum_v, adv_u)
    north = transport(sum_v, -coriolis * sum_u, adv_v)
    divergence = 0.5 * (roll(east, -1, 0) - roll(east, 1, 0) + roll(north, -1, 1) - roll(north, 1, 1))
    v = [forcing - gravity * sea * divergence]
    own_diagonal = diagonal - SHIFT
    for _ in range(ITERS):
        x = v[-1]
        v.append(own_diagonal * x - sea * (both(x, 1, 0) + both(x, 1, 1)))
    v = [x[ROWS : 2 * ROWS, 0:LANES] for x in v]
    for k in range(ITERS):
        basis_ref[tile(k), :] = v[k]
    line = jnp.zeros((ROWS, LANES), F32)
    for k in range(2 * ITERS):
        part = jnp.sum(v[k // 2] * v[k - k // 2], axis=0, keepdims=True)
        line = jnp.where(row == k, part, line)
    line = jnp.sum(line, axis=1, keepdims=True)
    line = jnp.sum(jnp.where(row == lane, line, 0.0), axis=0, keepdims=True)
    send_ref[...] = jnp.broadcast_to(line, send_ref.shape)


def solve_kernel(got_ref, basis_ref, done_ref, out_ref):
    line = jnp.sum(got_ref[...], axis=0, keepdims=True)
    lane = iota(1, 1)
    moment = [jnp.sum(jnp.where(lane == k, line, 0.0), axis=1, keepdims=True) for k in range(2 * ITERS)]

    def dot(a, b):
        total = None
        for k in range(len(a) + len(b) - 1):
            weight = sum(a[n] * b[k - n] for n in range(len(a)) if 0 <= k - n < len(b))
            total = weight * moment[k] if total is None else total + weight * moment[k]
        return total

    def add(a, scale, b):
        out = list(a) + [0.0] * (len(b) - len(a))
        return [x + scale * b[n] if n < len(b) else x for n, x in enumerate(out)]

    def image(a):
        return [SHIFT * (a[n] if n < len(a) else 0.0) + (a[n - 1] if n else 0.0) for n in range(len(a) + 1)]

    one = jnp.ones((1, 1), F32)
    residual, direction, surface = [one], [one], []
    norm = dot(residual, residual)
    for iteration in range(ITERS):
        applied = image(direction)
        alpha = norm / dot(direction, applied)
        surface = add(surface, alpha, direction)
        if iteration + 1 < ITERS:
            residual = add(residual, -alpha, applied)
            following = dot(residual, residual)
            direction = add(residual, following / norm, direction)
            norm = following
    out = surface[0] * basis_ref[tile(0), :]
    for k in range(1, ITERS):
        out = out + surface[k] * basis_ref[tile(k), :]
    out_ref[...] = out


def step_kernel(m_ref, pack_ref, delta_ref, one_ref, two_ref, mask_ref, new_ref, done_ref, ext_ref, corr_ref):
    lay = Layout(m_ref.shape[0] // ROWS)
    at = Place()
    row, lane = iota(0), iota(1)
    for t in range(lay.tiles):
        ext_ref[pl.ds(EXT * t + 2, ROWS), :] = m_ref[tile(t), :]
    for r in range(2):
        for s in range(lay.eights):
            one, two = one_ref[tile(r * lay.eights + s), :], two_ref[tile(r * lay.eights + s), :]
            ext_ref[pl.ds(EXT * ROWS * s + r, ROWS, stride=EXT), :] = at.from_up(one, two)
            ext_ref[pl.ds(EXT * ROWS * s + ROWS + 2 + r, ROWS, stride=EXT), :] = at.from_down(one, two)

    in_slot = lax.rem(lane, SLOT)
    half = in_slot < SLOT // 2
    near = (in_slot == 3) | (in_slot == 4)
    far = (in_slot >= 2) & (in_slot <= 5)
    sign = jnp.where(in_slot == 3, -0.5 * time_step, jnp.where(in_slot == 4, 0.5 * time_step, 0.0))
    for p in range(lay.packs):
        d = delta_ref[tile(p), :]
        one, two = one_ref[pl.ds(lay.delta + p, 1), :], two_ref[pl.ds(lay.delta + p, 1), :]
        dv = jnp.where(row == 0, at.from_up(one, two), roll(d, 1, 0)) + jnp.where(
            row == ROWS - 1, at.from_down(one, two), roll(d, -1, 0)
        )
        second = jnp.where(half, roll(d, -2, 1), roll(d, 2, 1))
        corr_ref[tile(p), :] = (
            jnp.where(far, -hyper_visc * second, 0.0)
            + jnp.where(near, across(hyper_visc * (8.0 * d - 2.0 * dv)), 0.0)
            + sign * spread(pack_ref[tile(p), :], 3) * across(d)
        )

    sea = mask_ref[...].astype(F32)
    done_ref[...] = sea
    edges = (
        jnp.where((row == 0) & (at.b == 0), 1.0, 0.0)
        + jnp.where((row == ROWS - 1) & (at.b == at.nb - 1), 1.0, 0.0)
        + jnp.where((lane == 0) & (at.g == 0), 1.0, 0.0)
        + jnp.where((lane == LANES - 1) & (at.g == at.ng - 1), 1.0, 0.0)
    )
    centre = 1.0 - 2.0 * mixing - hyper_visc * (20.0 - edges)
    col = (lane + at.g * LANES).astype(F32)
    coriolis = time_step * rotation * (2.0 * (col + 0.5) / (at.ng * LANES) - 1.0)
    border = (lane < SLOT // 2) | (lane >= LANES - SLOT // 2)

    def own(level, c):
        return m_ref[tile(COMPS * min(max(level, 0), lay.levels - 1) + c), :]

    for k in range(lay.levels):
        u, v = own(k, 2), own(k, 3)
        half_u, half_v = 0.5 * time_step * u, 0.5 * time_step * v
        for c in range(COMPS):
            t = COMPS * k + c
            x = own(k, c)
            up2, up1, dn1, dn2 = [ext_ref[pl.ds(EXT * t + n, ROWS), :] for n in (0, 1, 3, 4)]
            left, right = roll(x, 1, 1), roll(x, -1, 1)
            near1 = up1 + dn1
            q = 8.0 * hyper_visc * x - 2.0 * hyper_visc * near1
            out = (
                centre * x
                + (roll(q, 1, 1) + roll(q, -1, 1))
                + 8.0 * hyper_visc * near1
                - hyper_visc * ((up2 + dn2) + (roll(x, 2, 1) + roll(x, -2, 1)))
                - (half_u * (dn1 - up1) + half_v * (right - left))
                + mixing * (own(k - 1, c) + own(k + 1, c))
            )
            if c == 2:
                out = out + coriolis * v
            if c == 3:
                out = out - coriolis * u
            p, s = divmod(t, PER)
            fix = roll(corr_ref[tile(p), :], -(SLOT * s + SLOT // 2), 1)
            new_ref[tile(t), :] = sea * (out + jnp.where(border, fix, 0.0))


def call(kernel, outs, *args, scratch=(), specs=None, flops=0, vmem=8):
    return pl.pallas_call(
        kernel,
        out_shape=[jax.ShapeDtypeStruct(s, F32) if isinstance(s, tuple) else s for s in outs],
        in_specs=specs or [VMEM] * len(args),
        out_specs=[VMEM] * len(outs),
        scratch_shapes=[pltpu.VMEM(s, F32) if isinstance(s, tuple) else s for s in scratch],
        compiler_params=pltpu.CompilerParams(vmem_limit_bytes=vmem * 1024 * 1024),
        cost_estimate=pl.CostEstimate(flops=flops, bytes_accessed=0, transcendentals=0),
    )(*args)


def on_device(ocean_state, surface_height, surface_damping, land_mask, *, shape):
    nb, ng = shape
    axes = ("blocks", "group")
    state = ocean_state.reshape(-1, LANES)
    lay = Layout(state.shape[0] // ROWS)
    g_one, g_two = swap_pairs(shape, "group")
    b_one, b_two = swap_pairs(shape, "blocks")
    one_tile = (ROWS, LANES)
    packed = (lay.packs * ROWS, LANES)
    flats = (FLAT * ROWS, LANES)

    m, pack, flat = call(
        pack_kernel,
        [state.shape, (packed[0] + ROWS, LANES), flats],
        *[pltpu.with_memory_space_constraint(x, pltpu.HBM) for x in (state, land_mask, surface_height, surface_damping)],
        specs=[HBM] * 4,
        scratch=[
            state.shape,
            pltpu.VMEM(one_tile, land_mask.dtype),
            one_tile,
            one_tile,
            pltpu.SemaphoreType.DMA((3 + lay.packs,)),
        ],
    )
    first = lax.ppermute(pack, axes, g_one)
    second = lax.ppermute(pack, axes, g_two)
    message, rest = (lay.first, LANES), (lay.second, LANES)
    own, near, delta, one, two = call(
        edge_kernel,
        [(flats[0] + ROWS, LANES), (2 * lay.pad, LANES), packed, message, message],
        m,
        pack,
        flat,
        first,
        second,
    )
    one = lax.ppermute(one, axes, b_one)
    two = lax.ppermute(two, axes, b_two)
    one_rest, two_rest = call(rest_kernel, [rest, rest], m, delta)
    one_rest = lax.ppermute(one_rest, axes, b_one)
    two_rest = lax.ppermute(two_rest, axes, b_two)
    basis, sent = call(
        moment_kernel,
        [(ITERS * ROWS, LANES), pltpu.VMEM((nb * ng, LANES), F32)],
        m,
        own,
        near,
        one,
        two,
        scratch=[(FLAT * 3 * ROWS, 2 * LANES)],
        flops=FL_A,
    )
    got = lax.all_to_all(sent, axes, 0, 0, tiled=True)
    new_state, done = call(
        step_kernel, [state.shape, one_tile], m, pack, delta, one_rest, two_rest, land_mask, scratch=[(lay.tiles * EXT, LANES), packed],
        flops=FL_B,
    )
    (surface,) = call(solve_kernel, [one_tile], got, basis, done)
    return new_state.reshape(ocean_state.shape), surface


def solution(mesh):
    placed = (
        P(None, None, "blocks", "group"),
        P("blocks", "group"),
        P("blocks", "group"),
        P("blocks", "group"),
    )
    shape = (mesh.shape["blocks"], mesh.shape["group"])

    def body(*args):
        return on_device(*args, shape=shape)

    return jax.shard_map(
        body,
        mesh=mesh,
        in_specs=placed,
        out_specs=(P(None, None, "blocks", "group"), P("blocks", "group")),
        check_vma=False,
    )
```

```python
import functools

import jax
import jax.numpy as jnp
from jax import lax
from jax.experimental import pallas as pl
from jax.experimental.pallas import tpu as pltpu
from jax.sharding import PartitionSpec as P

ITERS = 3

time_step = 0.25
hyper_visc = 0.025
mixing = 0.2
gravity = 4.0
rotation = 0.2

COMPS = 4
ROWS = 8
LANES = 128
SLOT = 8
PER = LANES // SLOT
EXT = 12
FLAT = 6
STRIP = 16
LONG = 10**9
SHIFT = 4.5
F32 = jnp.float32
VMEM = pl.BlockSpec(memory_space=pltpu.VMEM)
HBM = pl.BlockSpec(memory_space=pltpu.HBM)


def iota(axis, rows=ROWS, lanes=LANES):
    return lax.broadcasted_iota(jnp.int32, (rows, lanes), axis)


def roll(x, shift, axis):
    return pltpu.roll(x, shift % x.shape[axis], axis)


def tile(k):
    return pl.ds(k * ROWS, ROWS)


def swap_pairs(mesh_shape, along):
    nb, ng = mesh_shape
    first, second = [], []
    for b in range(nb):
        for g in range(ng):
            me = b * ng + g
            if along == "blocks":
                one = (b ^ 1, g)
                two = ((b - 1) ^ 1) + 1
                two = (two, g) if 0 <= two < nb else (b, g ^ 1)
            else:
                one = (b, g ^ 1)
                two = ((g - 1) ^ 1) + 1
                two = (b, two) if 0 <= two < ng else (b ^ 1, g)
            first.append((me, one[0] * ng + one[1]))
            second.append((me, two[0] * ng + two[1]))
    return first, second


class Layout:
    def __init__(self, tiles):
        self.tiles = tiles
        self.levels = tiles // COMPS
        self.packs = tiles // PER
        self.eights = tiles // ROWS
        self.pad = -(-self.packs // ROWS) * ROWS
        self.flow = -(-self.levels // ROWS) * ROWS
        self.edge = 0
        self.delta = self.pad
        self.flat = 2 * self.pad
        self.strip = self.flat + FLAT * ROWS
        self.message = self.strip + ROWS


class Place:
    def __init__(self):
        self.b, self.nb = lax.axis_index("blocks"), lax.axis_size("blocks")
        self.g, self.ng = lax.axis_index("group"), lax.axis_size("group")
        self.b_even = lax.rem(self.b, 2) == 0
        self.g_even = lax.rem(self.g, 2) == 0
        self.up = (self.b > 0).astype(F32)
        self.down = (self.b < self.nb - 1).astype(F32)
        self.left = (self.g > 0).astype(F32)
        self.right = (self.g < self.ng - 1).astype(F32)

    def from_up(self, one, two):
        return jnp.where(self.b_even, two, one) * self.up

    def from_down(self, one, two):
        return jnp.where(self.b_even, one, two) * self.down


def pack_kernel(
    state_hbm, mask_hbm, height_hbm, damp_hbm, m_ref, pack_ref, flat_ref, state_ref, mask_ref, height_ref, damp_ref, sems
):
    lay = Layout(m_ref.shape[0] // ROWS)
    chunk = PER * ROWS
    small = [(mask_hbm, mask_ref), (height_hbm, height_ref), (damp_hbm, damp_ref)]
    copies = [pltpu.make_async_copy(a, b, sems.at[k]) for k, (a, b) in enumerate(small)]
    for p in range(lay.packs):
        at = pl.ds(p * chunk, chunk)
        copies.append(pltpu.make_async_copy(state_hbm.at[at], state_ref.at[at], sems.at[3 + p]))
    for copy in copies:
        copy.start()
    for copy in copies[: 3 + lay.packs // 2]:
        copy.wait()
    sea = mask_ref[...].astype(F32)
    row, lane = iota(0), iota(1)
    slot = lane // SLOT
    sum_u = sum_v = uu = uv = vu = zero = jnp.zeros((ROWS, LANES), F32)
    across_u = across_v = across_vu = zero
    for p in range(lay.packs):
        if p == lay.packs // 2:
            for copy in copies[3 + p :]:
                copy.wait()
        acc = zero
        for k in range(PER // COMPS):
            x = []
            for c in range(COMPS):
                q = COMPS * k + c
                x.append(state_ref[tile(p * PER + q), :] * sea)
                m_ref[tile(p * PER + q), :] = x[c]
                acc = jnp.where(slot == q, roll(x[c], SLOT * q + SLOT // 2, 1), acc)
            u, v = x[2:]
            below_u, below_v = roll(u, -1, 0), roll(v, -1, 0)
            right_u, right_v = roll(u, -1, 1), roll(v, -1, 1)
            sum_u, sum_v = sum_u + u, sum_v + v
            uu, uv, vu = uu + u * below_u, uv + u * below_v, vu + v * below_u
            across_u, across_v, across_vu = across_u + v * right_u, across_v + v * right_v, across_vu + u * right_v
        pack_ref[tile(p), :] = acc

    def step_down(ahead, back):
        inner = row < ROWS - 1
        return jnp.where(inner, ahead, 0.0) - roll(jnp.where(inner, back, 0.0), 1, 0)

    def step_right(ahead, back):
        inner = lane < LANES - 1
        return jnp.where(inner, ahead, 0.0) - roll(jnp.where(inner, back, 0.0), 1, 1)

    advect_u = 0.5 * (step_down(uu, uu) + step_right(across_u, across_vu))
    advect_v = 0.5 * (step_down(uv, vu) + step_right(across_v, across_v))
    damp = damp_ref[...]
    flat = [sum_u, sum_v, advect_u, advect_v, sea * damp * height_ref[...], sea * (4.0 + damp)]
    acc = jnp.zeros((ROWS, LANES), F32)
    for f in range(FLAT):
        flat_ref[tile(f), :] = flat[f]
        acc = jnp.where(lane // STRIP == f, roll(flat[f], STRIP * f + STRIP // 2, 1), acc)
    pack_ref[tile(lay.packs), :] = acc


def spread(x, of):
    comp = lax.rem(lax.broadcasted_iota(jnp.int32, x.shape, 1) // SLOT, COMPS)
    out = x
    for c in range(COMPS):
        if c != of:
            out = jnp.where(comp == c, roll(x, SLOT * (c - of), 1), out)
    return out


def across(x):
    half = lax.rem(lax.broadcasted_iota(jnp.int32, x.shape, 1), SLOT) < SLOT // 2
    return jnp.where(half, roll(x, -1, 1), roll(x, 1, 1))


def fold(x):
    step = SLOT * COMPS
    while step < LANES:
        x = x + roll(x, step, 1)
        step *= 2
    return x


def edge_kernel(
    m_ref, pack_ref, flat_ref, first_ref, second_ref, own_ref, near_ref, delta_ref, one_ref, two_ref
):
    lay = Layout(m_ref.shape[0] // ROWS)
    at = Place()
    lane = iota(1)
    in_slot = lax.rem(lane, SLOT)
    half = in_slot < SLOT // 2
    sign = jnp.where(in_slot == SLOT // 2 - 1, 0.5, jnp.where(in_slot == SLOT // 2, -0.5, 0.0))

    def beyond(p, low):
        first, second = first_ref[tile(p), :], second_ref[tile(p), :]
        from_left = jnp.where(at.g_even, second, first) * at.left
        from_right = jnp.where(at.g_even, first, second) * at.right
        return jnp.where(low, from_left, from_right)

    near_ref[...] = jnp.zeros(near_ref.shape, F32)
    inner = jnp.zeros((ROWS, LANES), F32)
    outer = jnp.zeros((ROWS, LANES), F32)
    for p in range(lay.packs):
        own, far = pack_ref[tile(p), :], beyond(p, half)
        delta_ref[tile(p), :] = far - own
        near_ref[p : p + 1, :] = far[0:1]
        near_ref[lay.pad + p : lay.pad + p + 1, :] = far[ROWS - 1 : ROWS]
        inner = inner + spread(own, 3) * across(far)
        outer = outer + spread(far, 3) * across(own)
    inner, outer = fold(sign * inner), fold(sign * outer)
    strip = beyond(lay.packs, lax.rem(lane, STRIP) < STRIP // 2)
    for f in range(FLAT):
        value = flat_ref[tile(f), :]
        if 2 <= f <= 3:
            border = (lane == 0) | (lane == LANES - 1)
            value = value + jnp.where(border, roll(inner, -(SLOT * f + SLOT // 2), 1), 0.0)
            mid = STRIP * f + STRIP // 2
            border = (lane == mid - 1) | (lane == mid)
            strip = strip + jnp.where(border, roll(outer, mid - (SLOT * f + SLOT // 2), 1), 0.0)
        own_ref[tile(f), :] = value
    own_ref[tile(FLAT), :] = strip

    def fill(low_ref, high_ref):
        for ref, row, rows in ((low_ref, 0, slice(0, lay.pad)), (high_ref, ROWS - 1, slice(lay.pad, 2 * lay.pad))):
            ref[pl.ds(lay.edge, lay.pad), :] = near_ref[rows, :]
            ref[pl.ds(lay.delta, lay.pad), :] = jnp.zeros((lay.pad, LANES), F32)
            for p in range(lay.packs):
                ref[pl.ds(lay.delta + p, 1), :] = delta_ref[pl.ds(ROWS * p + row, 1), :]
            ref[pl.ds(lay.flat, (FLAT + 1) * ROWS), :] = own_ref[...]

    pl.when(at.b_even)(lambda: fill(two_ref, one_ref))
    pl.when(jnp.logical_not(at.b_even))(lambda: fill(one_ref, two_ref))


def rows_kernel(m_ref, one_ref, two_ref):
    lay = Layout(m_ref.shape[0] // ROWS)

    def fill(low_ref, high_ref):
        for ref, row in ((low_ref, 0), (high_ref, ROWS - 2)):
            for r in range(2):
                for s in range(lay.eights):
                    at = pl.ds(ROWS * ROWS * s + row + r, ROWS, stride=ROWS)
                    ref[tile(r * lay.eights + s), :] = m_ref[at, :]

    even = Place().b_even
    pl.when(even)(lambda: fill(two_ref, one_ref))
    pl.when(jnp.logical_not(even))(lambda: fill(one_ref, two_ref))


def cross_kernel(m_ref, one_ref, two_ref, cross_ref):
    lay = Layout(m_ref.shape[0] // ROWS)
    at = Place()
    row = iota(0)

    def level_rows(ref, comp, first, count_rows):
        parts = []
        for start in range(0, lay.levels, ROWS):
            count = min(ROWS, lay.levels - start)
            x = ref[pl.ds((start * COMPS + comp) * count_rows + first, count, stride=COMPS * count_rows), :]
            if count < ROWS:
                x = jnp.concatenate([x, jnp.zeros((ROWS - count, LANES), F32)], axis=0)
            parts.append(x)
        return parts

    def beyond(first):
        return [[level_rows(ref, c, first, 1) for c in (2, 3)] for ref in (one_ref, two_ref)]

    one, two = beyond(lay.tiles)
    above = [[at.from_up(x, y) for x, y in zip(one[c], two[c])] for c in range(2)]
    one, two = beyond(0)
    below = [[at.from_down(x, y) for x, y in zip(one[c], two[c])] for c in range(2)]
    top, bottom = [[level_rows(m_ref, c, r, ROWS) for c in (2, 3)] for r in (0, ROWS - 1)]

    def total(flow, carried):
        return 0.5 * jnp.sum(sum(x * y for x, y in zip(flow, carried)), axis=0, keepdims=True)

    out = jnp.zeros((ROWS, LANES), F32)
    for f in range(2):
        sums = (total(above[0], top[f]), -total(top[0], above[f]), total(bottom[0], below[f]), -total(below[0], bottom[f]))
        for k in range(4):
            out = jnp.where(row == 4 * f + k, sums[k], out)
    cross_ref[...] = out


def moment_kernel(own_ref, near_ref, cross_ref, one_ref, two_ref, basis_ref, send_ref, wide_ref, *, levels):
    lay = Layout(levels * COMPS)
    at = Place()
    row, lane = iota(0), iota(1)
    outside = (lane < STRIP // 2) | (lane >= LANES - STRIP // 2)
    rows = 3 * ROWS

    def neighbours(where):
        return at.from_up(one_ref[where, :], two_ref[where, :]), at.from_down(one_ref[where, :], two_ref[where, :])

    strips = neighbours(pl.ds(lay.strip, ROWS))
    strips = (strips[0], own_ref[tile(FLAT), :], strips[1])
    for f in range(FLAT):
        fields = neighbours(pl.ds(lay.flat + f * ROWS, ROWS))
        fields = (fields[0], own_ref[tile(f), :], fields[1])
        for k in range(3):
            to = pl.ds(f * rows + k * ROWS, ROWS)
            wide_ref[to, 0:LANES] = fields[k]
            side = roll(strips[k], -(STRIP * f + STRIP // 2), 1)
            wide_ref[to, LANES : 2 * LANES] = jnp.where(outside, side, 0.0)

    above, below = neighbours(pl.ds(lay.edge, lay.pad))
    top, bottom = near_ref[0 : lay.pad, :], near_ref[lay.pad :, :]

    def flow_packed(x):
        return roll(x, SLOT, 1)

    def corner(a, b):
        comp = lax.rem(iota(1, lay.pad) // SLOT, COMPS)
        x = jnp.where(comp == 3, flow_packed(a), a) * b
        return 0.5 * fold(jnp.sum(x, axis=0, keepdims=True))

    corners = [corner(above, top), -corner(top, above), corner(bottom, below), -corner(below, bottom)]
    border = (iota(1, 1) < SLOT // 2) | (iota(1, 1) >= LANES - SLOT // 2)
    for f in (2, 3):
        for k, at_row in enumerate((ROWS - 1, ROWS, 2 * ROWS - 1, 2 * ROWS)):
            to = pl.ds(f * rows + at_row, 1)
            wide_ref[to, 0:LANES] = wide_ref[to, 0:LANES] + cross_ref[4 * (f - 2) + k : 4 * (f - 2) + k + 1, :]
            side = roll(corners[k], -(SLOT * f + SLOT // 2), 1)
            wide_ref[to, LANES : 2 * LANES] = wide_ref[to, LANES : 2 * LANES] + jnp.where(border, side, 0.0)

    sum_u, sum_v, adv_u, adv_v, forcing, diagonal = [wide_ref[pl.ds(f * rows, rows), :] for f in range(FLAT)]
    sea = jnp.where(diagonal > 0.0, 1.0, 0.0)
    shape = (rows, 2 * LANES)
    i = iota(0, *shape) - ROWS + at.b * ROWS
    j = iota(1, *shape)
    j = jnp.where(j < LANES + LANES // 2, j, j - 2 * LANES) + at.g * LANES
    total_rows, total_cols = at.nb * ROWS, at.ng * LANES
    edges = (
        jnp.where(i == 0, 1.0, 0.0)
        + jnp.where(i == total_rows - 1, 1.0, 0.0)
        + jnp.where(j == 0, 1.0, 0.0)
        + jnp.where(j == total_cols - 1, 1.0, 0.0)
    )
    coriolis = rotation * (2.0 * (j.astype(F32) + 0.5) / total_cols - 1.0)

    def both(x, n, axis):
        return roll(x, n, axis) + roll(x, -n, axis)

    def transport(x, turn, adv):
        near = both(x, 1, 0)
        linear = (
            (1.0 - hyper_visc * (20.0 - edges)) * x
            + 8.0 * hyper_visc * near
            - hyper_visc * (both(x, 2, 0) + both(x, 2, 1))
            + both(8.0 * hyper_visc * x - 2.0 * hyper_visc * near, 1, 1)
        )
        return sea * (linear + time_step * (turn - adv)) / lay.levels

    east = transport(sum_u, coriolis * sum_v, adv_u)
    north = transport(sum_v, -coriolis * sum_u, adv_v)
    divergence = 0.5 * (roll(east, -1, 0) - roll(east, 1, 0) + roll(north, -1, 1) - roll(north, 1, 1))
    v = [forcing - gravity * sea * divergence]
    own_diagonal = diagonal - SHIFT
    for _ in range(ITERS):
        x = v[-1]
        v.append(own_diagonal * x - sea * (both(x, 1, 0) + both(x, 1, 1)))
    v = [x[ROWS : 2 * ROWS, 0:LANES] for x in v]
    for k in range(ITERS):
        basis_ref[tile(k), :] = v[k]
    line = jnp.zeros((ROWS, LANES), F32)
    for k in range(2 * ITERS):
        part = jnp.sum(v[k // 2] * v[k - k // 2], axis=0, keepdims=True)
        line = jnp.where(row == k, part, line)
    line = jnp.sum(line, axis=1, keepdims=True)
    line = jnp.sum(jnp.where(row == lane, line, 0.0), axis=0, keepdims=True)
    send_ref[...] = jnp.broadcast_to(line, send_ref.shape)


def solve_kernel(got_ref, basis_ref, done_ref, out_ref):
    line = jnp.sum(got_ref[...], axis=0, keepdims=True)
    lane = iota(1, 1)
    moment = [jnp.sum(jnp.where(lane == k, line, 0.0), axis=1, keepdims=True) for k in range(2 * ITERS)]

    def dot(a, b):
        total = None
        for k in range(len(a) + len(b) - 1):
            weight = sum(a[n] * b[k - n] for n in range(len(a)) if 0 <= k - n < len(b))
            total = weight * moment[k] if total is None else total + weight * moment[k]
        return total

    def add(a, scale, b):
        out = list(a) + [0.0] * (len(b) - len(a))
        return [x + scale * b[n] if n < len(b) else x for n, x in enumerate(out)]

    def image(a):
        return [SHIFT * (a[n] if n < len(a) else 0.0) + (a[n - 1] if n else 0.0) for n in range(len(a) + 1)]

    one = jnp.ones((1, 1), F32)
    residual, direction, surface = [one], [one], []
    norm = dot(residual, residual)
    for iteration in range(ITERS):
        applied = image(direction)
        alpha = norm / dot(direction, applied)
        surface = add(surface, alpha, direction)
        if iteration + 1 < ITERS:
            residual = add(residual, -alpha, applied)
            following = dot(residual, residual)
            direction = add(residual, following / norm, direction)
            norm = following
    out = surface[0] * basis_ref[tile(0), :]
    for k in range(1, ITERS):
        out = out + surface[k] * basis_ref[tile(k), :]
    out_ref[...] = out


def step_kernel(
    m_ref, pack_ref, delta_ref, rows_one_ref, rows_two_ref, one_ref, two_ref, mask_ref, new_ref, done_ref, ext_ref, corr_ref
):
    lay = Layout(m_ref.shape[0] // ROWS)
    at = Place()
    row, lane = iota(0), iota(1)
    for t in range(lay.tiles):
        ext_ref[pl.ds(EXT * t + 2, ROWS), :] = m_ref[tile(t), :]
    for r in range(2):
        for s in range(lay.eights):
            one, two = rows_one_ref[tile(r * lay.eights + s), :], rows_two_ref[tile(r * lay.eights + s), :]
            ext_ref[pl.ds(EXT * ROWS * s + r, ROWS, stride=EXT), :] = at.from_up(one, two)
            ext_ref[pl.ds(EXT * ROWS * s + ROWS + 2 + r, ROWS, stride=EXT), :] = at.from_down(one, two)

    in_slot = lax.rem(lane, SLOT)
    half = in_slot < SLOT // 2
    near = (in_slot == 3) | (in_slot == 4)
    far = (in_slot >= 2) & (in_slot <= 5)
    sign = jnp.where(in_slot == 3, -0.5 * time_step, jnp.where(in_slot == 4, 0.5 * time_step, 0.0))
    for p in range(lay.packs):
        d = delta_ref[tile(p), :]
        one, two = one_ref[pl.ds(lay.delta + p, 1), :], two_ref[pl.ds(lay.delta + p, 1), :]
        dv = jnp.where(row == 0, at.from_up(one, two), roll(d, 1, 0)) + jnp.where(
            row == ROWS - 1, at.from_down(one, two), roll(d, -1, 0)
        )
        second = jnp.where(half, roll(d, -2, 1), roll(d, 2, 1))
        corr_ref[tile(p), :] = (
            jnp.where(far, -hyper_visc * second, 0.0)
            + jnp.where(near, across(hyper_visc * (8.0 * d - 2.0 * dv)), 0.0)
            + sign * spread(pack_ref[tile(p), :], 3) * across(d)
        )

    sea = mask_ref[...].astype(F32)
    done_ref[...] = sea
    edges = (
        jnp.where((row == 0) & (at.b == 0), 1.0, 0.0)
        + jnp.where((row == ROWS - 1) & (at.b == at.nb - 1), 1.0, 0.0)
        + jnp.where((lane == 0) & (at.g == 0), 1.0, 0.0)
        + jnp.where((lane == LANES - 1) & (at.g == at.ng - 1), 1.0, 0.0)
    )
    centre = 1.0 - 2.0 * mixing - hyper_visc * (20.0 - edges)
    col = (lane + at.g * LANES).astype(F32)
    coriolis = time_step * rotation * (2.0 * (col + 0.5) / (at.ng * LANES) - 1.0)
    border = (lane < SLOT // 2) | (lane >= LANES - SLOT // 2)

    def own(level, c):
        return m_ref[tile(COMPS * min(max(level, 0), lay.levels - 1) + c), :]

    for k in range(lay.levels):
        u, v = own(k, 2), own(k, 3)
        half_u, half_v = 0.5 * time_step * u, 0.5 * time_step * v
        for c in range(COMPS):
            t = COMPS * k + c
            x = own(k, c)
            up2, up1, dn1, dn2 = [ext_ref[pl.ds(EXT * t + n, ROWS), :] for n in (0, 1, 3, 4)]
            left, right = roll(x, 1, 1), roll(x, -1, 1)
            near1 = up1 + dn1
            q = 8.0 * hyper_visc * x - 2.0 * hyper_visc * near1
            out = (
                centre * x
                + (roll(q, 1, 1) + roll(q, -1, 1))
                + 8.0 * hyper_visc * near1
                - hyper_visc * ((up2 + dn2) + (roll(x, 2, 1) + roll(x, -2, 1)))
                - (half_u * (dn1 - up1) + half_v * (right - left))
                + mixing * (own(k - 1, c) + own(k + 1, c))
            )
            if c == 2:
                out = out + coriolis * v
            if c == 3:
                out = out - coriolis * u
            p, s = divmod(t, PER)
            fix = roll(corr_ref[tile(p), :], -(SLOT * s + SLOT // 2), 1)
            new_ref[tile(t), :] = sea * (out + jnp.where(border, fix, 0.0))


def call(kernel, outs, *args, scratch=(), specs=None, flops=0, vmem=8):
    return pl.pallas_call(
        kernel,
        out_shape=[jax.ShapeDtypeStruct(s, F32) if isinstance(s, tuple) else s for s in outs],
        in_specs=specs or [VMEM] * len(args),
        out_specs=[VMEM] * len(outs),
        scratch_shapes=[pltpu.VMEM(s, F32) if isinstance(s, tuple) else s for s in scratch],
        compiler_params=pltpu.CompilerParams(vmem_limit_bytes=vmem * 1024 * 1024),
        cost_estimate=pl.CostEstimate(flops=flops, bytes_accessed=0, transcendentals=0),
    )(*args)


def on_device(ocean_state, surface_height, surface_damping, land_mask, *, shape):
    nb, ng = shape
    axes = ("blocks", "group")
    state = ocean_state.reshape(-1, LANES)
    lay = Layout(state.shape[0] // ROWS)
    g_one, g_two = swap_pairs(shape, "group")
    b_one, b_two = swap_pairs(shape, "blocks")
    one_tile = (ROWS, LANES)
    packed = (lay.packs * ROWS, LANES)
    flats = (FLAT * ROWS, LANES)

    m, pack, flat = call(
        pack_kernel,
        [state.shape, (packed[0] + ROWS, LANES), flats],
        *[pltpu.with_memory_space_constraint(x, pltpu.HBM) for x in (state, land_mask, surface_height, surface_damping)],
        specs=[HBM] * 4,
        scratch=[
            state.shape,
            pltpu.VMEM(one_tile, land_mask.dtype),
            one_tile,
            one_tile,
            pltpu.SemaphoreType.DMA((3 + lay.packs,)),
        ],
    )
    first = lax.ppermute(pack, axes, g_one)
    second = lax.ppermute(pack, axes, g_two)
    rows_one, rows_two = call(rows_kernel, [(2 * lay.tiles, LANES)] * 2, m)
    rows_one = lax.ppermute(rows_one, axes, b_one)
    rows_two = lax.ppermute(rows_two, axes, b_two)
    message = (lay.message, LANES)
    own, near, delta, one, two = call(
        edge_kernel,
        [(flats[0] + ROWS, LANES), (2 * lay.pad, LANES), packed, message, message],
        m,
        pack,
        flat,
        first,
        second,
        flops=LONG,
    )
    one = lax.ppermute(one, axes, b_one)
    two = lax.ppermute(two, axes, b_two)
    (cross,) = call(cross_kernel, [one_tile], m, rows_one, rows_two)
    basis, sent = call(
        functools.partial(moment_kernel, levels=lay.levels),
        [(ITERS * ROWS, LANES), (nb * ng, LANES)],
        own,
        near,
        cross,
        one,
        two,
        scratch=[(FLAT * 3 * ROWS, 2 * LANES)],
        flops=LONG,
    )
    got = lax.all_to_all(sent, axes, 0, 0, tiled=True)
    new_state, done = call(
        step_kernel,
        [state.shape, one_tile],
        m,
        pack,
        delta,
        rows_one,
        rows_two,
        one,
        two,
        land_mask,
        scratch=[(lay.tiles * EXT, LANES), packed],
        flops=LONG,
    )
    (surface,) = call(solve_kernel, [one_tile], got, basis, done)
    return new_state.reshape(ocean_state.shape), surface


def solution(mesh):
    placed = (
        P(None, None, "blocks", "group"),
        P("blocks", "group"),
        P("blocks", "group"),
        P("blocks", "group"),
    )
    shape = (mesh.shape["blocks"], mesh.shape["group"])

    def body(*args):
        return on_device(*args, shape=shape)

    return jax.shard_map(
        body,
        mesh=mesh,
        in_specs=placed,
        out_specs=(P(None, None, "blocks", "group"), P("blocks", "group")),
        check_vma=False,
    )
```

```python
import functools

import jax
import jax.numpy as jnp
from jax import lax
from jax.experimental import pallas as pl
from jax.experimental.pallas import tpu as pltpu
from jax.sharding import PartitionSpec as P

ITERS = 3

time_step = 0.25
hyper_visc = 0.025
mixing = 0.2
gravity = 4.0
rotation = 0.2

COMPS = 4
ROWS = 8
LANES = 128
SLOT = 8
PER = LANES // SLOT
EXT = 12
FLAT = 6
STRIP = 16
LONG = 10**9
SHIFT = 4.5
F32 = jnp.float32
VMEM = pl.BlockSpec(memory_space=pltpu.VMEM)
HBM = pl.BlockSpec(memory_space=pltpu.HBM)


def iota(axis, rows=ROWS, lanes=LANES):
    return lax.broadcasted_iota(jnp.int32, (rows, lanes), axis)


def roll(x, shift, axis):
    return pltpu.roll(x, shift % x.shape[axis], axis)


def tile(k):
    return pl.ds(k * ROWS, ROWS)


def swap_pairs(mesh_shape, along):
    nb, ng = mesh_shape
    first, second = [], []
    for b in range(nb):
        for g in range(ng):
            me = b * ng + g
            if along == "blocks":
                one = (b ^ 1, g)
                two = ((b - 1) ^ 1) + 1
                two = (two, g) if 0 <= two < nb else (b, g ^ 1)
            else:
                one = (b, g ^ 1)
                two = ((g - 1) ^ 1) + 1
                two = (b, two) if 0 <= two < ng else (b ^ 1, g)
            first.append((me, one[0] * ng + one[1]))
            second.append((me, two[0] * ng + two[1]))
    return first, second


class Layout:
    def __init__(self, tiles):
        self.tiles = tiles
        self.levels = tiles // COMPS
        self.packs = tiles // PER
        self.eights = tiles // ROWS
        self.pad = -(-self.packs // ROWS) * ROWS
        self.flow = -(-self.levels // ROWS) * ROWS
        self.edge = 0
        self.delta = self.pad
        self.flat = 2 * self.pad
        self.strip = self.flat + FLAT * ROWS
        self.message = self.strip + ROWS


class Place:
    def __init__(self):
        self.b, self.nb = lax.axis_index("blocks"), lax.axis_size("blocks")
        self.g, self.ng = lax.axis_index("group"), lax.axis_size("group")
        self.b_even = lax.rem(self.b, 2) == 0
        self.g_even = lax.rem(self.g, 2) == 0
        self.up = (self.b > 0).astype(F32)
        self.down = (self.b < self.nb - 1).astype(F32)
        self.left = (self.g > 0).astype(F32)
        self.right = (self.g < self.ng - 1).astype(F32)

    def from_up(self, one, two):
        return jnp.where(self.b_even, two, one) * self.up

    def from_down(self, one, two):
        return jnp.where(self.b_even, one, two) * self.down


def pack_kernel(
    state_hbm, mask_hbm, height_hbm, damp_hbm, m_ref, pack_ref, flat_ref, state_ref, mask_ref, height_ref, damp_ref, sems
):
    lay = Layout(m_ref.shape[0] // ROWS)
    chunk = PER * ROWS
    small = [(mask_hbm, mask_ref), (height_hbm, height_ref), (damp_hbm, damp_ref)]
    copies = [pltpu.make_async_copy(a, b, sems.at[k]) for k, (a, b) in enumerate(small)]
    for p in range(lay.packs):
        at = pl.ds(p * chunk, chunk)
        copies.append(pltpu.make_async_copy(state_hbm.at[at], state_ref.at[at], sems.at[3 + p]))
    for copy in copies:
        copy.start()
    for copy in copies[: 3 + lay.packs // 2]:
        copy.wait()
    sea = mask_ref[...].astype(F32)
    row, lane = iota(0), iota(1)
    slot = lane // SLOT
    sum_u = sum_v = uu = uv = vu = zero = jnp.zeros((ROWS, LANES), F32)
    across_u = across_v = across_vu = zero
    for p in range(lay.packs):
        if p == lay.packs // 2:
            for copy in copies[3 + p :]:
                copy.wait()
        acc = zero
        for k in range(PER // COMPS):
            x = []
            for c in range(COMPS):
                q = COMPS * k + c
                x.append(state_ref[tile(p * PER + q), :] * sea)
                m_ref[tile(p * PER + q), :] = x[c]
                at = PER - 1 - q
                acc = jnp.where(slot == at, roll(x[c], SLOT * at + SLOT // 2, 1), acc)
            u, v = x[2:]
            below_u, below_v = roll(u, -1, 0), roll(v, -1, 0)
            right_u, right_v = roll(u, -1, 1), roll(v, -1, 1)
            sum_u, sum_v = sum_u + u, sum_v + v
            uu, uv, vu = uu + u * below_u, uv + u * below_v, vu + v * below_u
            across_u, across_v, across_vu = across_u + v * right_u, across_v + v * right_v, across_vu + u * right_v
        pack_ref[tile(p), :] = acc

    def step_down(ahead, back):
        inner = row < ROWS - 1
        return jnp.where(inner, ahead, 0.0) - roll(jnp.where(inner, back, 0.0), 1, 0)

    def step_right(ahead, back):
        inner = lane < LANES - 1
        return jnp.where(inner, ahead, 0.0) - roll(jnp.where(inner, back, 0.0), 1, 1)

    advect_u = 0.5 * (step_down(uu, uu) + step_right(across_u, across_vu))
    advect_v = 0.5 * (step_down(uv, vu) + step_right(across_v, across_v))
    damp = damp_ref[...]
    flat = [sum_u, sum_v, advect_u, advect_v, sea * damp * height_ref[...], sea * (4.0 + damp)]
    acc = jnp.zeros((ROWS, LANES), F32)
    for f in range(FLAT):
        flat_ref[tile(f), :] = flat[f]
        acc = jnp.where(lane // STRIP == f, roll(flat[f], STRIP * f + STRIP // 2, 1), acc)
    pack_ref[tile(lay.packs), :] = acc


def packed_comp(shape):
    return COMPS - 1 - lax.rem(lax.broadcasted_iota(jnp.int32, shape, 1) // SLOT, COMPS)


def unpack(x, t):
    return roll(x, -(SLOT * (PER - 1 - t % PER) + SLOT // 2), 1)


def spread(x, of):
    comp = packed_comp(x.shape)
    out = x
    for c in range(COMPS):
        if c != of:
            out = jnp.where(comp == c, roll(x, SLOT * (of - c), 1), out)
    return out


def across(x):
    half = lax.rem(lax.broadcasted_iota(jnp.int32, x.shape, 1), SLOT) < SLOT // 2
    return jnp.where(half, roll(x, -1, 1), roll(x, 1, 1))


def fold(x):
    step = SLOT * COMPS
    while step < LANES:
        x = x + roll(x, step, 1)
        step *= 2
    return x


def edge_kernel(
    m_ref, pack_ref, flat_ref, first_ref, second_ref, own_ref, near_ref, delta_ref, one_ref, two_ref
):
    lay = Layout(m_ref.shape[0] // ROWS)
    at = Place()
    lane = iota(1)
    in_slot = lax.rem(lane, SLOT)
    half = in_slot < SLOT // 2
    sign = jnp.where(in_slot == SLOT // 2 - 1, 0.5, jnp.where(in_slot == SLOT // 2, -0.5, 0.0))

    def beyond(p, low):
        first, second = first_ref[tile(p), :], second_ref[tile(p), :]
        from_left = jnp.where(at.g_even, second, first) * at.left
        from_right = jnp.where(at.g_even, first, second) * at.right
        return jnp.where(low, from_left, from_right)

    near_ref[...] = jnp.zeros(near_ref.shape, F32)
    inner = jnp.zeros((ROWS, LANES), F32)
    outer = jnp.zeros((ROWS, LANES), F32)
    for p in range(lay.packs):
        own, far = pack_ref[tile(p), :], beyond(p, half)
        delta_ref[tile(p), :] = far - own
        near_ref[p : p + 1, :] = far[0:1]
        near_ref[lay.pad + p : lay.pad + p + 1, :] = far[ROWS - 1 : ROWS]
        inner = inner + spread(own, 3) * across(far)
        outer = outer + spread(far, 3) * across(own)
    inner, outer = fold(sign * inner), fold(sign * outer)
    strip = beyond(lay.packs, lax.rem(lane, STRIP) < STRIP // 2)
    for f in range(FLAT):
        value = flat_ref[tile(f), :]
        if 2 <= f <= 3:
            border = (lane == 0) | (lane == LANES - 1)
            value = value + jnp.where(border, unpack(inner, f), 0.0)
            mid = STRIP * f + STRIP // 2
            border = (lane == mid - 1) | (lane == mid)
            strip = strip + jnp.where(border, roll(unpack(outer, f), mid, 1), 0.0)
        own_ref[tile(f), :] = value
    own_ref[tile(FLAT), :] = strip

    def fill(low_ref, high_ref):
        for ref, row, rows in ((low_ref, 0, slice(0, lay.pad)), (high_ref, ROWS - 1, slice(lay.pad, 2 * lay.pad))):
            ref[pl.ds(lay.edge, lay.pad), :] = near_ref[rows, :]
            ref[pl.ds(lay.delta, lay.pad), :] = jnp.zeros((lay.pad, LANES), F32)
            for p in range(lay.packs):
                ref[pl.ds(lay.delta + p, 1), :] = delta_ref[pl.ds(ROWS * p + row, 1), :]
            ref[pl.ds(lay.flat, (FLAT + 1) * ROWS), :] = own_ref[...]

    pl.when(at.b_even)(lambda: fill(two_ref, one_ref))
    pl.when(jnp.logical_not(at.b_even))(lambda: fill(one_ref, two_ref))


def rows_kernel(m_ref, one_ref, two_ref):
    lay = Layout(m_ref.shape[0] // ROWS)

    def fill(low_ref, high_ref):
        for ref, row in ((low_ref, 0), (high_ref, ROWS - 2)):
            for r in range(2):
                for s in range(lay.eights):
                    at = pl.ds(ROWS * ROWS * s + row + r, ROWS, stride=ROWS)
                    ref[tile(r * lay.eights + s), :] = m_ref[at, :]

    even = Place().b_even
    pl.when(even)(lambda: fill(two_ref, one_ref))
    pl.when(jnp.logical_not(even))(lambda: fill(one_ref, two_ref))


def cross_kernel(m_ref, one_ref, two_ref, cross_ref):
    lay = Layout(m_ref.shape[0] // ROWS)
    at = Place()
    row = iota(0)

    def level_rows(ref, comp, first, count_rows):
        parts = []
        for start in range(0, lay.levels, ROWS):
            count = min(ROWS, lay.levels - start)
            x = ref[pl.ds((start * COMPS + comp) * count_rows + first, count, stride=COMPS * count_rows), :]
            if count < ROWS:
                x = jnp.concatenate([x, jnp.zeros((ROWS - count, LANES), F32)], axis=0)
            parts.append(x)
        return parts

    def beyond(first):
        return [[level_rows(ref, c, first, 1) for c in (2, 3)] for ref in (one_ref, two_ref)]

    one, two = beyond(lay.tiles)
    above = [[at.from_up(x, y) for x, y in zip(one[c], two[c])] for c in range(2)]
    one, two = beyond(0)
    below = [[at.from_down(x, y) for x, y in zip(one[c], two[c])] for c in range(2)]
    top, bottom = [[level_rows(m_ref, c, r, ROWS) for c in (2, 3)] for r in (0, ROWS - 1)]

    def total(flow, carried):
        return 0.5 * jnp.sum(sum(x * y for x, y in zip(flow, carried)), axis=0, keepdims=True)

    out = jnp.zeros((ROWS, LANES), F32)
    for f in range(2):
        sums = (total(above[0], top[f]), -total(top[0], above[f]), total(bottom[0], below[f]), -total(below[0], bottom[f]))
        for k in range(4):
            out = jnp.where(row == 4 * f + k, sums[k], out)
    cross_ref[...] = out


def moment_kernel(own_ref, near_ref, cross_ref, one_ref, two_ref, done_ref, basis_ref, send_ref, wide_ref, *, levels):
    lay = Layout(levels * COMPS)
    at = Place()
    row, lane = iota(0), iota(1)
    outside = (lane < STRIP // 2) | (lane >= LANES - STRIP // 2)
    rows = 3 * ROWS

    def neighbours(where):
        return at.from_up(one_ref[where, :], two_ref[where, :]), at.from_down(one_ref[where, :], two_ref[where, :])

    strips = neighbours(pl.ds(lay.strip, ROWS))
    strips = (strips[0], own_ref[tile(FLAT), :], strips[1])
    for f in range(FLAT):
        fields = neighbours(pl.ds(lay.flat + f * ROWS, ROWS))
        fields = (fields[0], own_ref[tile(f), :], fields[1])
        for k in range(3):
            to = pl.ds(f * rows + k * ROWS, ROWS)
            wide_ref[to, 0:LANES] = fields[k]
            side = roll(strips[k], -(STRIP * f + STRIP // 2), 1)
            wide_ref[to, LANES : 2 * LANES] = jnp.where(outside, side, 0.0)

    above, below = neighbours(pl.ds(lay.edge, lay.pad))
    top, bottom = near_ref[0 : lay.pad, :], near_ref[lay.pad :, :]

    def flow_packed(x):
        return roll(x, -SLOT, 1)

    def corner(a, b):
        x = jnp.where(packed_comp(a.shape) == 3, flow_packed(a), a) * b
        return 0.5 * fold(jnp.sum(x, axis=0, keepdims=True))

    corners = [corner(above, top), -corner(top, above), corner(bottom, below), -corner(below, bottom)]
    border = (iota(1, 1) < SLOT // 2) | (iota(1, 1) >= LANES - SLOT // 2)
    for f in (2, 3):
        for k, at_row in enumerate((ROWS - 1, ROWS, 2 * ROWS - 1, 2 * ROWS)):
            to = pl.ds(f * rows + at_row, 1)
            wide_ref[to, 0:LANES] = wide_ref[to, 0:LANES] + cross_ref[4 * (f - 2) + k : 4 * (f - 2) + k + 1, :]
            side = unpack(corners[k], f)
            wide_ref[to, LANES : 2 * LANES] = wide_ref[to, LANES : 2 * LANES] + jnp.where(border, side, 0.0)

    sum_u, sum_v, adv_u, adv_v, forcing, diagonal = [wide_ref[pl.ds(f * rows, rows), :] for f in range(FLAT)]
    sea = jnp.where(diagonal > 0.0, 1.0, 0.0)
    shape = (rows, 2 * LANES)
    i = iota(0, *shape) - ROWS + at.b * ROWS
    j = iota(1, *shape)
    j = jnp.where(j < LANES + LANES // 2, j, j - 2 * LANES) + at.g * LANES
    total_rows, total_cols = at.nb * ROWS, at.ng * LANES
    edges = (
        jnp.where(i == 0, 1.0, 0.0)
        + jnp.where(i == total_rows - 1, 1.0, 0.0)
        + jnp.where(j == 0, 1.0, 0.0)
        + jnp.where(j == total_cols - 1, 1.0, 0.0)
    )
    coriolis = rotation * (2.0 * (j.astype(F32) + 0.5) / total_cols - 1.0)

    def both(x, n, axis):
        return roll(x, n, axis) + roll(x, -n, axis)

    def transport(x, turn, adv):
        near = both(x, 1, 0)
        linear = (
            (1.0 - hyper_visc * (20.0 - edges)) * x
            + 8.0 * hyper_visc * near
            - hyper_visc * (both(x, 2, 0) + both(x, 2, 1))
            + both(8.0 * hyper_visc * x - 2.0 * hyper_visc * near, 1, 1)
        )
        return sea * (linear + time_step * (turn - adv)) / lay.levels

    east = transport(sum_u, coriolis * sum_v, adv_u)
    north = transport(sum_v, -coriolis * sum_u, adv_v)
    divergence = 0.5 * (roll(east, -1, 0) - roll(east, 1, 0) + roll(north, -1, 1) - roll(north, 1, 1))
    v = [forcing - gravity * sea * divergence]
    own_diagonal = diagonal - SHIFT
    for _ in range(ITERS):
        x = v[-1]
        v.append(own_diagonal * x - sea * (both(x, 1, 0) + both(x, 1, 1)))
    v = [x[ROWS : 2 * ROWS, 0:LANES] for x in v]
    for k in range(ITERS):
        basis_ref[tile(k), :] = v[k]
    line = jnp.zeros((ROWS, LANES), F32)
    for k in range(2 * ITERS):
        part = jnp.sum(v[k // 2] * v[k - k // 2], axis=0, keepdims=True)
        line = jnp.where(row == k, part, line)
    line = jnp.sum(line, axis=1, keepdims=True)
    line = jnp.sum(jnp.where(row == lane, line, 0.0), axis=0, keepdims=True)
    send_ref[...] = jnp.broadcast_to(line, send_ref.shape)


def solve_kernel(
    got_ref, basis_ref, one_ref, two_ref, mask_ref, state_in, state_ref, state_hbm, surface_hbm, surface_ref, sems
):
    lay = Layout(state_ref.shape[0] // ROWS)
    at = Place()
    place = pl.ds(lay.delta, lay.pad)
    one, two = one_ref[place, :], two_ref[place, :]
    in_slot = lax.rem(iota(1, lay.pad), SLOT)
    border = (iota(1) < SLOT // 2) | (iota(1) >= LANES - SLOT // 2)
    near = (in_slot == SLOT // 2 - 1) | (in_slot == SLOT // 2)
    sea = mask_ref[...].astype(F32)
    for row, delta in ((0, at.from_up(one, two)), (ROWS - 1, at.from_down(one, two))):
        fix = jnp.where(near, across(-2.0 * hyper_visc * delta), 0.0)
        for s in range(lay.eights):
            p, q = divmod(s * ROWS, PER)
            x = jnp.broadcast_to(fix[p : p + 1], (ROWS, LANES))
            x = pltpu.roll(x, SLOT * q + SLOT // 2, 1, stride=SLOT, stride_axis=0)
            to = pl.ds(ROWS * ROWS * s + row, ROWS, stride=ROWS)
            state_ref[to, :] = state_ref[to, :] + sea[row : row + 1] * jnp.where(border, x, 0.0)
    write = pltpu.make_async_copy(state_ref, state_hbm, sems.at[0])
    write.start()

    line = jnp.sum(got_ref[...], axis=0, keepdims=True)
    lane = iota(1, 1)
    moment = [jnp.sum(jnp.where(lane == k, line, 0.0), axis=1, keepdims=True) for k in range(2 * ITERS)]

    def dot(a, b):
        total = None
        for k in range(len(a) + len(b) - 1):
            weight = sum(a[n] * b[k - n] for n in range(len(a)) if 0 <= k - n < len(b))
            total = weight * moment[k] if total is None else total + weight * moment[k]
        return total

    def add(a, scale, b):
        out = list(a) + [0.0] * (len(b) - len(a))
        return [x + scale * b[n] if n < len(b) else x for n, x in enumerate(out)]

    def image(a):
        return [SHIFT * (a[n] if n < len(a) else 0.0) + (a[n - 1] if n else 0.0) for n in range(len(a) + 1)]

    one = jnp.ones((1, 1), F32)
    residual, direction, surface = [one], [one], []
    norm = dot(residual, residual)
    for iteration in range(ITERS):
        applied = image(direction)
        alpha = norm / dot(direction, applied)
        surface = add(surface, alpha, direction)
        if iteration + 1 < ITERS:
            residual = add(residual, -alpha, applied)
            following = dot(residual, residual)
            direction = add(residual, following / norm, direction)
            norm = following
    out = surface[0] * basis_ref[tile(0), :]
    for k in range(1, ITERS):
        out = out + surface[k] * basis_ref[tile(k), :]
    surface_ref[...] = out
    write_surface = pltpu.make_async_copy(surface_ref, surface_hbm, sems.at[1])
    write_surface.start()
    write.wait()
    write_surface.wait()


def step_kernel(m_ref, pack_ref, delta_ref, rows_one_ref, rows_two_ref, mask_ref, new_ref, done_ref, ext_ref, corr_ref):
    lay = Layout(m_ref.shape[0] // ROWS)
    at = Place()
    row, lane = iota(0), iota(1)
    for t in range(lay.tiles):
        ext_ref[pl.ds(EXT * t + 2, ROWS), :] = m_ref[tile(t), :]
    for r in range(2):
        for s in range(lay.eights):
            one, two = rows_one_ref[tile(r * lay.eights + s), :], rows_two_ref[tile(r * lay.eights + s), :]
            ext_ref[pl.ds(EXT * ROWS * s + r, ROWS, stride=EXT), :] = at.from_up(one, two)
            ext_ref[pl.ds(EXT * ROWS * s + ROWS + 2 + r, ROWS, stride=EXT), :] = at.from_down(one, two)

    in_slot = lax.rem(lane, SLOT)
    half = in_slot < SLOT // 2
    near = (in_slot == 3) | (in_slot == 4)
    far = (in_slot >= 2) & (in_slot <= 5)
    sign = jnp.where(in_slot == 3, -0.5 * time_step, jnp.where(in_slot == 4, 0.5 * time_step, 0.0))
    for p in range(lay.packs):
        d = delta_ref[tile(p), :]
        dv = jnp.where(row == 0, 0.0, roll(d, 1, 0)) + jnp.where(row == ROWS - 1, 0.0, roll(d, -1, 0))
        second = jnp.where(half, roll(d, -2, 1), roll(d, 2, 1))
        corr_ref[tile(p), :] = (
            jnp.where(far, -hyper_visc * second, 0.0)
            + jnp.where(near, across(hyper_visc * (8.0 * d - 2.0 * dv)), 0.0)
            + sign * spread(pack_ref[tile(p), :], 3) * across(d)
        )

    sea = mask_ref[...].astype(F32)
    done_ref[...] = sea
    edges = (
        jnp.where((row == 0) & (at.b == 0), 1.0, 0.0)
        + jnp.where((row == ROWS - 1) & (at.b == at.nb - 1), 1.0, 0.0)
        + jnp.where((lane == 0) & (at.g == 0), 1.0, 0.0)
        + jnp.where((lane == LANES - 1) & (at.g == at.ng - 1), 1.0, 0.0)
    )
    centre = 1.0 - 2.0 * mixing - hyper_visc * (20.0 - edges)
    col = (lane + at.g * LANES).astype(F32)
    coriolis = time_step * rotation * (2.0 * (col + 0.5) / (at.ng * LANES) - 1.0)
    border = (lane < SLOT // 2) | (lane >= LANES - SLOT // 2)

    def own(level, c):
        return m_ref[tile(COMPS * min(max(level, 0), lay.levels - 1) + c), :]

    for k in range(lay.levels):
        u, v = own(k, 2), own(k, 3)
        half_u, half_v = 0.5 * time_step * u, 0.5 * time_step * v
        for c in range(COMPS):
            t = COMPS * k + c
            x = own(k, c)
            up2, up1, dn1, dn2 = [ext_ref[pl.ds(EXT * t + n, ROWS), :] for n in (0, 1, 3, 4)]
            left, right = roll(x, 1, 1), roll(x, -1, 1)
            near1 = up1 + dn1
            q = 8.0 * hyper_visc * x - 2.0 * hyper_visc * near1
            out = (
                centre * x
                + (roll(q, 1, 1) + roll(q, -1, 1))
                + 8.0 * hyper_visc * near1
                - hyper_visc * ((up2 + dn2) + (roll(x, 2, 1) + roll(x, -2, 1)))
                - (half_u * (dn1 - up1) + half_v * (right - left))
                + mixing * (own(k - 1, c) + own(k + 1, c))
            )
            if c == 2:
                out = out + coriolis * v
            if c == 3:
                out = out - coriolis * u
            fix = unpack(corr_ref[tile(t // PER), :], t)
            new_ref[tile(t), :] = sea * (out + jnp.where(border, fix, 0.0))


def call(kernel, outs, *args, scratch=(), specs=None, out_specs=None, aliases=None, flops=0):
    return pl.pallas_call(
        kernel,
        out_shape=[jax.ShapeDtypeStruct(s, F32) for s in outs],
        in_specs=specs or [VMEM] * len(args),
        out_specs=out_specs or [VMEM] * len(outs),
        scratch_shapes=[pltpu.VMEM(s, F32) if isinstance(s, tuple) else s for s in scratch],
        input_output_aliases=aliases or {},
        compiler_params=pltpu.CompilerParams(vmem_limit_bytes=8 * 1024 * 1024),
        cost_estimate=pl.CostEstimate(flops=flops, bytes_accessed=0, transcendentals=0),
    )(*args)


def on_device(ocean_state, surface_height, surface_damping, land_mask, *, shape):
    nb, ng = shape
    axes = ("blocks", "group")
    state = ocean_state.reshape(-1, LANES)
    lay = Layout(state.shape[0] // ROWS)
    g_one, g_two = swap_pairs(shape, "group")
    b_one, b_two = swap_pairs(shape, "blocks")
    one_tile = (ROWS, LANES)
    packed = (lay.packs * ROWS, LANES)
    flats = (FLAT * ROWS, LANES)

    m, pack, flat = call(
        pack_kernel,
        [state.shape, (packed[0] + ROWS, LANES), flats],
        *[pltpu.with_memory_space_constraint(x, pltpu.HBM) for x in (state, land_mask, surface_height, surface_damping)],
        specs=[HBM] * 4,
        scratch=[
            state.shape,
            pltpu.VMEM(one_tile, land_mask.dtype),
            one_tile,
            one_tile,
            pltpu.SemaphoreType.DMA((3 + lay.packs,)),
        ],
    )
    first = lax.ppermute(pack, axes, g_one)
    second = lax.ppermute(pack, axes, g_two)
    rows_one, rows_two = call(rows_kernel, [(2 * lay.tiles, LANES)] * 2, m)
    rows_one = lax.ppermute(rows_one, axes, b_one)
    rows_two = lax.ppermute(rows_two, axes, b_two)
    message = (lay.message, LANES)
    own, near, delta, one, two = call(
        edge_kernel,
        [(flats[0] + ROWS, LANES), (2 * lay.pad, LANES), packed, message, message],
        m,
        pack,
        flat,
        first,
        second,
        flops=10 * LONG,
    )
    one = lax.ppermute(one, axes, b_one)
    two = lax.ppermute(two, axes, b_two)
    (cross,) = call(cross_kernel, [one_tile], m, rows_one, rows_two)
    part, done = call(
        step_kernel,
        [state.shape, one_tile],
        m,
        pack,
        delta,
        rows_one,
        rows_two,
        land_mask,
        scratch=[(lay.tiles * EXT, LANES), packed],
        flops=LONG,
    )
    basis, sent = call(
        functools.partial(moment_kernel, levels=lay.levels),
        [(ITERS * ROWS, LANES), (nb * ng, LANES)],
        own,
        near,
        cross,
        one,
        two,
        done,
        scratch=[(FLAT * 3 * ROWS, 2 * LANES)],
        flops=LONG,
    )
    got = lax.all_to_all(sent, axes, 0, 0, tiled=True)
    _, new_state, surface = call(
        solve_kernel,
        [state.shape, state.shape, one_tile],
        got,
        basis,
        one,
        two,
        land_mask,
        part,
        scratch=[one_tile, pltpu.SemaphoreType.DMA((2,))],
        out_specs=[VMEM, HBM, HBM],
        aliases={5: 0},
    )
    return new_state.reshape(ocean_state.shape), surface


def solution(mesh):
    placed = (
        P(None, None, "blocks", "group"),
        P("blocks", "group"),
        P("blocks", "group"),
        P("blocks", "group"),
    )
    shape = (mesh.shape["blocks"], mesh.shape["group"])

    def body(*args):
        return on_device(*args, shape=shape)

    return jax.shard_map(
        body,
        mesh=mesh,
        in_specs=placed,
        out_specs=(P(None, None, "blocks", "group"), P("blocks", "group")),
        check_vma=False,
    )
```

```python
import functools

import jax
import jax.numpy as jnp
from jax import lax
from jax.experimental import pallas as pl
from jax.experimental.pallas import tpu as pltpu
from jax.sharding import PartitionSpec as P

ITERS = 3

time_step = 0.25
hyper_visc = 0.025
mixing = 0.2
gravity = 4.0
rotation = 0.2

COMPS = 4
ROWS = 8
LANES = 128
SLOT = 8
PER = LANES // SLOT
FLAT = 6
STRIP = 16
LONG = 10**9
SHIFT = 4.5
F32 = jnp.float32
VMEM = pl.BlockSpec(memory_space=pltpu.VMEM)
HBM = pl.BlockSpec(memory_space=pltpu.HBM)


def iota(axis, rows=ROWS, lanes=LANES):
    return lax.broadcasted_iota(jnp.int32, (rows, lanes), axis)


def roll(x, shift, axis):
    return pltpu.roll(x, shift % x.shape[axis], axis)


def tile(k):
    return pl.ds(k * ROWS, ROWS)


def swap_pairs(mesh_shape, along):
    nb, ng = mesh_shape
    first, second = [], []
    for b in range(nb):
        for g in range(ng):
            me = b * ng + g
            if along == "blocks":
                one = (b ^ 1, g)
                two = ((b - 1) ^ 1) + 1
                two = (two, g) if 0 <= two < nb else (b, g ^ 1)
            else:
                one = (b, g ^ 1)
                two = ((g - 1) ^ 1) + 1
                two = (b, two) if 0 <= two < ng else (b ^ 1, g)
            first.append((me, one[0] * ng + one[1]))
            second.append((me, two[0] * ng + two[1]))
    return first, second


class Layout:
    def __init__(self, tiles):
        self.tiles = tiles
        self.levels = tiles // COMPS
        self.packs = tiles // PER
        self.eights = tiles // ROWS
        self.pad = -(-self.packs // ROWS) * ROWS
        self.flow = -(-self.levels // ROWS) * ROWS
        self.edge = 0
        self.flat = self.pad
        self.strip = self.flat + FLAT * ROWS
        self.message = self.strip + ROWS
        self.delta = 2 * tiles
        self.rest = self.delta + self.pad


class Place:
    def __init__(self):
        self.b, self.nb = lax.axis_index("blocks"), lax.axis_size("blocks")
        self.g, self.ng = lax.axis_index("group"), lax.axis_size("group")
        self.b_even = lax.rem(self.b, 2) == 0
        self.g_even = lax.rem(self.g, 2) == 0
        self.up = (self.b > 0).astype(F32)
        self.down = (self.b < self.nb - 1).astype(F32)
        self.left = (self.g > 0).astype(F32)
        self.right = (self.g < self.ng - 1).astype(F32)

    def from_up(self, one, two):
        return jnp.where(self.b_even, two, one) * self.up

    def from_down(self, one, two):
        return jnp.where(self.b_even, one, two) * self.down


def pack_kernel(
    state_hbm, mask_hbm, height_hbm, damp_hbm, m_ref, pack_ref, flat_ref, state_ref, mask_ref, height_ref, damp_ref, sems
):
    lay = Layout(m_ref.shape[0] // ROWS)
    chunk = PER * ROWS
    small = [(mask_hbm, mask_ref), (height_hbm, height_ref), (damp_hbm, damp_ref)]
    copies = [pltpu.make_async_copy(a, b, sems.at[k]) for k, (a, b) in enumerate(small)]
    for p in range(lay.packs):
        at = pl.ds(p * chunk, chunk)
        copies.append(pltpu.make_async_copy(state_hbm.at[at], state_ref.at[at], sems.at[3 + p]))
    for copy in copies:
        copy.start()
    for copy in copies[: 3 + lay.packs // 2]:
        copy.wait()
    sea = mask_ref[...].astype(F32)
    row, lane = iota(0), iota(1)
    slot = lane // SLOT
    sum_u = sum_v = uu = uv = vu = zero = jnp.zeros((ROWS, LANES), F32)
    across_u = across_v = across_vu = zero
    for p in range(lay.packs):
        if p == lay.packs // 2:
            for copy in copies[3 + p :]:
                copy.wait()
        acc = zero
        for k in range(PER // COMPS):
            x = []
            for c in range(COMPS):
                q = COMPS * k + c
                x.append(state_ref[tile(p * PER + q), :] * sea)
                m_ref[tile(p * PER + q), :] = x[c]
                at = PER - 1 - q
                acc = jnp.where(slot == at, roll(x[c], SLOT * at + SLOT // 2, 1), acc)
            u, v = x[2:]
            below_u, below_v = roll(u, -1, 0), roll(v, -1, 0)
            right_u, right_v = roll(u, -1, 1), roll(v, -1, 1)
            sum_u, sum_v = sum_u + u, sum_v + v
            uu, uv, vu = uu + u * below_u, uv + u * below_v, vu + v * below_u
            across_u, across_v, across_vu = across_u + v * right_u, across_v + v * right_v, across_vu + u * right_v
        pack_ref[tile(p), :] = acc

    def step_down(ahead, back):
        inner = row < ROWS - 1
        return jnp.where(inner, ahead, 0.0) - roll(jnp.where(inner, back, 0.0), 1, 0)

    def step_right(ahead, back):
        inner = lane < LANES - 1
        return jnp.where(inner, ahead, 0.0) - roll(jnp.where(inner, back, 0.0), 1, 1)

    advect_u = 0.5 * (step_down(uu, uu) + step_right(across_u, across_vu))
    advect_v = 0.5 * (step_down(uv, vu) + step_right(across_v, across_v))
    damp = damp_ref[...]
    flat = [sum_u, sum_v, advect_u, advect_v, sea * damp * height_ref[...], sea * (4.0 + damp)]
    acc = jnp.zeros((ROWS, LANES), F32)
    for f in range(FLAT):
        flat_ref[tile(f), :] = flat[f]
        acc = jnp.where(lane // STRIP == f, roll(flat[f], STRIP * f + STRIP // 2, 1), acc)
    pack_ref[tile(lay.packs), :] = acc


def packed_comp(shape):
    return COMPS - 1 - lax.rem(lax.broadcasted_iota(jnp.int32, shape, 1) // SLOT, COMPS)


def unpack(x, t):
    return roll(x, -(SLOT * (PER - 1 - t % PER) + SLOT // 2), 1)


def spread(x, of):
    comp = packed_comp(x.shape)
    out = x
    for c in range(COMPS):
        if c != of:
            out = jnp.where(comp == c, roll(x, SLOT * (of - c), 1), out)
    return out


def across(x):
    half = lax.rem(lax.broadcasted_iota(jnp.int32, x.shape, 1), SLOT) < SLOT // 2
    return jnp.where(half, roll(x, -1, 1), roll(x, 1, 1))


def fold(x):
    step = SLOT * COMPS
    while step < LANES:
        x = x + roll(x, step, 1)
        step *= 2
    return x


def edge_kernel(
    m_ref, pack_ref, flat_ref, first_ref, second_ref, done_ref, own_ref, near_ref, delta_ref, one_ref, two_ref
):
    lay = Layout(m_ref.shape[0] // ROWS)
    at = Place()
    lane = iota(1)
    in_slot = lax.rem(lane, SLOT)
    half = in_slot < SLOT // 2
    sign = jnp.where(in_slot == SLOT // 2 - 1, 0.5, jnp.where(in_slot == SLOT // 2, -0.5, 0.0))

    def beyond(p, low):
        first, second = first_ref[tile(p), :], second_ref[tile(p), :]
        from_left = jnp.where(at.g_even, second, first) * at.left
        from_right = jnp.where(at.g_even, first, second) * at.right
        return jnp.where(low, from_left, from_right)

    near_ref[...] = jnp.zeros(near_ref.shape, F32)
    inner = jnp.zeros((ROWS, LANES), F32)
    outer = jnp.zeros((ROWS, LANES), F32)
    for p in range(lay.packs):
        own, far = pack_ref[tile(p), :], beyond(p, half)
        delta_ref[tile(p), :] = far - own
        near_ref[p : p + 1, :] = far[0:1]
        near_ref[lay.pad + p : lay.pad + p + 1, :] = far[ROWS - 1 : ROWS]
        inner = inner + spread(own, 3) * across(far)
        outer = outer + spread(far, 3) * across(own)
    inner, outer = fold(sign * inner), fold(sign * outer)
    strip = beyond(lay.packs, lax.rem(lane, STRIP) < STRIP // 2)
    for f in range(FLAT):
        value = flat_ref[tile(f), :]
        if 2 <= f <= 3:
            border = (lane == 0) | (lane == LANES - 1)
            value = value + jnp.where(border, unpack(inner, f), 0.0)
            mid = STRIP * f + STRIP // 2
            border = (lane == mid - 1) | (lane == mid)
            strip = strip + jnp.where(border, roll(unpack(outer, f), mid, 1), 0.0)
        own_ref[tile(f), :] = value
    own_ref[tile(FLAT), :] = strip

    def fill(low_ref, high_ref):
        for ref, rows in ((low_ref, slice(0, lay.pad)), (high_ref, slice(lay.pad, 2 * lay.pad))):
            ref[pl.ds(lay.edge, lay.pad), :] = near_ref[rows, :]
            ref[pl.ds(lay.flat, (FLAT + 1) * ROWS), :] = own_ref[...]

    pl.when(at.b_even)(lambda: fill(two_ref, one_ref))
    pl.when(jnp.logical_not(at.b_even))(lambda: fill(one_ref, two_ref))


def level_rows(m_ref, comp, row):
    lay = Layout(m_ref.shape[0] // ROWS)
    step = COMPS * ROWS
    parts = []
    for start in range(0, lay.levels, ROWS):
        count = min(ROWS, lay.levels - start)
        x = m_ref[pl.ds(start * step + comp * ROWS + row, count, stride=step), :]
        if count < ROWS:
            x = jnp.concatenate([x, jnp.zeros((ROWS - count, LANES), F32)], axis=0)
        parts.append(x)
    return parts


def flow_kernel(m_ref, one_ref, two_ref):
    lay = Layout(m_ref.shape[0] // ROWS)

    def fill(low_ref, high_ref):
        for ref, row in ((low_ref, 0), (high_ref, ROWS - 1)):
            for c in range(2):
                for n, x in enumerate(level_rows(m_ref, 2 + c, row)):
                    ref[pl.ds(c * lay.flow + n * ROWS, ROWS), :] = x

    even = Place().b_even
    pl.when(even)(lambda: fill(two_ref, one_ref))
    pl.when(jnp.logical_not(even))(lambda: fill(one_ref, two_ref))


def rest_kernel(m_ref, delta_ref, after_ref, one_ref, two_ref):
    lay = Layout(m_ref.shape[0] // ROWS)

    def fill(low_ref, high_ref):
        for ref, row, near in ((low_ref, 0, 0), (high_ref, ROWS - 2, ROWS - 1)):
            for r in range(2):
                for s in range(lay.eights):
                    at = pl.ds(ROWS * ROWS * s + row + r, ROWS, stride=ROWS)
                    ref[tile(r * lay.eights + s), :] = m_ref[at, :]
            ref[pl.ds(lay.delta, lay.pad), :] = jnp.zeros((lay.pad, LANES), F32)
            for p in range(lay.packs):
                ref[pl.ds(lay.delta + p, 1), :] = delta_ref[pl.ds(ROWS * p + near, 1), :]

    even = Place().b_even
    pl.when(even)(lambda: fill(two_ref, one_ref))
    pl.when(jnp.logical_not(even))(lambda: fill(one_ref, two_ref))


def cross_kernel(m_ref, one_ref, two_ref, cross_ref):
    lay = Layout(m_ref.shape[0] // ROWS)
    at = Place()
    row = iota(0)
    count = lay.flow // ROWS

    def beyond(take, c):
        where = [pl.ds(c * lay.flow + n * ROWS, ROWS) for n in range(count)]
        return [take(one_ref[w, :], two_ref[w, :]) for w in where]

    above, below = [[beyond(take, c) for c in range(2)] for take in (at.from_up, at.from_down)]
    top, bottom = [[level_rows(m_ref, c, r) for c in (2, 3)] for r in (0, ROWS - 1)]

    def total(flow, carried):
        return 0.5 * jnp.sum(sum(x * y for x, y in zip(flow, carried)), axis=0, keepdims=True)

    out = jnp.zeros((ROWS, LANES), F32)
    for f in range(2):
        sums = (total(above[0], top[f]), -total(top[0], above[f]), total(bottom[0], below[f]), -total(below[0], bottom[f]))
        for k in range(4):
            out = jnp.where(row == 4 * f + k, sums[k], out)
    cross_ref[...] = out


def moment_kernel(own_ref, near_ref, cross_ref, one_ref, two_ref, done_ref, basis_ref, send_ref, wide_ref, *, levels):
    lay = Layout(levels * COMPS)
    at = Place()
    row, lane = iota(0), iota(1)
    outside = (lane < STRIP // 2) | (lane >= LANES - STRIP // 2)
    rows = 3 * ROWS

    def neighbours(where):
        return at.from_up(one_ref[where, :], two_ref[where, :]), at.from_down(one_ref[where, :], two_ref[where, :])

    strips = neighbours(pl.ds(lay.strip, ROWS))
    strips = (strips[0], own_ref[tile(FLAT), :], strips[1])
    for f in range(FLAT):
        fields = neighbours(pl.ds(lay.flat + f * ROWS, ROWS))
        fields = (fields[0], own_ref[tile(f), :], fields[1])
        for k in range(3):
            to = pl.ds(f * rows + k * ROWS, ROWS)
            wide_ref[to, 0:LANES] = fields[k]
            side = roll(strips[k], -(STRIP * f + STRIP // 2), 1)
            wide_ref[to, LANES : 2 * LANES] = jnp.where(outside, side, 0.0)

    above, below = neighbours(pl.ds(lay.edge, lay.pad))
    top, bottom = near_ref[0 : lay.pad, :], near_ref[lay.pad :, :]

    def flow_packed(x):
        return roll(x, -SLOT, 1)

    def corner(a, b):
        x = jnp.where(packed_comp(a.shape) == 3, flow_packed(a), a) * b
        return 0.5 * fold(jnp.sum(x, axis=0, keepdims=True))

    corners = [corner(above, top), -corner(top, above), corner(bottom, below), -corner(below, bottom)]
    border = (iota(1, 1) < SLOT // 2) | (iota(1, 1) >= LANES - SLOT // 2)
    for f in (2, 3):
        for k, at_row in enumerate((ROWS - 1, ROWS, 2 * ROWS - 1, 2 * ROWS)):
            to = pl.ds(f * rows + at_row, 1)
            wide_ref[to, 0:LANES] = wide_ref[to, 0:LANES] + cross_ref[4 * (f - 2) + k : 4 * (f - 2) + k + 1, :]
            side = unpack(corners[k], f)
            wide_ref[to, LANES : 2 * LANES] = wide_ref[to, LANES : 2 * LANES] + jnp.where(border, side, 0.0)

    sum_u, sum_v, adv_u, adv_v, forcing, diagonal = [wide_ref[pl.ds(f * rows, rows), :] for f in range(FLAT)]
    sea = jnp.where(diagonal > 0.0, 1.0, 0.0)
    shape = (rows, 2 * LANES)
    i = iota(0, *shape) - ROWS + at.b * ROWS
    j = iota(1, *shape)
    j = jnp.where(j < LANES + LANES // 2, j, j - 2 * LANES) + at.g * LANES
    total_rows, total_cols = at.nb * ROWS, at.ng * LANES
    edges = (
        jnp.where(i == 0, 1.0, 0.0)
        + jnp.where(i == total_rows - 1, 1.0, 0.0)
        + jnp.where(j == 0, 1.0, 0.0)
        + jnp.where(j == total_cols - 1, 1.0, 0.0)
    )
    coriolis = rotation * (2.0 * (j.astype(F32) + 0.5) / total_cols - 1.0)

    def both(x, n, axis):
        return roll(x, n, axis) + roll(x, -n, axis)

    def transport(x, turn, adv):
        near = both(x, 1, 0)
        linear = (
            (1.0 - hyper_visc * (20.0 - edges)) * x
            + 8.0 * hyper_visc * near
            - hyper_visc * (both(x, 2, 0) + both(x, 2, 1))
            + both(8.0 * hyper_visc * x - 2.0 * hyper_visc * near, 1, 1)
        )
        return sea * (linear + time_step * (turn - adv)) / lay.levels

    east = transport(sum_u, coriolis * sum_v, adv_u)
    north = transport(sum_v, -coriolis * sum_u, adv_v)
    divergence = 0.5 * (roll(east, -1, 0) - roll(east, 1, 0) + roll(north, -1, 1) - roll(north, 1, 1))
    v = [forcing - gravity * sea * divergence]
    own_diagonal = diagonal - SHIFT
    for _ in range(ITERS):
        x = v[-1]
        v.append(own_diagonal * x - sea * (both(x, 1, 0) + both(x, 1, 1)))
    v = [x[ROWS : 2 * ROWS, 0:LANES] for x in v]
    for k in range(ITERS):
        basis_ref[tile(k), :] = v[k]
    line = jnp.zeros((ROWS, LANES), F32)
    for k in range(2 * ITERS):
        part = jnp.sum(v[k // 2] * v[k - k // 2], axis=0, keepdims=True)
        line = jnp.where(row == k, part, line)
    line = jnp.sum(line, axis=1, keepdims=True)
    line = jnp.sum(jnp.where(row == lane, line, 0.0), axis=0, keepdims=True)
    send_ref[...] = jnp.broadcast_to(line, send_ref.shape)


def solve_kernel(
    got_ref, basis_ref, m_ref, one_ref, two_ref, mask_ref, state_in, state_ref, state_hbm, surface_hbm, surface_ref, sems
):
    lay = Layout(state_ref.shape[0] // ROWS)
    at = Place()
    place = pl.ds(lay.delta, lay.pad)
    in_slot = lax.rem(iota(1, lay.pad), SLOT)
    comp = lax.rem(iota(0), COMPS)
    border = (iota(1) < SLOT // 2) | (iota(1) >= LANES - SLOT // 2)
    near = (in_slot == SLOT // 2 - 1) | (in_slot == SLOT // 2)
    sea = mask_ref[...].astype(F32)
    sides = ((at.from_up, 1, 0, 0, 1, 0.5 * time_step), (at.from_down, 0, 1, ROWS - 1, ROWS - 2, -0.5 * time_step))
    for take, first, second, row, inner, slope in sides:
        fix = jnp.where(near, across(-2.0 * hyper_visc * take(one_ref[place, :], two_ref[place, :])), 0.0)
        for s in range(lay.eights):
            x1, x2 = [take(one_ref[w, :], two_ref[w, :]) for w in (tile(n * lay.eights + s) for n in (first, second))]
            flow = m_ref[pl.ds(ROWS * ROWS * s + row, ROWS, stride=ROWS), :]
            u = flow
            for c in (0, 1, 3):
                u = jnp.where(comp == c, roll(flow, c - 2, 0), u)
            p, q = divmod(s * ROWS, PER)
            corner = jnp.broadcast_to(fix[p : p + 1], (ROWS, LANES))
            corner = pltpu.roll(corner, SLOT * q + SLOT // 2, 1, stride=SLOT, stride_axis=0)
            more = (
                hyper_visc * (8.0 * x1 - x2 - 2.0 * (roll(x1, 1, 1) + roll(x1, -1, 1)))
                + slope * u * x1
                + jnp.where(border, corner, 0.0)
            )
            to = pl.ds(ROWS * ROWS * s + row, ROWS, stride=ROWS)
            state_ref[to, :] = state_ref[to, :] + sea[row : row + 1] * more
            to = pl.ds(ROWS * ROWS * s + inner, ROWS, stride=ROWS)
            state_ref[to, :] = state_ref[to, :] - (hyper_visc * sea[inner : inner + 1]) * x1
    write = pltpu.make_async_copy(state_ref, state_hbm, sems.at[0])
    write.start()

    line = jnp.sum(got_ref[...], axis=0, keepdims=True)
    lane = iota(1, 1)
    moment = [jnp.sum(jnp.where(lane == k, line, 0.0), axis=1, keepdims=True) for k in range(2 * ITERS)]

    def dot(a, b):
        total = None
        for k in range(len(a) + len(b) - 1):
            weight = sum(a[n] * b[k - n] for n in range(len(a)) if 0 <= k - n < len(b))
            total = weight * moment[k] if total is None else total + weight * moment[k]
        return total

    def add(a, scale, b):
        out = list(a) + [0.0] * (len(b) - len(a))
        return [x + scale * b[n] if n < len(b) else x for n, x in enumerate(out)]

    def image(a):
        return [SHIFT * (a[n] if n < len(a) else 0.0) + (a[n - 1] if n else 0.0) for n in range(len(a) + 1)]

    one = jnp.ones((1, 1), F32)
    residual, direction, surface = [one], [one], []
    norm = dot(residual, residual)
    for iteration in range(ITERS):
        applied = image(direction)
        alpha = norm / dot(direction, applied)
        surface = add(surface, alpha, direction)
        if iteration + 1 < ITERS:
            residual = add(residual, -alpha, applied)
            following = dot(residual, residual)
            direction = add(residual, following / norm, direction)
            norm = following
    out = surface[0] * basis_ref[tile(0), :]
    for k in range(1, ITERS):
        out = out + surface[k] * basis_ref[tile(k), :]
    surface_ref[...] = out
    write_surface = pltpu.make_async_copy(surface_ref, surface_hbm, sems.at[1])
    write_surface.start()
    write.wait()
    write_surface.wait()


def inner_kernel(m_ref, mask_ref, new_ref, done_ref):
    lay = Layout(m_ref.shape[0] // ROWS)
    at = Place()
    row, lane = iota(0), iota(1)
    sea = mask_ref[...].astype(F32)
    done_ref[...] = sea
    edges = (
        jnp.where((row == 0) & (at.b == 0), 1.0, 0.0)
        + jnp.where((row == ROWS - 1) & (at.b == at.nb - 1), 1.0, 0.0)
        + jnp.where((lane == 0) & (at.g == 0), 1.0, 0.0)
        + jnp.where((lane == LANES - 1) & (at.g == at.ng - 1), 1.0, 0.0)
    )
    centre = 1.0 - 2.0 * mixing - hyper_visc * (20.0 - edges)
    col = (lane + at.g * LANES).astype(F32)
    coriolis = time_step * rotation * (2.0 * (col + 0.5) / (at.ng * LANES) - 1.0)

    def own(level, c):
        return m_ref[tile(COMPS * min(max(level, 0), lay.levels - 1) + c), :]

    for k in range(lay.levels):
        u, v = own(k, 2), own(k, 3)
        half_u, half_v = 0.5 * time_step * u, 0.5 * time_step * v
        for c in range(COMPS):
            t = COMPS * k + c
            x = own(k, c)
            up1, dn1 = jnp.where(row == 0, 0.0, roll(x, 1, 0)), jnp.where(row == ROWS - 1, 0.0, roll(x, -1, 0))
            up2, dn2 = jnp.where(row < 2, 0.0, roll(x, 2, 0)), jnp.where(row >= ROWS - 2, 0.0, roll(x, -2, 0))
            left, right = roll(x, 1, 1), roll(x, -1, 1)
            near1 = up1 + dn1
            q = 8.0 * hyper_visc * x - 2.0 * hyper_visc * near1
            out = (
                centre * x
                + (roll(q, 1, 1) + roll(q, -1, 1))
                + 8.0 * hyper_visc * near1
                - hyper_visc * ((up2 + dn2) + (roll(x, 2, 1) + roll(x, -2, 1)))
                - (half_u * (dn1 - up1) + half_v * (right - left))
                + mixing * (own(k - 1, c) + own(k + 1, c))
            )
            if c == 2:
                out = out + coriolis * v
            if c == 3:
                out = out - coriolis * u
            new_ref[tile(t), :] = sea * out


def border_kernel(pack_ref, delta_ref, mask_ref, state_in, state_ref, done_ref):
    lay = Layout(state_ref.shape[0] // ROWS)
    row, lane = iota(0), iota(1)
    border = (lane < SLOT // 2) | (lane >= LANES - SLOT // 2)
    sea = mask_ref[...].astype(F32)
    sea = jnp.where(border, sea, 0.0)
    done_ref[...] = sea
    in_slot = lax.rem(lane, SLOT)
    half = in_slot < SLOT // 2
    near = (in_slot == 3) | (in_slot == 4)
    far = (in_slot >= 2) & (in_slot <= 5)
    sign = jnp.where(in_slot == 3, -0.5 * time_step, jnp.where(in_slot == 4, 0.5 * time_step, 0.0))
    for p in range(lay.packs):
        d = delta_ref[tile(p), :]
        dv = jnp.where(row == 0, 0.0, roll(d, 1, 0)) + jnp.where(row == ROWS - 1, 0.0, roll(d, -1, 0))
        second = jnp.where(half, roll(d, -2, 1), roll(d, 2, 1))
        fix = (
            jnp.where(far, -hyper_visc * second, 0.0)
            + jnp.where(near, across(hyper_visc * (8.0 * d - 2.0 * dv)), 0.0)
            + sign * spread(pack_ref[tile(p), :], 3) * across(d)
        )
        for t in range(p * PER, (p + 1) * PER):
            state_ref[tile(t), :] = state_ref[tile(t), :] + sea * unpack(fix, t)


def call(kernel, outs, *args, scratch=(), specs=None, out_specs=None, aliases=None, flops=0):
    return pl.pallas_call(
        kernel,
        out_shape=[jax.ShapeDtypeStruct(s, F32) for s in outs],
        in_specs=specs or [VMEM] * len(args),
        out_specs=out_specs or [VMEM] * len(outs),
        scratch_shapes=[pltpu.VMEM(s, F32) if isinstance(s, tuple) else s for s in scratch],
        input_output_aliases=aliases or {},
        compiler_params=pltpu.CompilerParams(vmem_limit_bytes=8 * 1024 * 1024),
        cost_estimate=pl.CostEstimate(flops=flops, bytes_accessed=0, transcendentals=0),
    )(*args)


def on_device(ocean_state, surface_height, surface_damping, land_mask, *, shape):
    nb, ng = shape
    axes = ("blocks", "group")
    state = ocean_state.reshape(-1, LANES)
    lay = Layout(state.shape[0] // ROWS)
    g_one, g_two = swap_pairs(shape, "group")
    b_one, b_two = swap_pairs(shape, "blocks")
    one_tile = (ROWS, LANES)
    packed = (lay.packs * ROWS, LANES)
    flats = (FLAT * ROWS, LANES)

    m, pack, flat = call(
        pack_kernel,
        [state.shape, (packed[0] + ROWS, LANES), flats],
        *[pltpu.with_memory_space_constraint(x, pltpu.HBM) for x in (state, land_mask, surface_height, surface_damping)],
        specs=[HBM] * 4,
        scratch=[
            state.shape,
            pltpu.VMEM(one_tile, land_mask.dtype),
            one_tile,
            one_tile,
            pltpu.SemaphoreType.DMA((3 + lay.packs,)),
        ],
    )
    first = lax.ppermute(pack, axes, g_one)
    second = lax.ppermute(pack, axes, g_two)
    flow_one, flow_two = call(flow_kernel, [(2 * lay.flow, LANES)] * 2, m)
    flow_one = lax.ppermute(flow_one, axes, b_one)
    flow_two = lax.ppermute(flow_two, axes, b_two)
    part, inner_done = call(inner_kernel, [state.shape, one_tile], m, land_mask, flops=LONG)
    message = (lay.message, LANES)
    own, near, delta, one, two = call(
        edge_kernel,
        [(flats[0] + ROWS, LANES), (2 * lay.pad, LANES), packed, message, message],
        m,
        pack,
        flat,
        first,
        second,
        inner_done,
        flops=10 * LONG,
    )
    one = lax.ppermute(one, axes, b_one)
    two = lax.ppermute(two, axes, b_two)
    (cross,) = call(cross_kernel, [one_tile], m, flow_one, flow_two)
    part, done = call(border_kernel, [state.shape, one_tile], pack, delta, land_mask, part, aliases={3: 0}, flops=LONG)
    rest_one, rest_two = call(rest_kernel, [(lay.rest, LANES)] * 2, m, delta, cross)
    rest_one = lax.ppermute(rest_one, axes, b_one)
    rest_two = lax.ppermute(rest_two, axes, b_two)
    basis, sent = call(
        functools.partial(moment_kernel, levels=lay.levels),
        [(ITERS * ROWS, LANES), (nb * ng, LANES)],
        own,
        near,
        cross,
        one,
        two,
        done,
        scratch=[(FLAT * 3 * ROWS, 2 * LANES)],
        flops=LONG,
    )
    got = lax.all_to_all(sent, axes, 0, 0, tiled=True)
    _, new_state, surface = call(
        solve_kernel,
        [state.shape, state.shape, one_tile],
        got,
        basis,
        m,
        rest_one,
        rest_two,
        land_mask,
        part,
        scratch=[one_tile, pltpu.SemaphoreType.DMA((2,))],
        out_specs=[VMEM, HBM, HBM],
        aliases={6: 0},
    )
    return new_state.reshape(ocean_state.shape), surface


def solution(mesh):
    placed = (
        P(None, None, "blocks", "group"),
        P("blocks", "group"),
        P("blocks", "group"),
        P("blocks", "group"),
    )
    shape = (mesh.shape["blocks"], mesh.shape["group"])

    def body(*args):
        return on_device(*args, shape=shape)

    return jax.shard_map(
        body,
        mesh=mesh,
        in_specs=placed,
        out_specs=(P(None, None, "blocks", "group"), P("blocks", "group")),
        check_vma=False,
    )
```

```python
import functools

import jax
import jax.numpy as jnp
from jax import lax
from jax.experimental import pallas as pl
from jax.experimental.pallas import tpu as pltpu
from jax.sharding import PartitionSpec as P

ITERS = 3

time_step = 0.25
hyper_visc = 0.025
mixing = 0.2
gravity = 4.0
rotation = 0.2

COMPS = 4
ROWS = 8
LANES = 128
SLOT = 8
PER = LANES // SLOT
FLAT = 6
STRIP = 16
LONG = 10**9
SHIFT = 4.5
F32 = jnp.float32
VMEM = pl.BlockSpec(memory_space=pltpu.VMEM)
HBM = pl.BlockSpec(memory_space=pltpu.HBM)


def iota(axis, rows=ROWS, lanes=LANES):
    return lax.broadcasted_iota(jnp.int32, (rows, lanes), axis)


def roll(x, shift, axis):
    return pltpu.roll(x, shift % x.shape[axis], axis)


def tile(k):
    return pl.ds(k * ROWS, ROWS)


def swap_pairs(mesh_shape, along):
    nb, ng = mesh_shape
    first, second = [], []
    for b in range(nb):
        for g in range(ng):
            me = b * ng + g
            if along == "blocks":
                one = (b ^ 1, g)
                two = ((b - 1) ^ 1) + 1
                two = (two, g) if 0 <= two < nb else (b, g ^ 1)
            else:
                one = (b, g ^ 1)
                two = ((g - 1) ^ 1) + 1
                two = (b, two) if 0 <= two < ng else (b ^ 1, g)
            first.append((me, one[0] * ng + one[1]))
            second.append((me, two[0] * ng + two[1]))
    return first, second


class Layout:
    def __init__(self, tiles):
        self.tiles = tiles
        self.levels = tiles // COMPS
        self.packs = tiles // PER
        self.eights = tiles // ROWS
        self.pad = -(-self.packs // ROWS) * ROWS
        self.flow = -(-self.levels // ROWS) * ROWS
        self.flat = 2 * self.flow
        self.early = self.flat + FLAT * ROWS
        self.edge = 0
        self.strip = self.pad
        self.inner = self.strip + ROWS
        self.message = self.inner + ROWS
        self.delta = 2 * tiles
        self.rest = self.delta + self.pad


class Place:
    def __init__(self):
        self.b, self.nb = lax.axis_index("blocks"), lax.axis_size("blocks")
        self.g, self.ng = lax.axis_index("group"), lax.axis_size("group")
        self.b_even = lax.rem(self.b, 2) == 0
        self.g_even = lax.rem(self.g, 2) == 0
        self.up = (self.b > 0).astype(F32)
        self.down = (self.b < self.nb - 1).astype(F32)
        self.left = (self.g > 0).astype(F32)
        self.right = (self.g < self.ng - 1).astype(F32)

    def from_up(self, one, two):
        return jnp.where(self.b_even, two, one) * self.up

    def from_down(self, one, two):
        return jnp.where(self.b_even, one, two) * self.down


def pack_kernel(
    state_hbm, mask_hbm, height_hbm, damp_hbm, m_ref, pack_ref, flat_ref, state_ref, mask_ref, height_ref, damp_ref, sems
):
    lay = Layout(m_ref.shape[0] // ROWS)
    chunk = PER * ROWS
    small = [(mask_hbm, mask_ref), (height_hbm, height_ref), (damp_hbm, damp_ref)]
    copies = [pltpu.make_async_copy(a, b, sems.at[k]) for k, (a, b) in enumerate(small)]
    for p in range(lay.packs):
        at = pl.ds(p * chunk, chunk)
        copies.append(pltpu.make_async_copy(state_hbm.at[at], state_ref.at[at], sems.at[3 + p]))
    for copy in copies:
        copy.start()
    for copy in copies[: 3 + lay.packs // 2]:
        copy.wait()
    sea = mask_ref[...].astype(F32)
    row, lane = iota(0), iota(1)
    slot = lane // SLOT
    sum_u = sum_v = uu = uv = vu = zero = jnp.zeros((ROWS, LANES), F32)
    across_u = across_v = across_vu = zero
    for p in range(lay.packs):
        if p == lay.packs // 2:
            for copy in copies[3 + p :]:
                copy.wait()
        acc = zero
        for k in range(PER // COMPS):
            x = []
            for c in range(COMPS):
                q = COMPS * k + c
                x.append(state_ref[tile(p * PER + q), :] * sea)
                m_ref[tile(p * PER + q), :] = x[c]
                at = PER - 1 - q
                acc = jnp.where(slot == at, roll(x[c], SLOT * at + SLOT // 2, 1), acc)
            u, v = x[2:]
            below_u, below_v = roll(u, -1, 0), roll(v, -1, 0)
            right_u, right_v = roll(u, -1, 1), roll(v, -1, 1)
            sum_u, sum_v = sum_u + u, sum_v + v
            uu, uv, vu = uu + u * below_u, uv + u * below_v, vu + v * below_u
            across_u, across_v, across_vu = across_u + v * right_u, across_v + v * right_v, across_vu + u * right_v
        pack_ref[tile(p), :] = acc

    def step_down(ahead, back):
        inner = row < ROWS - 1
        return jnp.where(inner, ahead, 0.0) - roll(jnp.where(inner, back, 0.0), 1, 0)

    def step_right(ahead, back):
        inner = lane < LANES - 1
        return jnp.where(inner, ahead, 0.0) - roll(jnp.where(inner, back, 0.0), 1, 1)

    advect_u = 0.5 * (step_down(uu, uu) + step_right(across_u, across_vu))
    advect_v = 0.5 * (step_down(uv, vu) + step_right(across_v, across_v))
    damp = damp_ref[...]
    flat = [sum_u, sum_v, advect_u, advect_v, sea * damp * height_ref[...], sea * (4.0 + damp)]
    acc = jnp.zeros((ROWS, LANES), F32)
    for f in range(FLAT):
        flat_ref[tile(f), :] = flat[f]
        acc = jnp.where(lane // STRIP == f, roll(flat[f], STRIP * f + STRIP // 2, 1), acc)
    pack_ref[tile(lay.packs), :] = acc


def packed_comp(shape):
    return COMPS - 1 - lax.rem(lax.broadcasted_iota(jnp.int32, shape, 1) // SLOT, COMPS)


def unpack(x, t):
    return roll(x, -(SLOT * (PER - 1 - t % PER) + SLOT // 2), 1)


def spread(x, of):
    comp = packed_comp(x.shape)
    out = x
    for c in range(COMPS):
        if c != of:
            out = jnp.where(comp == c, roll(x, SLOT * (of - c), 1), out)
    return out


def across(x):
    half = lax.rem(lax.broadcasted_iota(jnp.int32, x.shape, 1), SLOT) < SLOT // 2
    return jnp.where(half, roll(x, -1, 1), roll(x, 1, 1))


def fold(x):
    step = SLOT * COMPS
    while step < LANES:
        x = x + roll(x, step, 1)
        step *= 2
    return x


def edge_kernel(pack_ref, first_ref, second_ref, done_ref, own_ref, near_ref, delta_ref, one_ref, two_ref):
    lay = Layout((pack_ref.shape[0] // ROWS - 1) * PER)
    at = Place()
    lane = iota(1)
    comp = packed_comp((ROWS, LANES))
    in_slot = lax.rem(lane, SLOT)
    half = in_slot < SLOT // 2
    sign = jnp.where(in_slot == SLOT // 2 - 1, 0.5, jnp.where(in_slot == SLOT // 2, -0.5, 0.0))

    def beyond(p, low):
        first, second = first_ref[tile(p), :], second_ref[tile(p), :]
        from_left = jnp.where(at.g_even, second, first) * at.left
        from_right = jnp.where(at.g_even, first, second) * at.right
        return jnp.where(low, from_left, from_right)

    def flow(x):
        return jnp.where(comp == 2, roll(x, SLOT, 1), x)

    near_ref[...] = jnp.zeros(near_ref.shape, F32)
    inner = jnp.zeros((ROWS, LANES), F32)
    outer = jnp.zeros((ROWS, LANES), F32)
    for p in range(lay.packs):
        own, far = pack_ref[tile(p), :], beyond(p, half)
        delta_ref[tile(p), :] = far - own
        near_ref[p : p + 1, :] = far[0:1]
        near_ref[lay.pad + p : lay.pad + p + 1, :] = far[ROWS - 1 : ROWS]
        inner = inner + flow(own) * across(far)
        outer = outer + flow(far) * across(own)
    inner, outer = fold(sign * inner), fold(sign * outer)
    strip = beyond(lay.packs, lax.rem(lane, STRIP) < STRIP // 2)
    for f in (2, 3):
        mid = STRIP * f + STRIP // 2
        border = (lane == mid - 1) | (lane == mid)
        strip = strip + jnp.where(border, roll(unpack(outer, f), mid, 1), 0.0)
    own_ref[0:ROWS, :] = strip
    own_ref[ROWS : 2 * ROWS, :] = inner

    def fill(low_ref, high_ref):
        for ref, rows in ((low_ref, slice(0, lay.pad)), (high_ref, slice(lay.pad, 2 * lay.pad))):
            ref[pl.ds(lay.edge, lay.pad), :] = near_ref[rows, :]
            ref[pl.ds(lay.strip, ROWS), :] = strip
            ref[pl.ds(lay.inner, ROWS), :] = inner

    pl.when(at.b_even)(lambda: fill(two_ref, one_ref))
    pl.when(jnp.logical_not(at.b_even))(lambda: fill(one_ref, two_ref))


def level_rows(m_ref, comp, row):
    lay = Layout(m_ref.shape[0] // ROWS)
    step = COMPS * ROWS
    parts = []
    for start in range(0, lay.levels, ROWS):
        count = min(ROWS, lay.levels - start)
        x = m_ref[pl.ds(start * step + comp * ROWS + row, count, stride=step), :]
        if count < ROWS:
            x = jnp.concatenate([x, jnp.zeros((ROWS - count, LANES), F32)], axis=0)
        parts.append(x)
    return parts


def flow_kernel(m_ref, flat_ref, one_ref, two_ref):
    lay = Layout(m_ref.shape[0] // ROWS)

    def fill(low_ref, high_ref):
        for ref, row in ((low_ref, 0), (high_ref, ROWS - 1)):
            for c in range(2):
                for n, x in enumerate(level_rows(m_ref, 2 + c, row)):
                    ref[pl.ds(c * lay.flow + n * ROWS, ROWS), :] = x
            ref[pl.ds(lay.flat, FLAT * ROWS), :] = flat_ref[...]

    even = Place().b_even
    pl.when(even)(lambda: fill(two_ref, one_ref))
    pl.when(jnp.logical_not(even))(lambda: fill(one_ref, two_ref))


def rest_kernel(m_ref, delta_ref, after_ref, one_ref, two_ref):
    lay = Layout(m_ref.shape[0] // ROWS)

    def fill(low_ref, high_ref):
        for ref, row, near in ((low_ref, 0, 0), (high_ref, ROWS - 2, ROWS - 1)):
            for r in range(2):
                for s in range(lay.eights):
                    at = pl.ds(ROWS * ROWS * s + row + r, ROWS, stride=ROWS)
                    ref[tile(r * lay.eights + s), :] = m_ref[at, :]
            ref[pl.ds(lay.delta, lay.pad), :] = jnp.zeros((lay.pad, LANES), F32)
            for p in range(lay.packs):
                ref[pl.ds(lay.delta + p, 1), :] = delta_ref[pl.ds(ROWS * p + near, 1), :]

    even = Place().b_even
    pl.when(even)(lambda: fill(two_ref, one_ref))
    pl.when(jnp.logical_not(even))(lambda: fill(one_ref, two_ref))


def cross_kernel(m_ref, one_ref, two_ref, cross_ref):
    lay = Layout(m_ref.shape[0] // ROWS)
    at = Place()
    row = iota(0)
    count = lay.flow // ROWS

    def beyond(take, c):
        where = [pl.ds(c * lay.flow + n * ROWS, ROWS) for n in range(count)]
        return [take(one_ref[w, :], two_ref[w, :]) for w in where]

    above, below = [[beyond(take, c) for c in range(2)] for take in (at.from_up, at.from_down)]
    top, bottom = [[level_rows(m_ref, c, r) for c in (2, 3)] for r in (0, ROWS - 1)]

    def total(flow, carried):
        return 0.5 * jnp.sum(sum(x * y for x, y in zip(flow, carried)), axis=0, keepdims=True)

    out = jnp.zeros((ROWS, LANES), F32)
    for f in range(2):
        sums = (total(above[0], top[f]), -total(top[0], above[f]), total(bottom[0], below[f]), -total(below[0], bottom[f]))
        for k in range(4):
            out = jnp.where(row == 4 * f + k, sums[k], out)
    cross_ref[...] = out


def moment_kernel(
    flat_ref, own_ref, near_ref, cross_ref, flow_one_ref, flow_two_ref, one_ref, two_ref, done_ref, basis_ref, send_ref, wide_ref, *, levels
):
    lay = Layout(levels * COMPS)
    at = Place()
    row, lane = iota(0), iota(1)
    outside = (lane < STRIP // 2) | (lane >= LANES - STRIP // 2)
    rows = 3 * ROWS

    def neighbours(where, first_ref=one_ref, second_ref=two_ref):
        first, second = first_ref[where, :], second_ref[where, :]
        return at.from_up(first, second), at.from_down(first, second)

    def around(where, own, *refs):
        up, down = neighbours(where, *refs)
        return up, own, down

    strips = around(pl.ds(lay.strip, ROWS), own_ref[0:ROWS, :])
    inners = around(pl.ds(lay.inner, ROWS), own_ref[ROWS : 2 * ROWS, :])
    border = (lane == 0) | (lane == LANES - 1)
    for f in range(FLAT):
        fields = around(pl.ds(lay.flat + f * ROWS, ROWS), flat_ref[tile(f), :], flow_one_ref, flow_two_ref)
        for k in range(3):
            to = pl.ds(f * rows + k * ROWS, ROWS)
            value = fields[k]
            if 2 <= f <= 3:
                value = value + jnp.where(border, unpack(inners[k], f), 0.0)
            wide_ref[to, 0:LANES] = value
            side = roll(strips[k], -(STRIP * f + STRIP // 2), 1)
            wide_ref[to, LANES : 2 * LANES] = jnp.where(outside, side, 0.0)

    above, below = neighbours(pl.ds(lay.edge, lay.pad))
    top, bottom = near_ref[0 : lay.pad, :], near_ref[lay.pad :, :]

    def flow_packed(x):
        return roll(x, -SLOT, 1)

    def corner(a, b):
        x = jnp.where(packed_comp(a.shape) == 3, flow_packed(a), a) * b
        return 0.5 * fold(jnp.sum(x, axis=0, keepdims=True))

    corners = [corner(above, top), -corner(top, above), corner(bottom, below), -corner(below, bottom)]
    border = (iota(1, 1) < SLOT // 2) | (iota(1, 1) >= LANES - SLOT // 2)
    for f in (2, 3):
        for k, at_row in enumerate((ROWS - 1, ROWS, 2 * ROWS - 1, 2 * ROWS)):
            to = pl.ds(f * rows + at_row, 1)
            wide_ref[to, 0:LANES] = wide_ref[to, 0:LANES] + cross_ref[4 * (f - 2) + k : 4 * (f - 2) + k + 1, :]
            side = unpack(corners[k], f)
            wide_ref[to, LANES : 2 * LANES] = wide_ref[to, LANES : 2 * LANES] + jnp.where(border, side, 0.0)

    sum_u, sum_v, adv_u, adv_v, forcing, diagonal = [wide_ref[pl.ds(f * rows, rows), :] for f in range(FLAT)]
    sea = jnp.where(diagonal > 0.0, 1.0, 0.0)
    shape = (rows, 2 * LANES)
    i = iota(0, *shape) - ROWS + at.b * ROWS
    j = iota(1, *shape)
    j = jnp.where(j < LANES + LANES // 2, j, j - 2 * LANES) + at.g * LANES
    total_rows, total_cols = at.nb * ROWS, at.ng * LANES
    edges = (
        jnp.where(i == 0, 1.0, 0.0)
        + jnp.where(i == total_rows - 1, 1.0, 0.0)
        + jnp.where(j == 0, 1.0, 0.0)
        + jnp.where(j == total_cols - 1, 1.0, 0.0)
    )
    coriolis = rotation * (2.0 * (j.astype(F32) + 0.5) / total_cols - 1.0)

    def both(x, n, axis):
        return roll(x, n, axis) + roll(x, -n, axis)

    def transport(x, turn, adv):
        near = both(x, 1, 0)
        linear = (
            (1.0 - hyper_visc * (20.0 - edges)) * x
            + 8.0 * hyper_visc * near
            - hyper_visc * (both(x, 2, 0) + both(x, 2, 1))
            + both(8.0 * hyper_visc * x - 2.0 * hyper_visc * near, 1, 1)
        )
        return sea * (linear + time_step * (turn - adv)) / lay.levels

    east = transport(sum_u, coriolis * sum_v, adv_u)
    north = transport(sum_v, -coriolis * sum_u, adv_v)
    divergence = 0.5 * (roll(east, -1, 0) - roll(east, 1, 0) + roll(north, -1, 1) - roll(north, 1, 1))
    v = [forcing - gravity * sea * divergence]
    own_diagonal = diagonal - SHIFT
    for _ in range(ITERS):
        x = v[-1]
        v.append(own_diagonal * x - sea * (both(x, 1, 0) + both(x, 1, 1)))
    v = [x[ROWS : 2 * ROWS, 0:LANES] for x in v]
    for k in range(ITERS):
        basis_ref[tile(k), :] = v[k]
    line = jnp.zeros((ROWS, LANES), F32)
    for k in range(2 * ITERS):
        part = jnp.sum(v[k // 2] * v[k - k // 2], axis=0, keepdims=True)
        line = jnp.where(row == k, part, line)
    line = jnp.sum(line, axis=1, keepdims=True)
    line = jnp.sum(jnp.where(row == lane, line, 0.0), axis=0, keepdims=True)
    send_ref[...] = jnp.broadcast_to(line, send_ref.shape)


def solve_kernel(
    got_ref, basis_ref, m_ref, one_ref, two_ref, mask_ref, state_in, state_ref, state_hbm, surface_hbm, surface_ref, sems
):
    lay = Layout(state_ref.shape[0] // ROWS)
    at = Place()
    place = pl.ds(lay.delta, lay.pad)
    in_slot = lax.rem(iota(1, lay.pad), SLOT)
    comp = lax.rem(iota(0), COMPS)
    border = (iota(1) < SLOT // 2) | (iota(1) >= LANES - SLOT // 2)
    near = (in_slot == SLOT // 2 - 1) | (in_slot == SLOT // 2)
    sea = mask_ref[...].astype(F32)
    sides = ((at.from_up, 1, 0, 0, 1, 0.5 * time_step), (at.from_down, 0, 1, ROWS - 1, ROWS - 2, -0.5 * time_step))
    fixes = [across(-2.0 * hyper_visc * side[0](one_ref[place, :], two_ref[place, :])) for side in sides]
    fixes = [jnp.where(near, x, 0.0) for x in fixes]
    writes = []
    for s in range(lay.eights):
        for (take, first, second, row, inner, slope), fix in zip(sides, fixes):
            x1, x2 = [take(one_ref[w, :], two_ref[w, :]) for w in (tile(n * lay.eights + s) for n in (first, second))]
            flow = m_ref[pl.ds(ROWS * ROWS * s + row, ROWS, stride=ROWS), :]
            u = flow
            for c in (0, 1, 3):
                u = jnp.where(comp == c, roll(flow, c - 2, 0), u)
            p, q = divmod(s * ROWS, PER)
            corner = jnp.broadcast_to(fix[p : p + 1], (ROWS, LANES))
            corner = pltpu.roll(corner, SLOT * q + SLOT // 2, 1, stride=SLOT, stride_axis=0)
            more = (
                hyper_visc * (8.0 * x1 - x2 - 2.0 * (roll(x1, 1, 1) + roll(x1, -1, 1)))
                + slope * u * x1
                + jnp.where(border, corner, 0.0)
            )
            to = pl.ds(ROWS * ROWS * s + row, ROWS, stride=ROWS)
            state_ref[to, :] = state_ref[to, :] + sea[row : row + 1] * more
            to = pl.ds(ROWS * ROWS * s + inner, ROWS, stride=ROWS)
            state_ref[to, :] = state_ref[to, :] - (hyper_visc * sea[inner : inner + 1]) * x1
        if s + 1 in (lay.eights // 2, lay.eights):
            start = len(writes) * (lay.eights // 2) * ROWS * ROWS
            part = pl.ds(start, (s + 1) * ROWS * ROWS - start)
            writes.append(pltpu.make_async_copy(state_ref.at[part], state_hbm.at[part], sems.at[len(writes)]))
            writes[-1].start()

    line = jnp.sum(got_ref[...], axis=0, keepdims=True)
    lane = iota(1, 1)
    moment = [jnp.sum(jnp.where(lane == k, line, 0.0), axis=1, keepdims=True) for k in range(2 * ITERS)]

    def dot(a, b):
        total = None
        for k in range(len(a) + len(b) - 1):
            weight = sum(a[n] * b[k - n] for n in range(len(a)) if 0 <= k - n < len(b))
            total = weight * moment[k] if total is None else total + weight * moment[k]
        return total

    def add(a, scale, b):
        out = list(a) + [0.0] * (len(b) - len(a))
        return [x + scale * b[n] if n < len(b) else x for n, x in enumerate(out)]

    def image(a):
        return [SHIFT * (a[n] if n < len(a) else 0.0) + (a[n - 1] if n else 0.0) for n in range(len(a) + 1)]

    one = jnp.ones((1, 1), F32)
    residual, direction, surface = [one], [one], []
    norm = dot(residual, residual)
    for iteration in range(ITERS):
        applied = image(direction)
        alpha = norm / dot(direction, applied)
        surface = add(surface, alpha, direction)
        if iteration + 1 < ITERS:
            residual = add(residual, -alpha, applied)
            following = dot(residual, residual)
            direction = add(residual, following / norm, direction)
            norm = following
    out = surface[0] * basis_ref[tile(0), :]
    for k in range(1, ITERS):
        out = out + surface[k] * basis_ref[tile(k), :]
    surface_ref[...] = out
    writes.append(pltpu.make_async_copy(surface_ref, surface_hbm, sems.at[len(writes)]))
    writes[-1].start()
    for write in writes:
        write.wait()


def inner_kernel(m_ref, mask_ref, new_ref, done_ref):
    lay = Layout(m_ref.shape[0] // ROWS)
    at = Place()
    row, lane = iota(0), iota(1)
    sea = mask_ref[...].astype(F32)
    done_ref[...] = sea
    edges = (
        jnp.where((row == 0) & (at.b == 0), 1.0, 0.0)
        + jnp.where((row == ROWS - 1) & (at.b == at.nb - 1), 1.0, 0.0)
        + jnp.where((lane == 0) & (at.g == 0), 1.0, 0.0)
        + jnp.where((lane == LANES - 1) & (at.g == at.ng - 1), 1.0, 0.0)
    )
    centre = 1.0 - 2.0 * mixing - hyper_visc * (20.0 - edges)
    col = (lane + at.g * LANES).astype(F32)
    coriolis = time_step * rotation * (2.0 * (col + 0.5) / (at.ng * LANES) - 1.0)

    def own(level, c):
        return m_ref[tile(COMPS * min(max(level, 0), lay.levels - 1) + c), :]

    for k in range(lay.levels):
        u, v = own(k, 2), own(k, 3)
        half_u, half_v = 0.5 * time_step * u, 0.5 * time_step * v
        for c in range(COMPS):
            t = COMPS * k + c
            x = own(k, c)
            up1, dn1 = jnp.where(row == 0, 0.0, roll(x, 1, 0)), jnp.where(row == ROWS - 1, 0.0, roll(x, -1, 0))
            up2, dn2 = jnp.where(row < 2, 0.0, roll(x, 2, 0)), jnp.where(row >= ROWS - 2, 0.0, roll(x, -2, 0))
            left, right = roll(x, 1, 1), roll(x, -1, 1)
            near1 = up1 + dn1
            q = 8.0 * hyper_visc * x - 2.0 * hyper_visc * near1
            out = (
                centre * x
                + (roll(q, 1, 1) + roll(q, -1, 1))
                + 8.0 * hyper_visc * near1
                - hyper_visc * ((up2 + dn2) + (roll(x, 2, 1) + roll(x, -2, 1)))
                - (half_u * (dn1 - up1) + half_v * (right - left))
                + mixing * (own(k - 1, c) + own(k + 1, c))
            )
            if c == 2:
                out = out + coriolis * v
            if c == 3:
                out = out - coriolis * u
            new_ref[tile(t), :] = sea * out


def border_kernel(pack_ref, delta_ref, mask_ref, state_in, state_ref, done_ref):
    lay = Layout(state_ref.shape[0] // ROWS)
    lane = iota(1)
    border = (lane < SLOT // 2) | (lane >= LANES - SLOT // 2)
    sea = mask_ref[...].astype(F32)
    sea = jnp.where(border, sea, 0.0)
    done_ref[...] = sea
    d = delta_ref[...]
    row, in_slot = lax.rem(iota(0, d.shape[0]), ROWS), lax.rem(iota(1, d.shape[0]), SLOT)
    mid = SLOT // 2
    near = (in_slot == mid - 1) | (in_slot == mid)
    far = (in_slot >= mid - 2) & (in_slot <= mid + 1)
    sign = jnp.where(in_slot == mid - 1, -0.5 * time_step, jnp.where(in_slot == mid, 0.5 * time_step, 0.0))
    dv = jnp.where(row == 0, 0.0, roll(d, 1, 0)) + jnp.where(row == ROWS - 1, 0.0, roll(d, -1, 0))
    second = jnp.where(in_slot < mid, roll(d, -2, 1), roll(d, 2, 1))
    fix = (
        jnp.where(far, -hyper_visc * second, 0.0)
        + jnp.where(near, across(hyper_visc * (8.0 * d - 2.0 * dv)), 0.0)
        + sign * spread(pack_ref[0 : d.shape[0], :], 3) * across(d)
    )
    for t in range(lay.tiles):
        p = t // PER
        state_ref[tile(t), :] = state_ref[tile(t), :] + sea * unpack(fix[p * ROWS : (p + 1) * ROWS], t)


def call(kernel, outs, *args, scratch=(), specs=None, out_specs=None, aliases=None, flops=0):
    return pl.pallas_call(
        kernel,
        out_shape=[jax.ShapeDtypeStruct(s, F32) for s in outs],
        in_specs=specs or [VMEM] * len(args),
        out_specs=out_specs or [VMEM] * len(outs),
        scratch_shapes=[pltpu.VMEM(s, F32) if isinstance(s, tuple) else s for s in scratch],
        input_output_aliases=aliases or {},
        compiler_params=pltpu.CompilerParams(vmem_limit_bytes=8 * 1024 * 1024),
        cost_estimate=pl.CostEstimate(flops=flops, bytes_accessed=0, transcendentals=0),
    )(*args)


def on_device(ocean_state, surface_height, surface_damping, land_mask, *, shape):
    nb, ng = shape
    axes = ("blocks", "group")
    state = ocean_state.reshape(-1, LANES)
    lay = Layout(state.shape[0] // ROWS)
    g_one, g_two = swap_pairs(shape, "group")
    b_one, b_two = swap_pairs(shape, "blocks")
    one_tile = (ROWS, LANES)
    packed = (lay.packs * ROWS, LANES)
    flats = (FLAT * ROWS, LANES)

    m, pack, flat = call(
        pack_kernel,
        [state.shape, (packed[0] + ROWS, LANES), flats],
        *[pltpu.with_memory_space_constraint(x, pltpu.HBM) for x in (state, land_mask, surface_height, surface_damping)],
        specs=[HBM] * 4,
        scratch=[
            state.shape,
            pltpu.VMEM(one_tile, land_mask.dtype),
            one_tile,
            one_tile,
            pltpu.SemaphoreType.DMA((3 + lay.packs,)),
        ],
    )
    first = lax.ppermute(pack, axes, g_one)
    second = lax.ppermute(pack, axes, g_two)
    flow_one, flow_two = call(flow_kernel, [(lay.early, LANES)] * 2, m, flat)
    flow_one = lax.ppermute(flow_one, axes, b_one)
    flow_two = lax.ppermute(flow_two, axes, b_two)
    part, inner_done = call(inner_kernel, [state.shape, one_tile], m, land_mask, flops=LONG)
    message = (lay.message, LANES)
    own, near, delta, one, two = call(
        edge_kernel,
        [(2 * ROWS, LANES), (2 * lay.pad, LANES), packed, message, message],
        pack,
        first,
        second,
        inner_done,
        flops=10 * LONG,
    )
    one = lax.ppermute(one, axes, b_one)
    two = lax.ppermute(two, axes, b_two)
    (cross,) = call(cross_kernel, [one_tile], m, flow_one, flow_two)
    part, done = call(border_kernel, [state.shape, one_tile], pack, delta, land_mask, part, aliases={3: 0}, flops=LONG)
    rest_one, rest_two = call(rest_kernel, [(lay.rest, LANES)] * 2, m, delta, cross)
    rest_one = lax.ppermute(rest_one, axes, b_one)
    rest_two = lax.ppermute(rest_two, axes, b_two)
    basis, sent = call(
        functools.partial(moment_kernel, levels=lay.levels),
        [(ITERS * ROWS, LANES), (nb * ng, LANES)],
        flat,
        own,
        near,
        cross,
        flow_one,
        flow_two,
        one,
        two,
        done,
        scratch=[(FLAT * 3 * ROWS, 2 * LANES)],
        flops=LONG,
    )
    got = lax.all_to_all(sent, axes, 0, 0, tiled=True)
    _, new_state, surface = call(
        solve_kernel,
        [state.shape, state.shape, one_tile],
        got,
        basis,
        m,
        rest_one,
        rest_two,
        land_mask,
        part,
        scratch=[one_tile, pltpu.SemaphoreType.DMA((3,))],
        out_specs=[VMEM, HBM, HBM],
        aliases={6: 0},
    )
    return new_state.reshape(ocean_state.shape), surface


def solution(mesh):
    placed = (
        P(None, None, "blocks", "group"),
        P("blocks", "group"),
        P("blocks", "group"),
        P("blocks", "group"),
    )
    shape = (mesh.shape["blocks"], mesh.shape["group"])

    def body(*args):
        return on_device(*args, shape=shape)

    return jax.shard_map(
        body,
        mesh=mesh,
        in_specs=placed,
        out_specs=(P(None, None, "blocks", "group"), P("blocks", "group")),
        check_vma=False,
    )
```

```python
import functools

import jax
import jax.numpy as jnp
from jax import lax
from jax.experimental import pallas as pl
from jax.experimental.pallas import tpu as pltpu
from jax.sharding import PartitionSpec as P

ITERS = 3

time_step = 0.25
hyper_visc = 0.025
mixing = 0.2
gravity = 4.0
rotation = 0.2

COMPS = 4
ROWS = 8
LANES = 128
SLOT = 8
PER = LANES // SLOT
FLAT = 6
STRIP = 16
LONG = 10**9
SHIFT = 4.5
PAIRS = [(i, j) for i in range(ITERS) for j in range(i, ITERS + 1)]
F32 = jnp.float32
VMEM = pl.BlockSpec(memory_space=pltpu.VMEM)
HBM = pl.BlockSpec(memory_space=pltpu.HBM)


def iota(axis, rows=ROWS, lanes=LANES):
    return lax.broadcasted_iota(jnp.int32, (rows, lanes), axis)


def roll(x, shift, axis):
    return pltpu.roll(x, shift % x.shape[axis], axis)


def tile(k):
    return pl.ds(k * ROWS, ROWS)


def swap_pairs(mesh_shape, along):
    nb, ng = mesh_shape
    first, second = [], []
    for b in range(nb):
        for g in range(ng):
            me = b * ng + g
            if along == "blocks":
                one = (b ^ 1, g)
                two = ((b - 1) ^ 1) + 1
                two = (two, g) if 0 <= two < nb else (b, g ^ 1)
            else:
                one = (b, g ^ 1)
                two = ((g - 1) ^ 1) + 1
                two = (b, two) if 0 <= two < ng else (b ^ 1, g)
            first.append((me, one[0] * ng + one[1]))
            second.append((me, two[0] * ng + two[1]))
    return first, second


class Layout:
    def __init__(self, tiles):
        self.tiles = tiles
        self.levels = tiles // COMPS
        self.packs = tiles // PER
        self.eights = tiles // ROWS
        self.pad = -(-self.packs // ROWS) * ROWS
        self.flow = -(-self.levels // ROWS) * ROWS
        self.flat = 2 * self.flow
        self.early = self.flat + FLAT * ROWS
        self.edge = 0
        self.strip = self.pad
        self.inner = self.strip + ROWS
        self.message = self.inner + ROWS
        self.delta = 2 * tiles
        self.rest = self.delta + self.pad


class Place:
    def __init__(self):
        self.b, self.nb = lax.axis_index("blocks"), lax.axis_size("blocks")
        self.g, self.ng = lax.axis_index("group"), lax.axis_size("group")
        self.b_even = lax.rem(self.b, 2) == 0
        self.g_even = lax.rem(self.g, 2) == 0
        self.up = (self.b > 0).astype(F32)
        self.down = (self.b < self.nb - 1).astype(F32)
        self.left = (self.g > 0).astype(F32)
        self.right = (self.g < self.ng - 1).astype(F32)

    def from_up(self, one, two):
        return jnp.where(self.b_even, two, one) * self.up

    def from_down(self, one, two):
        return jnp.where(self.b_even, one, two) * self.down


def pack_kernel(
    state_hbm, mask_hbm, height_hbm, damp_hbm, m_ref, pack_ref, flat_ref, state_ref, mask_ref, height_ref, damp_ref, sems
):
    lay = Layout(m_ref.shape[0] // ROWS)
    chunk = PER * ROWS
    small = [(mask_hbm, mask_ref), (height_hbm, height_ref), (damp_hbm, damp_ref)]
    copies = [pltpu.make_async_copy(a, b, sems.at[k]) for k, (a, b) in enumerate(small)]
    for p in range(lay.packs):
        at = pl.ds(p * chunk, chunk)
        copies.append(pltpu.make_async_copy(state_hbm.at[at], state_ref.at[at], sems.at[3 + p]))
    for copy in copies:
        copy.start()
    for copy in copies[: 3 + lay.packs // 2]:
        copy.wait()
    sea = mask_ref[...].astype(F32)
    row, lane = iota(0), iota(1)
    slot = lane // SLOT
    sum_u = sum_v = uu = uv = vu = zero = jnp.zeros((ROWS, LANES), F32)
    across_u = across_v = across_vu = zero
    for p in range(lay.packs):
        if p == lay.packs // 2:
            for copy in copies[3 + p :]:
                copy.wait()
        acc = zero
        for k in range(PER // COMPS):
            x = []
            for c in range(COMPS):
                q = COMPS * k + c
                x.append(state_ref[tile(p * PER + q), :] * sea)
                m_ref[tile(p * PER + q), :] = x[c]
                at = PER - 1 - q
                acc = jnp.where(slot == at, roll(x[c], SLOT * at + SLOT // 2, 1), acc)
            u, v = x[2:]
            below_u, below_v = roll(u, -1, 0), roll(v, -1, 0)
            right_u, right_v = roll(u, -1, 1), roll(v, -1, 1)
            sum_u, sum_v = sum_u + u, sum_v + v
            uu, uv, vu = uu + u * below_u, uv + u * below_v, vu + v * below_u
            across_u, across_v, across_vu = across_u + v * right_u, across_v + v * right_v, across_vu + u * right_v
        pack_ref[tile(p), :] = acc

    def step_down(ahead, back):
        inner = row < ROWS - 1
        return jnp.where(inner, ahead, 0.0) - roll(jnp.where(inner, back, 0.0), 1, 0)

    def step_right(ahead, back):
        inner = lane < LANES - 1
        return jnp.where(inner, ahead, 0.0) - roll(jnp.where(inner, back, 0.0), 1, 1)

    advect_u = 0.5 * (step_down(uu, uu) + step_right(across_u, across_vu))
    advect_v = 0.5 * (step_down(uv, vu) + step_right(across_v, across_v))
    damp = damp_ref[...]
    flat = [sum_u, sum_v, advect_u, advect_v, sea * damp * height_ref[...], sea * (4.0 + damp)]
    acc = jnp.zeros((ROWS, LANES), F32)
    for f in range(FLAT):
        flat_ref[tile(f), :] = flat[f]
        acc = jnp.where(lane // STRIP == f, roll(flat[f], STRIP * f + STRIP // 2, 1), acc)
    pack_ref[tile(lay.packs), :] = acc


def packed_comp(shape):
    return COMPS - 1 - lax.rem(lax.broadcasted_iota(jnp.int32, shape, 1) // SLOT, COMPS)


def unpack(x, t):
    return roll(x, -(SLOT * (PER - 1 - t % PER) + SLOT // 2), 1)


def spread(x, of):
    comp = packed_comp(x.shape)
    out = x
    for c in range(COMPS):
        if c != of:
            out = jnp.where(comp == c, roll(x, SLOT * (of - c), 1), out)
    return out


def across(x):
    half = lax.rem(lax.broadcasted_iota(jnp.int32, x.shape, 1), SLOT) < SLOT // 2
    return jnp.where(half, roll(x, -1, 1), roll(x, 1, 1))


def fold(x):
    step = SLOT * COMPS
    while step < LANES:
        x = x + roll(x, step, 1)
        step *= 2
    return x


def edge_kernel(pack_ref, first_ref, second_ref, done_ref, own_ref, near_ref, delta_ref, one_ref, two_ref):
    lay = Layout((pack_ref.shape[0] // ROWS - 1) * PER)
    at = Place()
    lane = iota(1)
    comp = packed_comp((ROWS, LANES))
    in_slot = lax.rem(lane, SLOT)
    half = in_slot < SLOT // 2
    sign = jnp.where(in_slot == SLOT // 2 - 1, 0.5, jnp.where(in_slot == SLOT // 2, -0.5, 0.0))

    def beyond(p, low):
        first, second = first_ref[tile(p), :], second_ref[tile(p), :]
        from_left = jnp.where(at.g_even, second, first) * at.left
        from_right = jnp.where(at.g_even, first, second) * at.right
        return jnp.where(low, from_left, from_right)

    def flow(x):
        return jnp.where(comp == 2, roll(x, SLOT, 1), x)

    near_ref[...] = jnp.zeros(near_ref.shape, F32)
    inner = jnp.zeros((ROWS, LANES), F32)
    outer = jnp.zeros((ROWS, LANES), F32)
    for p in range(lay.packs):
        own, far = pack_ref[tile(p), :], beyond(p, half)
        delta_ref[tile(p), :] = far - own
        near_ref[p : p + 1, :] = far[0:1]
        near_ref[lay.pad + p : lay.pad + p + 1, :] = far[ROWS - 1 : ROWS]
        inner = inner + flow(own) * across(far)
        outer = outer + flow(far) * across(own)
    inner, outer = fold(sign * inner), fold(sign * outer)
    strip = beyond(lay.packs, lax.rem(lane, STRIP) < STRIP // 2)
    for f in (2, 3):
        mid = STRIP * f + STRIP // 2
        border = (lane == mid - 1) | (lane == mid)
        strip = strip + jnp.where(border, roll(unpack(outer, f), mid, 1), 0.0)
    own_ref[0:ROWS, :] = strip
    own_ref[ROWS : 2 * ROWS, :] = inner

    def fill(low_ref, high_ref):
        for ref, rows in ((low_ref, slice(0, lay.pad)), (high_ref, slice(lay.pad, 2 * lay.pad))):
            ref[pl.ds(lay.edge, lay.pad), :] = near_ref[rows, :]
            ref[pl.ds(lay.strip, ROWS), :] = strip
            ref[pl.ds(lay.inner, ROWS), :] = inner

    pl.when(at.b_even)(lambda: fill(two_ref, one_ref))
    pl.when(jnp.logical_not(at.b_even))(lambda: fill(one_ref, two_ref))


def level_rows(m_ref, comp, row):
    lay = Layout(m_ref.shape[0] // ROWS)
    step = COMPS * ROWS
    parts = []
    for first in range(0, lay.levels, ROWS):
        start = min(first, lay.levels - ROWS)
        x = m_ref[pl.ds(start * step + comp * ROWS + row, ROWS, stride=step), :]
        parts.append(jnp.where(iota(0) < first - start, 0.0, x))
    return parts


def flow_kernel(m_ref, flat_ref, one_ref, two_ref):
    lay = Layout(m_ref.shape[0] // ROWS)

    def fill(low_ref, high_ref):
        for ref, row in ((low_ref, 0), (high_ref, ROWS - 1)):
            for c in range(2):
                for n, x in enumerate(level_rows(m_ref, 2 + c, row)):
                    ref[pl.ds(c * lay.flow + n * ROWS, ROWS), :] = x
            ref[pl.ds(lay.flat, FLAT * ROWS), :] = flat_ref[...]

    even = Place().b_even
    pl.when(even)(lambda: fill(two_ref, one_ref))
    pl.when(jnp.logical_not(even))(lambda: fill(one_ref, two_ref))


def rest_kernel(m_ref, delta_ref, after_ref, one_ref, two_ref):
    lay = Layout(m_ref.shape[0] // ROWS)

    def fill(low_ref, high_ref):
        for ref, row, near in ((low_ref, 0, 0), (high_ref, ROWS - 2, ROWS - 1)):
            for r in range(2):
                for s in range(lay.eights):
                    at = pl.ds(ROWS * ROWS * s + row + r, ROWS, stride=ROWS)
                    ref[tile(r * lay.eights + s), :] = m_ref[at, :]
            ref[pl.ds(lay.delta, lay.pad), :] = jnp.zeros((lay.pad, LANES), F32)
            for p in range(lay.packs):
                ref[pl.ds(lay.delta + p, 1), :] = delta_ref[pl.ds(ROWS * p + near, 1), :]

    even = Place().b_even
    pl.when(even)(lambda: fill(two_ref, one_ref))
    pl.when(jnp.logical_not(even))(lambda: fill(one_ref, two_ref))


def cross_kernel(m_ref, one_ref, two_ref, cross_ref):
    lay = Layout(m_ref.shape[0] // ROWS)
    at = Place()
    row = iota(0)
    count = lay.flow // ROWS

    def beyond(take, c):
        where = [pl.ds(c * lay.flow + n * ROWS, ROWS) for n in range(count)]
        return [take(one_ref[w, :], two_ref[w, :]) for w in where]

    above, below = [[beyond(take, c) for c in range(2)] for take in (at.from_up, at.from_down)]
    top, bottom = [[level_rows(m_ref, c, r) for c in (2, 3)] for r in (0, ROWS - 1)]

    def total(flow, carried):
        return 0.5 * jnp.sum(sum(x * y for x, y in zip(flow, carried)), axis=0, keepdims=True)

    out = jnp.zeros((ROWS, LANES), F32)
    for f in range(2):
        sums = (total(above[0], top[f]), -total(top[0], above[f]), total(bottom[0], below[f]), -total(below[0], bottom[f]))
        for k in range(4):
            out = jnp.where(row == 4 * f + k, sums[k], out)
    cross_ref[...] = out


def moment_kernel(
    flat_ref, own_ref, near_ref, cross_ref, flow_one_ref, flow_two_ref, one_ref, two_ref, done_ref, basis_ref, send_ref, wide_ref, *, levels
):
    lay = Layout(levels * COMPS)
    at = Place()
    row, lane = iota(0), iota(1)
    outside = (lane < STRIP // 2) | (lane >= LANES - STRIP // 2)
    rows = 3 * ROWS

    def neighbours(where, first_ref=one_ref, second_ref=two_ref):
        first, second = first_ref[where, :], second_ref[where, :]
        return at.from_up(first, second), at.from_down(first, second)

    def around(where, own, *refs):
        up, down = neighbours(where, *refs)
        return up, own, down

    strips = around(pl.ds(lay.strip, ROWS), own_ref[0:ROWS, :])
    inners = around(pl.ds(lay.inner, ROWS), own_ref[ROWS : 2 * ROWS, :])
    border = (lane == 0) | (lane == LANES - 1)
    for f in range(FLAT):
        fields = around(pl.ds(lay.flat + f * ROWS, ROWS), flat_ref[tile(f), :], flow_one_ref, flow_two_ref)
        for k in range(3):
            to = pl.ds(f * rows + k * ROWS, ROWS)
            value = fields[k]
            if 2 <= f <= 3:
                value = value + jnp.where(border, unpack(inners[k], f), 0.0)
            wide_ref[to, 0:LANES] = value
            side = roll(strips[k], -(STRIP * f + STRIP // 2), 1)
            wide_ref[to, LANES : 2 * LANES] = jnp.where(outside, side, 0.0)

    above, below = neighbours(pl.ds(lay.edge, lay.pad))
    top, bottom = near_ref[0 : lay.pad, :], near_ref[lay.pad :, :]

    def flow_packed(x):
        return roll(x, -SLOT, 1)

    def corner(a, b):
        x = jnp.where(packed_comp(a.shape) == 3, flow_packed(a), a) * b
        return 0.5 * fold(jnp.sum(x, axis=0, keepdims=True))

    corners = [corner(above, top), -corner(top, above), corner(bottom, below), -corner(below, bottom)]
    border = (iota(1, 1) < SLOT // 2) | (iota(1, 1) >= LANES - SLOT // 2)
    for f in (2, 3):
        for k, at_row in enumerate((ROWS - 1, ROWS, 2 * ROWS - 1, 2 * ROWS)):
            to = pl.ds(f * rows + at_row, 1)
            wide_ref[to, 0:LANES] = wide_ref[to, 0:LANES] + cross_ref[4 * (f - 2) + k : 4 * (f - 2) + k + 1, :]
            side = unpack(corners[k], f)
            wide_ref[to, LANES : 2 * LANES] = wide_ref[to, LANES : 2 * LANES] + jnp.where(border, side, 0.0)

    sum_u, sum_v, adv_u, adv_v, forcing, diagonal = [wide_ref[pl.ds(f * rows, rows), :] for f in range(FLAT)]
    sea = jnp.where(diagonal > 0.0, 1.0, 0.0)
    shape = (rows, 2 * LANES)
    i = iota(0, *shape) - ROWS + at.b * ROWS
    j = iota(1, *shape)
    j = jnp.where(j < LANES + LANES // 2, j, j - 2 * LANES) + at.g * LANES
    total_rows, total_cols = at.nb * ROWS, at.ng * LANES
    edges = (
        jnp.where(i == 0, 1.0, 0.0)
        + jnp.where(i == total_rows - 1, 1.0, 0.0)
        + jnp.where(j == 0, 1.0, 0.0)
        + jnp.where(j == total_cols - 1, 1.0, 0.0)
    )
    coriolis = rotation * (2.0 * (j.astype(F32) + 0.5) / total_cols - 1.0)

    def both(x, n, axis):
        return roll(x, n, axis) + roll(x, -n, axis)

    def transport(x, turn, adv):
        near = both(x, 1, 0)
        linear = (
            (1.0 - hyper_visc * (20.0 - edges)) * x
            + 8.0 * hyper_visc * near
            - hyper_visc * (both(x, 2, 0) + both(x, 2, 1))
            + both(8.0 * hyper_visc * x - 2.0 * hyper_visc * near, 1, 1)
        )
        return sea * (linear + time_step * (turn - adv)) / lay.levels

    east = transport(sum_u, coriolis * sum_v, adv_u)
    north = transport(sum_v, -coriolis * sum_u, adv_v)
    divergence = 0.5 * (roll(east, -1, 0) - roll(east, 1, 0) + roll(north, -1, 1) - roll(north, 1, 1))
    v = [forcing - gravity * sea * divergence]
    own_diagonal = diagonal - SHIFT
    for _ in range(ITERS):
        x = v[-1]
        v.append(own_diagonal * x - sea * (both(x, 1, 0) + both(x, 1, 1)))
    v = [x[ROWS : 2 * ROWS, 0:LANES] for x in v]

    def over_rows(x, y):
        return jnp.sum(x * y, axis=0, keepdims=True)

    norm, slope = [jnp.sum(over_rows(v[0], x), axis=1, keepdims=True) for x in v[:2]]
    theta = jnp.where(norm > 0.0, slope / jnp.where(norm > 0.0, norm, 1.0), 0.0)
    q = [v[0]] + [v[k] - theta * v[k - 1] for k in range(1, ITERS + 1)]
    for k in range(ITERS):
        basis_ref[tile(k), :] = q[k]
    basis_ref[tile(ITERS), :] = jnp.broadcast_to(theta, (ROWS, LANES))
    row, lane = iota(0, 2 * ROWS), iota(1, 2 * ROWS)
    line = jnp.zeros((2 * ROWS, LANES), F32)
    for k, (i, j) in enumerate(PAIRS):
        line = jnp.where(row == k, over_rows(q[i], q[j]), line)
    line = jnp.sum(line, axis=1, keepdims=True)
    line = jnp.where(row == len(PAIRS), theta, line)
    line = jnp.sum(jnp.where(row == lane, line, 0.0), axis=0, keepdims=True)
    send_ref[...] = jnp.broadcast_to(line, send_ref.shape)


def solve_kernel(
    got_ref, basis_ref, m_ref, one_ref, two_ref, mask_ref, state_in, state_ref, state_hbm, surface_hbm, surface_ref, sems
):
    lay = Layout(state_ref.shape[0] // ROWS)
    at = Place()
    place = pl.ds(lay.delta, lay.pad)
    in_slot = lax.rem(iota(1, lay.pad), SLOT)
    comp = lax.rem(iota(0), COMPS)
    border = (iota(1) < SLOT // 2) | (iota(1) >= LANES - SLOT // 2)
    near = (in_slot == SLOT // 2 - 1) | (in_slot == SLOT // 2)
    sea = mask_ref[...].astype(F32)
    sides = ((at.from_up, 1, 0, 0, 1, 0.5 * time_step), (at.from_down, 0, 1, ROWS - 1, ROWS - 2, -0.5 * time_step))
    fixes = [across(-2.0 * hyper_visc * side[0](one_ref[place, :], two_ref[place, :])) for side in sides]
    fixes = [jnp.where(near, x, 0.0) for x in fixes]
    writes = []
    for s in range(lay.eights):
        for (take, first, second, row, inner, slope), fix in zip(sides, fixes):
            x1, x2 = [take(one_ref[w, :], two_ref[w, :]) for w in (tile(n * lay.eights + s) for n in (first, second))]
            flow = m_ref[pl.ds(ROWS * ROWS * s + row, ROWS, stride=ROWS), :]
            u = flow
            for c in (0, 1, 3):
                u = jnp.where(comp == c, roll(flow, c - 2, 0), u)
            p, q = divmod(s * ROWS, PER)
            corner = jnp.broadcast_to(fix[p : p + 1], (ROWS, LANES))
            corner = pltpu.roll(corner, SLOT * q + SLOT // 2, 1, stride=SLOT, stride_axis=0)
            more = (
                hyper_visc * (8.0 * x1 - x2 - 2.0 * (roll(x1, 1, 1) + roll(x1, -1, 1)))
                + slope * u * x1
                + jnp.where(border, corner, 0.0)
            )
            to = pl.ds(ROWS * ROWS * s + row, ROWS, stride=ROWS)
            state_ref[to, :] = state_ref[to, :] + sea[row : row + 1] * more
            to = pl.ds(ROWS * ROWS * s + inner, ROWS, stride=ROWS)
            state_ref[to, :] = state_ref[to, :] - (hyper_visc * sea[inner : inner + 1]) * x1
        if s + 1 in (lay.eights // 2, lay.eights):
            start = len(writes) * (lay.eights // 2) * ROWS * ROWS
            part = pl.ds(start, (s + 1) * ROWS * ROWS - start)
            writes.append(pltpu.make_async_copy(state_ref.at[part], state_hbm.at[part], sems.at[len(writes)]))
            writes[-1].start()

    got = got_ref[...]
    gram = {pair: jnp.broadcast_to(got[:, k : k + 1], got.shape) for k, pair in enumerate(PAIRS)}
    theta = jnp.broadcast_to(got[:, len(PAIRS) : len(PAIRS) + 1], got.shape)

    def local(a, theta):
        out = [a[-1]]
        for x in a[-2::-1]:
            out.insert(0, x + theta * out[0])
        return out

    def dot(a, b):
        total = None
        for i, x in enumerate(local(a, theta)):
            part = None
            for j, y in enumerate(local(b, theta)):
                term = y * gram[min(i, j), max(i, j)]
                part = term if part is None else part + term
            total = x * part if total is None else total + x * part
        return jnp.sum(total, axis=0, keepdims=True)

    def add(a, scale, b):
        out = list(a) + [jnp.zeros_like(one)] * (len(b) - len(a))
        return [x + scale * b[n] if n < len(b) else x for n, x in enumerate(out)]

    def image(a):
        return [SHIFT * a[0]] + [SHIFT * a[n] + a[n - 1] for n in range(1, len(a))] + [a[-1]]

    one = jnp.ones((1, LANES), F32)
    residual, direction, surface = [one], [one], []
    norm = dot(residual, residual)
    for iteration in range(ITERS):
        applied = image(direction)
        alpha = norm / dot(direction, applied)
        if iteration:
            alpha = jnp.where(norm > 0.0, alpha, 0.0)
        surface = add(surface, alpha, direction)
        if iteration + 1 < ITERS:
            residual = add(residual, -alpha, applied)
            following = dot(residual, residual)
            ratio = following / norm
            if iteration:
                ratio = jnp.where(norm > 0.0, ratio, 0.0)
            direction = add(residual, ratio, direction)
            norm = following
    out = jnp.zeros((ROWS, LANES), F32)
    for k, x in enumerate(local(surface, basis_ref[tile(ITERS), :])):
        out = out + x * basis_ref[tile(k), :]
    surface_ref[...] = out
    writes.append(pltpu.make_async_copy(surface_ref, surface_hbm, sems.at[len(writes)]))
    writes[-1].start()
    for write in writes:
        write.wait()


def inner_kernel(m_ref, mask_ref, new_ref, done_ref):
    lay = Layout(m_ref.shape[0] // ROWS)
    at = Place()
    row, lane = iota(0), iota(1)
    sea = mask_ref[...].astype(F32)
    done_ref[...] = sea
    edges = (
        jnp.where((row == 0) & (at.b == 0), 1.0, 0.0)
        + jnp.where((row == ROWS - 1) & (at.b == at.nb - 1), 1.0, 0.0)
        + jnp.where((lane == 0) & (at.g == 0), 1.0, 0.0)
        + jnp.where((lane == LANES - 1) & (at.g == at.ng - 1), 1.0, 0.0)
    )
    centre = 1.0 - 2.0 * mixing - hyper_visc * (20.0 - edges)
    col = (lane + at.g * LANES).astype(F32)
    coriolis = time_step * rotation * (2.0 * (col + 0.5) / (at.ng * LANES) - 1.0)

    def own(level, c):
        return m_ref[tile(COMPS * min(max(level, 0), lay.levels - 1) + c), :]

    for k in range(lay.levels):
        u, v = own(k, 2), own(k, 3)
        half_u, half_v = 0.5 * time_step * u, 0.5 * time_step * v
        for c in range(COMPS):
            t = COMPS * k + c
            x = own(k, c)
            up1, dn1 = jnp.where(row == 0, 0.0, roll(x, 1, 0)), jnp.where(row == ROWS - 1, 0.0, roll(x, -1, 0))
            up2, dn2 = jnp.where(row < 2, 0.0, roll(x, 2, 0)), jnp.where(row >= ROWS - 2, 0.0, roll(x, -2, 0))
            left, right = roll(x, 1, 1), roll(x, -1, 1)
            near1 = up1 + dn1
            q = 8.0 * hyper_visc * x - 2.0 * hyper_visc * near1
            out = (
                centre * x
                + (roll(q, 1, 1) + roll(q, -1, 1))
                + 8.0 * hyper_visc * near1
                - hyper_visc * ((up2 + dn2) + (roll(x, 2, 1) + roll(x, -2, 1)))
                - (half_u * (dn1 - up1) + half_v * (right - left))
                + mixing * (own(k - 1, c) + own(k + 1, c))
            )
            if c == 2:
                out = out + coriolis * v
            if c == 3:
                out = out - coriolis * u
            new_ref[tile(t), :] = sea * out


def border_kernel(pack_ref, delta_ref, mask_ref, state_in, state_ref, done_ref):
    lay = Layout(state_ref.shape[0] // ROWS)
    lane = iota(1)
    border = (lane < SLOT // 2) | (lane >= LANES - SLOT // 2)
    sea = mask_ref[...].astype(F32)
    sea = jnp.where(border, sea, 0.0)
    done_ref[...] = sea
    d = delta_ref[...]
    row, in_slot = lax.rem(iota(0, d.shape[0]), ROWS), lax.rem(iota(1, d.shape[0]), SLOT)
    mid = SLOT // 2
    near = (in_slot == mid - 1) | (in_slot == mid)
    far = (in_slot >= mid - 2) & (in_slot <= mid + 1)
    sign = jnp.where(in_slot == mid - 1, -0.5 * time_step, jnp.where(in_slot == mid, 0.5 * time_step, 0.0))
    dv = jnp.where(row == 0, 0.0, roll(d, 1, 0)) + jnp.where(row == ROWS - 1, 0.0, roll(d, -1, 0))
    second = jnp.where(in_slot < mid, roll(d, -2, 1), roll(d, 2, 1))
    fix = (
        jnp.where(far, -hyper_visc * second, 0.0)
        + jnp.where(near, across(hyper_visc * (8.0 * d - 2.0 * dv)), 0.0)
        + sign * spread(pack_ref[0 : d.shape[0], :], 3) * across(d)
    )
    for t in range(lay.tiles):
        p = t // PER
        state_ref[tile(t), :] = state_ref[tile(t), :] + sea * unpack(fix[p * ROWS : (p + 1) * ROWS], t)


def call(kernel, outs, *args, scratch=(), specs=None, out_specs=None, aliases=None, flops=0):
    return pl.pallas_call(
        kernel,
        out_shape=[jax.ShapeDtypeStruct(s, F32) for s in outs],
        in_specs=specs or [VMEM] * len(args),
        out_specs=out_specs or [VMEM] * len(outs),
        scratch_shapes=[pltpu.VMEM(s, F32) if isinstance(s, tuple) else s for s in scratch],
        input_output_aliases=aliases or {},
        compiler_params=pltpu.CompilerParams(vmem_limit_bytes=8 * 1024 * 1024),
        cost_estimate=pl.CostEstimate(flops=flops, bytes_accessed=0, transcendentals=0),
    )(*args)


def on_device(ocean_state, surface_height, surface_damping, land_mask, *, shape):
    nb, ng = shape
    axes = ("blocks", "group")
    state = ocean_state.reshape(-1, LANES)
    lay = Layout(state.shape[0] // ROWS)
    g_one, g_two = swap_pairs(shape, "group")
    b_one, b_two = swap_pairs(shape, "blocks")
    one_tile = (ROWS, LANES)
    packed = (lay.packs * ROWS, LANES)
    flats = (FLAT * ROWS, LANES)

    m, pack, flat = call(
        pack_kernel,
        [state.shape, (packed[0] + ROWS, LANES), flats],
        *[pltpu.with_memory_space_constraint(x, pltpu.HBM) for x in (state, land_mask, surface_height, surface_damping)],
        specs=[HBM] * 4,
        scratch=[
            state.shape,
            pltpu.VMEM(one_tile, land_mask.dtype),
            one_tile,
            one_tile,
            pltpu.SemaphoreType.DMA((3 + lay.packs,)),
        ],
    )
    first = lax.ppermute(pack, axes, g_one)
    second = lax.ppermute(pack, axes, g_two)
    flow_one, flow_two = call(flow_kernel, [(lay.early, LANES)] * 2, m, flat)
    flow_one = lax.ppermute(flow_one, axes, b_one)
    flow_two = lax.ppermute(flow_two, axes, b_two)
    part, inner_done = call(inner_kernel, [state.shape, one_tile], m, land_mask, flops=LONG)
    message = (lay.message, LANES)
    own, near, delta, one, two = call(
        edge_kernel,
        [(2 * ROWS, LANES), (2 * lay.pad, LANES), packed, message, message],
        pack,
        first,
        second,
        inner_done,
        flops=10 * LONG,
    )
    one = lax.ppermute(one, axes, b_one)
    two = lax.ppermute(two, axes, b_two)
    (cross,) = call(cross_kernel, [one_tile], m, flow_one, flow_two)
    part, done = call(border_kernel, [state.shape, one_tile], pack, delta, land_mask, part, aliases={3: 0}, flops=LONG)
    rest_one, rest_two = call(rest_kernel, [(lay.rest, LANES)] * 2, m, delta, cross)
    rest_one = lax.ppermute(rest_one, axes, b_one)
    rest_two = lax.ppermute(rest_two, axes, b_two)
    basis, sent = call(
        functools.partial(moment_kernel, levels=lay.levels),
        [((ITERS + 1) * ROWS, LANES), (nb * ng, LANES)],
        flat,
        own,
        near,
        cross,
        flow_one,
        flow_two,
        one,
        two,
        done,
        scratch=[(FLAT * 3 * ROWS, 2 * LANES)],
        flops=LONG,
    )
    got = lax.all_to_all(sent, axes, 0, 0, tiled=True)
    _, new_state, surface = call(
        solve_kernel,
        [state.shape, state.shape, one_tile],
        got,
        basis,
        m,
        rest_one,
        rest_two,
        land_mask,
        part,
        scratch=[one_tile, pltpu.SemaphoreType.DMA((3,))],
        out_specs=[VMEM, HBM, HBM],
        aliases={6: 0},
    )
    return new_state.reshape(ocean_state.shape), surface


def solution(mesh):
    placed = (
        P(None, None, "blocks", "group"),
        P("blocks", "group"),
        P("blocks", "group"),
        P("blocks", "group"),
    )
    shape = (mesh.shape["blocks"], mesh.shape["group"])

    def body(*args):
        return on_device(*args, shape=shape)

    return jax.shard_map(
        body,
        mesh=mesh,
        in_specs=placed,
        out_specs=(P(None, None, "blocks", "group"), P("blocks", "group")),
        check_vma=False,
    )
```

```python
import functools

import jax
import jax.numpy as jnp
from jax import lax
from jax.experimental import pallas as pl
from jax.experimental.pallas import tpu as pltpu
from jax.sharding import PartitionSpec as P

ITERS = 3

time_step = 0.25
hyper_visc = 0.025
mixing = 0.2
gravity = 4.0
rotation = 0.2

COMPS = 4
ROWS = 8
LANES = 128
SLOT = 8
PER = LANES // SLOT
FLAT = 6
STRIP = 16
LONG = 10**9
SHIFT = 4.5
PAIRS = [(i, j) for i in range(ITERS) for j in range(i, ITERS + 1)]
F32 = jnp.float32
VMEM = pl.BlockSpec(memory_space=pltpu.VMEM)
HBM = pl.BlockSpec(memory_space=pltpu.HBM)


def iota(axis, rows=ROWS, lanes=LANES):
    return lax.broadcasted_iota(jnp.int32, (rows, lanes), axis)


def roll(x, shift, axis):
    return pltpu.roll(x, shift % x.shape[axis], axis)


def tile(k):
    return pl.ds(k * ROWS, ROWS)


def swap_pairs(mesh_shape, along):
    nb, ng = mesh_shape
    first, second = [], []
    for b in range(nb):
        for g in range(ng):
            me = b * ng + g
            if along == "blocks":
                one = (b ^ 1, g)
                two = ((b - 1) ^ 1) + 1
                two = (two, g) if 0 <= two < nb else (b, g ^ 1)
            else:
                one = (b, g ^ 1)
                two = ((g - 1) ^ 1) + 1
                two = (b, two) if 0 <= two < ng else (b ^ 1, g)
            first.append((me, one[0] * ng + one[1]))
            second.append((me, two[0] * ng + two[1]))
    return first, second


class Layout:
    def __init__(self, tiles):
        self.tiles = tiles
        self.levels = tiles // COMPS
        self.packs = tiles // PER
        self.eights = tiles // ROWS
        self.pad = -(-self.packs // ROWS) * ROWS
        self.flow = -(-self.levels // ROWS) * ROWS
        self.flat = 2 * self.flow
        self.early = self.flat + FLAT * ROWS
        self.edge = 0
        self.strip = self.pad
        self.inner = self.strip + ROWS
        self.message = self.inner + ROWS
        self.delta = 2 * tiles
        self.rest = self.delta + self.pad


class Place:
    def __init__(self):
        self.b, self.nb = lax.axis_index("blocks"), lax.axis_size("blocks")
        self.g, self.ng = lax.axis_index("group"), lax.axis_size("group")
        self.b_even = lax.rem(self.b, 2) == 0
        self.g_even = lax.rem(self.g, 2) == 0
        self.up = (self.b > 0).astype(F32)
        self.down = (self.b < self.nb - 1).astype(F32)
        self.left = (self.g > 0).astype(F32)
        self.right = (self.g < self.ng - 1).astype(F32)

    def from_up(self, one, two):
        return jnp.where(self.b_even, two, one) * self.up

    def from_down(self, one, two):
        return jnp.where(self.b_even, one, two) * self.down


def pack_kernel(
    state_hbm, mask_hbm, height_hbm, damp_hbm, m_ref, pack_ref, flat_ref, state_ref, mask_ref, height_ref, damp_ref, sems
):
    lay = Layout(m_ref.shape[0] // ROWS)
    chunk = PER * ROWS
    small = [(mask_hbm, mask_ref), (height_hbm, height_ref), (damp_hbm, damp_ref)]
    copies = [pltpu.make_async_copy(a, b, sems.at[k]) for k, (a, b) in enumerate(small)]
    for p in range(lay.packs):
        at = pl.ds(p * chunk, chunk)
        copies.append(pltpu.make_async_copy(state_hbm.at[at], state_ref.at[at], sems.at[3 + p]))
    for copy in copies:
        copy.start()
    for copy in copies[: 3 + lay.packs // 2]:
        copy.wait()
    sea = mask_ref[...].astype(F32)
    row, lane = iota(0), iota(1)
    slot = lane // SLOT
    sum_u = sum_v = uu = uv = vu = zero = jnp.zeros((ROWS, LANES), F32)
    across_u = across_v = across_vu = zero
    for p in range(lay.packs):
        if p == lay.packs // 2:
            for copy in copies[3 + p :]:
                copy.wait()
        acc = zero
        for k in range(PER // COMPS):
            x = []
            for c in range(COMPS):
                q = COMPS * k + c
                x.append(state_ref[tile(p * PER + q), :] * sea)
                m_ref[tile(p * PER + q), :] = x[c]
                at = PER - 1 - q
                acc = jnp.where(slot == at, roll(x[c], SLOT * at + SLOT // 2, 1), acc)
            u, v = x[2:]
            below_u, below_v = roll(u, -1, 0), roll(v, -1, 0)
            right_u, right_v = roll(u, -1, 1), roll(v, -1, 1)
            sum_u, sum_v = sum_u + u, sum_v + v
            uu, uv, vu = uu + u * below_u, uv + u * below_v, vu + v * below_u
            across_u, across_v, across_vu = across_u + v * right_u, across_v + v * right_v, across_vu + u * right_v
        pack_ref[tile(p), :] = acc

    def step_down(ahead, back):
        inner = row < ROWS - 1
        return jnp.where(inner, ahead, 0.0) - roll(jnp.where(inner, back, 0.0), 1, 0)

    def step_right(ahead, back):
        inner = lane < LANES - 1
        return jnp.where(inner, ahead, 0.0) - roll(jnp.where(inner, back, 0.0), 1, 1)

    advect_u = 0.5 * (step_down(uu, uu) + step_right(across_u, across_vu))
    advect_v = 0.5 * (step_down(uv, vu) + step_right(across_v, across_v))
    damp = damp_ref[...]
    flat = [sum_u, sum_v, advect_u, advect_v, sea * damp * height_ref[...], sea * (4.0 + damp)]
    acc = jnp.zeros((ROWS, LANES), F32)
    for f in range(FLAT):
        flat_ref[tile(f), :] = flat[f]
        acc = jnp.where(lane // STRIP == f, roll(flat[f], STRIP * f + STRIP // 2, 1), acc)
    pack_ref[tile(lay.packs), :] = acc


def packed_comp(shape):
    return COMPS - 1 - lax.rem(lax.broadcasted_iota(jnp.int32, shape, 1) // SLOT, COMPS)


def unpack(x, t):
    return roll(x, -(SLOT * (PER - 1 - t % PER) + SLOT // 2), 1)


def spread(x, of):
    comp = packed_comp(x.shape)
    out = x
    for c in range(COMPS):
        if c != of:
            out = jnp.where(comp == c, roll(x, SLOT * (of - c), 1), out)
    return out


def across(x):
    half = lax.rem(lax.broadcasted_iota(jnp.int32, x.shape, 1), SLOT) < SLOT // 2
    return jnp.where(half, roll(x, -1, 1), roll(x, 1, 1))


def fold(x):
    step = SLOT * COMPS
    while step < LANES:
        x = x + roll(x, step, 1)
        step *= 2
    return x


def edge_kernel(pack_ref, first_ref, second_ref, done_ref, own_ref, near_ref, delta_ref, one_ref, two_ref):
    lay = Layout((pack_ref.shape[0] // ROWS - 1) * PER)
    at = Place()
    lane = iota(1)
    comp = packed_comp((ROWS, LANES))
    in_slot = lax.rem(lane, SLOT)
    half = in_slot < SLOT // 2
    sign = jnp.where(in_slot == SLOT // 2 - 1, 0.5, jnp.where(in_slot == SLOT // 2, -0.5, 0.0))

    def beyond(p, low):
        first, second = first_ref[tile(p), :], second_ref[tile(p), :]
        from_left = jnp.where(at.g_even, second, first) * at.left
        from_right = jnp.where(at.g_even, first, second) * at.right
        return jnp.where(low, from_left, from_right)

    def flow(x):
        return jnp.where(comp == 2, roll(x, SLOT, 1), x)

    near_ref[...] = jnp.zeros(near_ref.shape, F32)
    inner = jnp.zeros((ROWS, LANES), F32)
    outer = jnp.zeros((ROWS, LANES), F32)
    for p in range(lay.packs):
        own, far = pack_ref[tile(p), :], beyond(p, half)
        delta_ref[tile(p), :] = far - own
        near_ref[p : p + 1, :] = far[0:1]
        near_ref[lay.pad + p : lay.pad + p + 1, :] = far[ROWS - 1 : ROWS]
        inner = inner + flow(own) * across(far)
        outer = outer + flow(far) * across(own)
    inner, outer = fold(sign * inner), fold(sign * outer)
    strip = beyond(lay.packs, lax.rem(lane, STRIP) < STRIP // 2)
    for f in (2, 3):
        mid = STRIP * f + STRIP // 2
        border = (lane == mid - 1) | (lane == mid)
        strip = strip + jnp.where(border, roll(unpack(outer, f), mid, 1), 0.0)
    own_ref[0:ROWS, :] = strip
    own_ref[ROWS : 2 * ROWS, :] = inner

    def fill(low_ref, high_ref):
        for ref, rows in ((low_ref, slice(0, lay.pad)), (high_ref, slice(lay.pad, 2 * lay.pad))):
            ref[pl.ds(lay.edge, lay.pad), :] = near_ref[rows, :]
            ref[pl.ds(lay.strip, ROWS), :] = strip
            ref[pl.ds(lay.inner, ROWS), :] = inner

    pl.when(at.b_even)(lambda: fill(two_ref, one_ref))
    pl.when(jnp.logical_not(at.b_even))(lambda: fill(one_ref, two_ref))


def level_rows(m_ref, comp, row):
    lay = Layout(m_ref.shape[0] // ROWS)
    step = COMPS * ROWS
    parts = []
    for first in range(0, lay.levels, ROWS):
        start = min(first, lay.levels - ROWS)
        x = m_ref[pl.ds(start * step + comp * ROWS + row, ROWS, stride=step), :]
        parts.append(jnp.where(iota(0) < first - start, 0.0, x))
    return parts


def flow_kernel(m_ref, flat_ref, one_ref, two_ref):
    lay = Layout(m_ref.shape[0] // ROWS)

    def fill(low_ref, high_ref):
        for ref, row in ((low_ref, 0), (high_ref, ROWS - 1)):
            for c in range(2):
                for n, x in enumerate(level_rows(m_ref, 2 + c, row)):
                    ref[pl.ds(c * lay.flow + n * ROWS, ROWS), :] = x
            ref[pl.ds(lay.flat, FLAT * ROWS), :] = flat_ref[...]

    even = Place().b_even
    pl.when(even)(lambda: fill(two_ref, one_ref))
    pl.when(jnp.logical_not(even))(lambda: fill(one_ref, two_ref))


def rest_kernel(m_ref, delta_ref, after_ref, one_ref, two_ref):
    lay = Layout(m_ref.shape[0] // ROWS)

    def fill(low_ref, high_ref):
        for ref, row, near in ((low_ref, 0, 0), (high_ref, ROWS - 2, ROWS - 1)):
            for r in range(2):
                for s in range(lay.eights):
                    at = pl.ds(ROWS * ROWS * s + row + r, ROWS, stride=ROWS)
                    ref[tile(r * lay.eights + s), :] = m_ref[at, :]
            ref[pl.ds(lay.delta, lay.pad), :] = jnp.zeros((lay.pad, LANES), F32)
            for p in range(lay.packs):
                ref[pl.ds(lay.delta + p, 1), :] = delta_ref[pl.ds(ROWS * p + near, 1), :]

    even = Place().b_even
    pl.when(even)(lambda: fill(two_ref, one_ref))
    pl.when(jnp.logical_not(even))(lambda: fill(one_ref, two_ref))


def cross_kernel(m_ref, one_ref, two_ref, cross_ref):
    lay = Layout(m_ref.shape[0] // ROWS)
    at = Place()
    row = iota(0)
    count = lay.flow // ROWS

    def beyond(take, c):
        where = [pl.ds(c * lay.flow + n * ROWS, ROWS) for n in range(count)]
        return [take(one_ref[w, :], two_ref[w, :]) for w in where]

    above, below = [[beyond(take, c) for c in range(2)] for take in (at.from_up, at.from_down)]
    top, bottom = [[level_rows(m_ref, c, r) for c in (2, 3)] for r in (0, ROWS - 1)]

    def total(flow, carried):
        return 0.5 * jnp.sum(sum(x * y for x, y in zip(flow, carried)), axis=0, keepdims=True)

    out = jnp.zeros((ROWS, LANES), F32)
    for f in range(2):
        sums = (total(above[0], top[f]), -total(top[0], above[f]), total(bottom[0], below[f]), -total(below[0], bottom[f]))
        for k in range(4):
            out = jnp.where(row == 4 * f + k, sums[k], out)
    cross_ref[...] = out


def moment_kernel(
    flat_ref, own_ref, near_ref, cross_ref, flow_one_ref, flow_two_ref, one_ref, two_ref, done_ref, basis_ref, send_ref, wide_ref, *, levels
):
    lay = Layout(levels * COMPS)
    at = Place()
    row, lane = iota(0), iota(1)
    outside = (lane < STRIP // 2) | (lane >= LANES - STRIP // 2)
    rows = 3 * ROWS

    def neighbours(where, first_ref=one_ref, second_ref=two_ref):
        first, second = first_ref[where, :], second_ref[where, :]
        return at.from_up(first, second), at.from_down(first, second)

    def around(where, own, *refs):
        up, down = neighbours(where, *refs)
        return up, own, down

    strips = around(pl.ds(lay.strip, ROWS), own_ref[0:ROWS, :])
    inners = around(pl.ds(lay.inner, ROWS), own_ref[ROWS : 2 * ROWS, :])
    border = (lane == 0) | (lane == LANES - 1)
    for f in range(FLAT):
        fields = around(pl.ds(lay.flat + f * ROWS, ROWS), flat_ref[tile(f), :], flow_one_ref, flow_two_ref)
        for k in range(3):
            to = pl.ds(f * rows + k * ROWS, ROWS)
            value = fields[k]
            if 2 <= f <= 3:
                value = value + jnp.where(border, unpack(inners[k], f), 0.0)
            wide_ref[to, 0:LANES] = value
            side = roll(strips[k], -(STRIP * f + STRIP // 2), 1)
            wide_ref[to, LANES : 2 * LANES] = jnp.where(outside, side, 0.0)

    above, below = neighbours(pl.ds(lay.edge, lay.pad))
    top, bottom = near_ref[0 : lay.pad, :], near_ref[lay.pad :, :]

    def flow_packed(x):
        return roll(x, -SLOT, 1)

    def corner(a, b):
        x = jnp.where(packed_comp(a.shape) == 3, flow_packed(a), a) * b
        return 0.5 * fold(jnp.sum(x, axis=0, keepdims=True))

    corners = [corner(above, top), -corner(top, above), corner(bottom, below), -corner(below, bottom)]
    border = (iota(1, 1) < SLOT // 2) | (iota(1, 1) >= LANES - SLOT // 2)
    for f in (2, 3):
        for k, at_row in enumerate((ROWS - 1, ROWS, 2 * ROWS - 1, 2 * ROWS)):
            to = pl.ds(f * rows + at_row, 1)
            wide_ref[to, 0:LANES] = wide_ref[to, 0:LANES] + cross_ref[4 * (f - 2) + k : 4 * (f - 2) + k + 1, :]
            side = unpack(corners[k], f)
            wide_ref[to, LANES : 2 * LANES] = wide_ref[to, LANES : 2 * LANES] + jnp.where(border, side, 0.0)

    sum_u, sum_v, adv_u, adv_v, forcing, diagonal = [wide_ref[pl.ds(f * rows, rows), :] for f in range(FLAT)]
    sea = jnp.where(diagonal > 0.0, 1.0, 0.0)
    shape = (rows, 2 * LANES)
    i = iota(0, *shape) - ROWS + at.b * ROWS
    j = iota(1, *shape)
    j = jnp.where(j < LANES + LANES // 2, j, j - 2 * LANES) + at.g * LANES
    total_rows, total_cols = at.nb * ROWS, at.ng * LANES
    edges = (
        jnp.where(i == 0, 1.0, 0.0)
        + jnp.where(i == total_rows - 1, 1.0, 0.0)
        + jnp.where(j == 0, 1.0, 0.0)
        + jnp.where(j == total_cols - 1, 1.0, 0.0)
    )
    coriolis = rotation * (2.0 * (j.astype(F32) + 0.5) / total_cols - 1.0)

    def both(x, n, axis):
        return roll(x, n, axis) + roll(x, -n, axis)

    def transport(x, turn, adv):
        near = both(x, 1, 0)
        linear = (
            (1.0 - hyper_visc * (20.0 - edges)) * x
            + 8.0 * hyper_visc * near
            - hyper_visc * (both(x, 2, 0) + both(x, 2, 1))
            + both(8.0 * hyper_visc * x - 2.0 * hyper_visc * near, 1, 1)
        )
        return sea * (linear + time_step * (turn - adv)) / lay.levels

    east = transport(sum_u, coriolis * sum_v, adv_u)
    north = transport(sum_v, -coriolis * sum_u, adv_v)
    divergence = 0.5 * (roll(east, -1, 0) - roll(east, 1, 0) + roll(north, -1, 1) - roll(north, 1, 1))
    v = [forcing - gravity * sea * divergence]
    own_diagonal = diagonal - SHIFT
    for _ in range(ITERS):
        x = v[-1]
        v.append(own_diagonal * x - sea * (both(x, 1, 0) + both(x, 1, 1)))
    v = [x[ROWS : 2 * ROWS, 0:LANES] for x in v]

    def over_rows(x, y):
        return jnp.sum(x * y, axis=0, keepdims=True)

    norm, slope = [jnp.sum(over_rows(v[0], x), axis=1, keepdims=True) for x in v[:2]]
    theta = jnp.where(norm > 0.0, slope / jnp.where(norm > 0.0, norm, 1.0), 0.0)
    q = [v[0]] + [v[k] - theta * v[k - 1] for k in range(1, ITERS + 1)]
    for k in range(ITERS):
        basis_ref[tile(k), :] = q[k]
    basis_ref[tile(ITERS), :] = jnp.broadcast_to(theta, (ROWS, LANES))
    row, lane = iota(0, 2 * ROWS), iota(1, 2 * ROWS)
    line = jnp.zeros((2 * ROWS, LANES), F32)
    for k, (i, j) in enumerate(PAIRS):
        line = jnp.where(row == k, over_rows(q[i], q[j]), line)
    line = jnp.sum(line, axis=1, keepdims=True)
    line = jnp.where(row == len(PAIRS), theta, line)
    line = jnp.sum(jnp.where(row == lane, line, 0.0), axis=0, keepdims=True)
    send_ref[...] = jnp.broadcast_to(line, send_ref.shape)


def solve_kernel(
    got_ref, basis_ref, m_ref, one_ref, two_ref, mask_ref, part_ref, state_hbm, surface_hbm, state_ref, surface_ref, sems
):
    lay = Layout(state_ref.shape[0] // ROWS)
    at = Place()
    place = pl.ds(lay.delta, lay.pad)
    in_slot = lax.rem(iota(1, lay.pad), SLOT)
    comp = lax.rem(iota(0), COMPS)
    border = (iota(1) < SLOT // 2) | (iota(1) >= LANES - SLOT // 2)
    near = (in_slot == SLOT // 2 - 1) | (in_slot == SLOT // 2)
    sea = mask_ref[...].astype(F32)
    sides = ((at.from_up, 1, 0, 0, 1, 0.5 * time_step), (at.from_down, 0, 1, ROWS - 1, ROWS - 2, -0.5 * time_step))
    fixes = [across(-2.0 * hyper_visc * side[0](one_ref[place, :], two_ref[place, :])) for side in sides]
    fixes = [jnp.where(near, x, 0.0) for x in fixes]
    writes = []
    for s in range(lay.eights):
        group = pl.ds(ROWS * ROWS * s, ROWS * ROWS)
        state_ref[group, :] = part_ref[group, :]
        for (take, first, second, row, inner, slope), fix in zip(sides, fixes):
            x1, x2 = [take(one_ref[w, :], two_ref[w, :]) for w in (tile(n * lay.eights + s) for n in (first, second))]
            flow = m_ref[pl.ds(ROWS * ROWS * s + row, ROWS, stride=ROWS), :]
            u = flow
            for c in (0, 1, 3):
                u = jnp.where(comp == c, roll(flow, c - 2, 0), u)
            p, q = divmod(s * ROWS, PER)
            corner = jnp.broadcast_to(fix[p : p + 1], (ROWS, LANES))
            corner = pltpu.roll(corner, SLOT * q + SLOT // 2, 1, stride=SLOT, stride_axis=0)
            more = (
                hyper_visc * (8.0 * x1 - x2 - 2.0 * (roll(x1, 1, 1) + roll(x1, -1, 1)))
                + slope * u * x1
                + jnp.where(border, corner, 0.0)
            )
            to = pl.ds(ROWS * ROWS * s + row, ROWS, stride=ROWS)
            state_ref[to, :] = state_ref[to, :] + sea[row : row + 1] * more
            to = pl.ds(ROWS * ROWS * s + inner, ROWS, stride=ROWS)
            state_ref[to, :] = state_ref[to, :] - (hyper_visc * sea[inner : inner + 1]) * x1
        if s + 1 in (lay.eights // 2, lay.eights):
            start = len(writes) * (lay.eights // 2) * ROWS * ROWS
            part = pl.ds(start, (s + 1) * ROWS * ROWS - start)
            writes.append(pltpu.make_async_copy(state_ref.at[part], state_hbm.at[part], sems.at[len(writes)]))
            writes[-1].start()

    got = got_ref[...]
    gram = {pair: jnp.broadcast_to(got[:, k : k + 1], got.shape) for k, pair in enumerate(PAIRS)}
    theta = jnp.broadcast_to(got[:, len(PAIRS) : len(PAIRS) + 1], got.shape)

    def local(a, theta):
        out = [a[-1]]
        for x in a[-2::-1]:
            out.insert(0, x + theta * out[0])
        return out

    def dot(a, b):
        total = None
        for i, x in enumerate(local(a, theta)):
            part = None
            for j, y in enumerate(local(b, theta)):
                term = y * gram[min(i, j), max(i, j)]
                part = term if part is None else part + term
            total = x * part if total is None else total + x * part
        return jnp.sum(total, axis=0, keepdims=True)

    def add(a, scale, b):
        out = list(a) + [jnp.zeros_like(one)] * (len(b) - len(a))
        return [x + scale * b[n] if n < len(b) else x for n, x in enumerate(out)]

    def image(a):
        return [SHIFT * a[0]] + [SHIFT * a[n] + a[n - 1] for n in range(1, len(a))] + [a[-1]]

    one = jnp.ones((1, LANES), F32)
    residual, direction, surface = [one], [one], []
    norm = dot(residual, residual)
    for iteration in range(ITERS):
        applied = image(direction)
        alpha = norm / dot(direction, applied)
        if iteration:
            alpha = jnp.where(norm > 0.0, alpha, 0.0)
        surface = add(surface, alpha, direction)
        if iteration + 1 < ITERS:
            residual = add(residual, -alpha, applied)
            following = dot(residual, residual)
            ratio = following / norm
            if iteration:
                ratio = jnp.where(norm > 0.0, ratio, 0.0)
            direction = add(residual, ratio, direction)
            norm = following
    out = jnp.zeros((ROWS, LANES), F32)
    for k, x in enumerate(local(surface, basis_ref[tile(ITERS), :])):
        out = out + x * basis_ref[tile(k), :]
    surface_ref[...] = out
    writes.append(pltpu.make_async_copy(surface_ref, surface_hbm, sems.at[len(writes)]))
    writes[-1].start()
    for write in writes:
        write.wait()


def inner_kernel(m_ref, mask_ref, new_ref, done_ref):
    lay = Layout(m_ref.shape[0] // ROWS)
    at = Place()
    row, lane = iota(0), iota(1)
    sea = mask_ref[...].astype(F32)
    done_ref[...] = sea
    edges = (
        jnp.where((row == 0) & (at.b == 0), 1.0, 0.0)
        + jnp.where((row == ROWS - 1) & (at.b == at.nb - 1), 1.0, 0.0)
        + jnp.where((lane == 0) & (at.g == 0), 1.0, 0.0)
        + jnp.where((lane == LANES - 1) & (at.g == at.ng - 1), 1.0, 0.0)
    )
    centre = 1.0 - 2.0 * mixing - hyper_visc * (20.0 - edges)
    col = (lane + at.g * LANES).astype(F32)
    coriolis = time_step * rotation * (2.0 * (col + 0.5) / (at.ng * LANES) - 1.0)

    def own(level, c):
        return m_ref[tile(COMPS * min(max(level, 0), lay.levels - 1) + c), :]

    for k in range(lay.levels):
        u, v = own(k, 2), own(k, 3)
        half_u, half_v = 0.5 * time_step * u, 0.5 * time_step * v
        for c in range(COMPS):
            t = COMPS * k + c
            x = own(k, c)
            up1, dn1 = jnp.where(row == 0, 0.0, roll(x, 1, 0)), jnp.where(row == ROWS - 1, 0.0, roll(x, -1, 0))
            up2, dn2 = jnp.where(row < 2, 0.0, roll(x, 2, 0)), jnp.where(row >= ROWS - 2, 0.0, roll(x, -2, 0))
            left, right = roll(x, 1, 1), roll(x, -1, 1)
            near1 = up1 + dn1
            q = 8.0 * hyper_visc * x - 2.0 * hyper_visc * near1
            out = (
                centre * x
                + (roll(q, 1, 1) + roll(q, -1, 1))
                + 8.0 * hyper_visc * near1
                - hyper_visc * ((up2 + dn2) + (roll(x, 2, 1) + roll(x, -2, 1)))
                - (half_u * (dn1 - up1) + half_v * (right - left))
                + mixing * (own(k - 1, c) + own(k + 1, c))
            )
            if c == 2:
                out = out + coriolis * v
            if c == 3:
                out = out - coriolis * u
            new_ref[tile(t), :] = sea * out


def border_kernel(pack_ref, delta_ref, mask_ref, part_ref, state_ref, done_ref):
    lay = Layout(state_ref.shape[0] // ROWS)
    lane = iota(1)
    border = (lane < SLOT // 2) | (lane >= LANES - SLOT // 2)
    sea = mask_ref[...].astype(F32)
    sea = jnp.where(border, sea, 0.0)
    done_ref[...] = sea
    d = delta_ref[...]
    row, in_slot = lax.rem(iota(0, d.shape[0]), ROWS), lax.rem(iota(1, d.shape[0]), SLOT)
    mid = SLOT // 2
    near = (in_slot == mid - 1) | (in_slot == mid)
    far = (in_slot >= mid - 2) & (in_slot <= mid + 1)
    sign = jnp.where(in_slot == mid - 1, -0.5 * time_step, jnp.where(in_slot == mid, 0.5 * time_step, 0.0))
    dv = jnp.where(row == 0, 0.0, roll(d, 1, 0)) + jnp.where(row == ROWS - 1, 0.0, roll(d, -1, 0))
    second = jnp.where(in_slot < mid, roll(d, -2, 1), roll(d, 2, 1))
    fix = (
        jnp.where(far, -hyper_visc * second, 0.0)
        + jnp.where(near, across(hyper_visc * (8.0 * d - 2.0 * dv)), 0.0)
        + sign * spread(pack_ref[0 : d.shape[0], :], 3) * across(d)
    )
    for t in range(lay.tiles):
        p = t // PER
        state_ref[tile(t), :] = part_ref[tile(t), :] + sea * unpack(fix[p * ROWS : (p + 1) * ROWS], t)


def call(kernel, outs, *args, scratch=(), specs=None, out_specs=None, flops=0):
    return pl.pallas_call(
        kernel,
        out_shape=[jax.ShapeDtypeStruct(s, F32) for s in outs],
        in_specs=specs or [VMEM] * len(args),
        out_specs=out_specs or [VMEM] * len(outs),
        scratch_shapes=[pltpu.VMEM(s, F32) if isinstance(s, tuple) else s for s in scratch],
        compiler_params=pltpu.CompilerParams(vmem_limit_bytes=8 * 1024 * 1024),
        cost_estimate=pl.CostEstimate(flops=flops, bytes_accessed=0, transcendentals=0),
    )(*args)


def on_device(ocean_state, surface_height, surface_damping, land_mask, *, shape):
    nb, ng = shape
    axes = ("blocks", "group")
    state = ocean_state.reshape(-1, LANES)
    lay = Layout(state.shape[0] // ROWS)
    g_one, g_two = swap_pairs(shape, "group")
    b_one, b_two = swap_pairs(shape, "blocks")
    one_tile = (ROWS, LANES)
    packed = (lay.packs * ROWS, LANES)
    flats = (FLAT * ROWS, LANES)

    m, pack, flat = call(
        pack_kernel,
        [state.shape, (packed[0] + ROWS, LANES), flats],
        *[pltpu.with_memory_space_constraint(x, pltpu.HBM) for x in (state, land_mask, surface_height, surface_damping)],
        specs=[HBM] * 4,
        scratch=[
            state.shape,
            pltpu.VMEM(one_tile, land_mask.dtype),
            one_tile,
            one_tile,
            pltpu.SemaphoreType.DMA((3 + lay.packs,)),
        ],
    )
    first = lax.ppermute(pack, axes, g_one)
    second = lax.ppermute(pack, axes, g_two)
    flow_one, flow_two = call(flow_kernel, [(lay.early, LANES)] * 2, m, flat)
    flow_one = lax.ppermute(flow_one, axes, b_one)
    flow_two = lax.ppermute(flow_two, axes, b_two)
    part, inner_done = call(inner_kernel, [state.shape, one_tile], m, land_mask, flops=LONG)
    message = (lay.message, LANES)
    own, near, delta, one, two = call(
        edge_kernel,
        [(2 * ROWS, LANES), (2 * lay.pad, LANES), packed, message, message],
        pack,
        first,
        second,
        inner_done,
        flops=10 * LONG,
    )
    one = lax.ppermute(one, axes, b_one)
    two = lax.ppermute(two, axes, b_two)
    (cross,) = call(cross_kernel, [one_tile], m, flow_one, flow_two)
    part, done = call(border_kernel, [state.shape, one_tile], pack, delta, land_mask, part, flops=LONG)
    rest_one, rest_two = call(rest_kernel, [(lay.rest, LANES)] * 2, m, delta, cross)
    rest_one = lax.ppermute(rest_one, axes, b_one)
    rest_two = lax.ppermute(rest_two, axes, b_two)
    basis, sent = call(
        functools.partial(moment_kernel, levels=lay.levels),
        [((ITERS + 1) * ROWS, LANES), (nb * ng, LANES)],
        flat,
        own,
        near,
        cross,
        flow_one,
        flow_two,
        one,
        two,
        done,
        scratch=[(FLAT * 3 * ROWS, 2 * LANES)],
        flops=LONG,
    )
    got = lax.all_to_all(sent, axes, 0, 0, tiled=True)
    new_state, surface = call(
        solve_kernel,
        [state.shape, one_tile],
        got,
        basis,
        m,
        rest_one,
        rest_two,
        land_mask,
        part,
        scratch=[state.shape, one_tile, pltpu.SemaphoreType.DMA((3,))],
        out_specs=[HBM, HBM],
    )
    return new_state.reshape(ocean_state.shape), surface


def solution(mesh):
    placed = (
        P(None, None, "blocks", "group"),
        P("blocks", "group"),
        P("blocks", "group"),
        P("blocks", "group"),
    )
    shape = (mesh.shape["blocks"], mesh.shape["group"])

    def body(*args):
        return on_device(*args, shape=shape)

    return jax.shard_map(
        body,
        mesh=mesh,
        in_specs=placed,
        out_specs=(P(None, None, "blocks", "group"), P("blocks", "group")),
        check_vma=False,
    )
```

```python
import functools

import jax
import jax.numpy as jnp
from jax import lax
from jax.experimental import pallas as pl
from jax.experimental.pallas import tpu as pltpu
from jax.sharding import PartitionSpec as P

ITERS = 3

time_step = 0.25
hyper_visc = 0.025
mixing = 0.2
gravity = 4.0
rotation = 0.2

COMPS = 4
ROWS = 8
LANES = 128
SLOT = 8
PER = LANES // SLOT
FLAT = 6
STRIP = 16
LONG = 10**9
SHIFT = 4.5
PAIRS = [(i, j) for i in range(ITERS) for j in range(i, ITERS + 1)]
F32 = jnp.float32
VMEM = pl.BlockSpec(memory_space=pltpu.VMEM)
HBM = pl.BlockSpec(memory_space=pltpu.HBM)


def iota(axis, rows=ROWS, lanes=LANES):
    return lax.broadcasted_iota(jnp.int32, (rows, lanes), axis)


def roll(x, shift, axis):
    return pltpu.roll(x, shift % x.shape[axis], axis)


def tile(k):
    return pl.ds(k * ROWS, ROWS)


def swap_pairs(mesh_shape, along):
    nb, ng = mesh_shape
    first, second = [], []
    for b in range(nb):
        for g in range(ng):
            me = b * ng + g
            if along == "blocks":
                one = (b ^ 1, g)
                two = ((b - 1) ^ 1) + 1
                two = (two, g) if 0 <= two < nb else (b, g ^ 1)
            else:
                one = (b, g ^ 1)
                two = ((g - 1) ^ 1) + 1
                two = (b, two) if 0 <= two < ng else (b ^ 1, g)
            first.append((me, one[0] * ng + one[1]))
            second.append((me, two[0] * ng + two[1]))
    return first, second


class Layout:
    def __init__(self, tiles):
        self.tiles = tiles
        self.levels = tiles // COMPS
        self.packs = tiles // PER
        self.eights = tiles // ROWS
        self.pad = -(-self.packs // ROWS) * ROWS
        self.flow = -(-self.levels // ROWS) * ROWS
        self.flat = 2 * self.flow
        self.early = self.flat + FLAT * ROWS
        self.edge = 0
        self.strip = self.pad
        self.inner = self.strip + ROWS
        self.message = self.inner + ROWS
        self.delta = 2 * tiles
        self.rest = self.delta + self.pad


class Place:
    def __init__(self):
        self.b, self.nb = lax.axis_index("blocks"), lax.axis_size("blocks")
        self.g, self.ng = lax.axis_index("group"), lax.axis_size("group")
        self.b_even = lax.rem(self.b, 2) == 0
        self.g_even = lax.rem(self.g, 2) == 0
        self.up = (self.b > 0).astype(F32)
        self.down = (self.b < self.nb - 1).astype(F32)
        self.left = (self.g > 0).astype(F32)
        self.right = (self.g < self.ng - 1).astype(F32)

    def from_up(self, one, two):
        return jnp.where(self.b_even, two, one) * self.up

    def from_down(self, one, two):
        return jnp.where(self.b_even, one, two) * self.down


def pack_kernel(
    state_hbm, mask_hbm, height_hbm, damp_hbm, m_ref, pack_ref, flat_ref, state_ref, mask_ref, height_ref, damp_ref, sems
):
    lay = Layout(m_ref.shape[0] // ROWS)
    chunk = PER * ROWS
    small = [(mask_hbm, mask_ref), (height_hbm, height_ref), (damp_hbm, damp_ref)]
    copies = [pltpu.make_async_copy(a, b, sems.at[k]) for k, (a, b) in enumerate(small)]
    for p in range(lay.packs):
        at = pl.ds(p * chunk, chunk)
        copies.append(pltpu.make_async_copy(state_hbm.at[at], state_ref.at[at], sems.at[3 + p]))
    for copy in copies:
        copy.start()
    for copy in copies[: 3 + lay.packs // 2]:
        copy.wait()
    sea = mask_ref[...].astype(F32)
    row, lane = iota(0), iota(1)
    slot = lane // SLOT
    sum_u = sum_v = uu = uv = vu = zero = jnp.zeros((ROWS, LANES), F32)
    across_u = across_v = across_vu = zero
    for p in range(lay.packs):
        if p == lay.packs // 2:
            for copy in copies[3 + p :]:
                copy.wait()
        acc = zero
        for k in range(PER // COMPS):
            x = []
            for c in range(COMPS):
                q = COMPS * k + c
                x.append(state_ref[tile(p * PER + q), :] * sea)
                m_ref[tile(p * PER + q), :] = x[c]
                at = PER - 1 - q
                acc = jnp.where(slot == at, roll(x[c], SLOT * at + SLOT // 2, 1), acc)
            u, v = x[2:]
            below_u, below_v = roll(u, -1, 0), roll(v, -1, 0)
            right_u, right_v = roll(u, -1, 1), roll(v, -1, 1)
            sum_u, sum_v = sum_u + u, sum_v + v
            uu, uv, vu = uu + u * below_u, uv + u * below_v, vu + v * below_u
            across_u, across_v, across_vu = across_u + v * right_u, across_v + v * right_v, across_vu + u * right_v
        pack_ref[tile(p), :] = acc

    def step_down(ahead, back):
        inner = row < ROWS - 1
        return jnp.where(inner, ahead, 0.0) - roll(jnp.where(inner, back, 0.0), 1, 0)

    def step_right(ahead, back):
        inner = lane < LANES - 1
        return jnp.where(inner, ahead, 0.0) - roll(jnp.where(inner, back, 0.0), 1, 1)

    advect_u = 0.5 * (step_down(uu, uu) + step_right(across_u, across_vu))
    advect_v = 0.5 * (step_down(uv, vu) + step_right(across_v, across_v))
    damp = damp_ref[...]
    flat = [sum_u, sum_v, advect_u, advect_v, sea * damp * height_ref[...], sea * (4.0 + damp)]
    acc = jnp.zeros((ROWS, LANES), F32)
    for f in range(FLAT):
        flat_ref[tile(f), :] = flat[f]
        acc = jnp.where(lane // STRIP == f, roll(flat[f], STRIP * f + STRIP // 2, 1), acc)
    pack_ref[tile(lay.packs), :] = acc


def packed_comp(shape):
    return COMPS - 1 - lax.rem(lax.broadcasted_iota(jnp.int32, shape, 1) // SLOT, COMPS)


def unpack(x, t):
    return roll(x, -(SLOT * (PER - 1 - t % PER) + SLOT // 2), 1)


def spread(x, of):
    comp = packed_comp(x.shape)
    out = x
    for c in range(COMPS):
        if c != of:
            out = jnp.where(comp == c, roll(x, SLOT * (of - c), 1), out)
    return out


def across(x):
    half = lax.rem(lax.broadcasted_iota(jnp.int32, x.shape, 1), SLOT) < SLOT // 2
    return jnp.where(half, roll(x, -1, 1), roll(x, 1, 1))


def fold(x):
    step = SLOT * COMPS
    while step < LANES:
        x = x + roll(x, step, 1)
        step *= 2
    return x


def edge_kernel(pack_ref, first_ref, second_ref, done_ref, own_ref, near_ref, delta_ref, one_ref, two_ref):
    lay = Layout((pack_ref.shape[0] // ROWS - 1) * PER)
    at = Place()
    lane = iota(1)
    comp = packed_comp((ROWS, LANES))
    in_slot = lax.rem(lane, SLOT)
    half = in_slot < SLOT // 2
    sign = jnp.where(in_slot == SLOT // 2 - 1, 0.5, jnp.where(in_slot == SLOT // 2, -0.5, 0.0))

    def beyond(p, low):
        first, second = first_ref[tile(p), :], second_ref[tile(p), :]
        from_left = jnp.where(at.g_even, second, first) * at.left
        from_right = jnp.where(at.g_even, first, second) * at.right
        return jnp.where(low, from_left, from_right)

    def flow(x):
        return jnp.where(comp == 2, roll(x, SLOT, 1), x)

    near_ref[...] = jnp.zeros(near_ref.shape, F32)
    inner = jnp.zeros((ROWS, LANES), F32)
    outer = jnp.zeros((ROWS, LANES), F32)
    for p in range(lay.packs):
        own, far = pack_ref[tile(p), :], beyond(p, half)
        delta_ref[tile(p), :] = far - own
        near_ref[p : p + 1, :] = far[0:1]
        near_ref[lay.pad + p : lay.pad + p + 1, :] = far[ROWS - 1 : ROWS]
        inner = inner + flow(own) * across(far)
        outer = outer + flow(far) * across(own)
    inner, outer = fold(sign * inner), fold(sign * outer)
    strip = beyond(lay.packs, lax.rem(lane, STRIP) < STRIP // 2)
    for f in (2, 3):
        mid = STRIP * f + STRIP // 2
        border = (lane == mid - 1) | (lane == mid)
        strip = strip + jnp.where(border, roll(unpack(outer, f), mid, 1), 0.0)
    own_ref[0:ROWS, :] = strip
    own_ref[ROWS : 2 * ROWS, :] = inner

    def fill(low_ref, high_ref):
        for ref, rows in ((low_ref, slice(0, lay.pad)), (high_ref, slice(lay.pad, 2 * lay.pad))):
            ref[pl.ds(lay.edge, lay.pad), :] = near_ref[rows, :]
            ref[pl.ds(lay.strip, ROWS), :] = strip
            ref[pl.ds(lay.inner, ROWS), :] = inner

    pl.when(at.b_even)(lambda: fill(two_ref, one_ref))
    pl.when(jnp.logical_not(at.b_even))(lambda: fill(one_ref, two_ref))


def level_rows(m_ref, comp, row):
    lay = Layout(m_ref.shape[0] // ROWS)
    step = COMPS * ROWS
    parts = []
    for first in range(0, lay.levels, ROWS):
        start = min(first, lay.levels - ROWS)
        x = m_ref[pl.ds(start * step + comp * ROWS + row, ROWS, stride=step), :]
        parts.append(jnp.where(iota(0) < first - start, 0.0, x))
    return parts


def flow_kernel(m_ref, flat_ref, one_ref, two_ref):
    lay = Layout(m_ref.shape[0] // ROWS)

    def fill(low_ref, high_ref):
        for ref, row in ((low_ref, 0), (high_ref, ROWS - 1)):
            for c in range(2):
                for n, x in enumerate(level_rows(m_ref, 2 + c, row)):
                    ref[pl.ds(c * lay.flow + n * ROWS, ROWS), :] = x
            ref[pl.ds(lay.flat, FLAT * ROWS), :] = flat_ref[...]

    even = Place().b_even
    pl.when(even)(lambda: fill(two_ref, one_ref))
    pl.when(jnp.logical_not(even))(lambda: fill(one_ref, two_ref))


def rest_kernel(m_ref, delta_ref, after_ref, one_ref, two_ref):
    lay = Layout(m_ref.shape[0] // ROWS)

    def fill(low_ref, high_ref):
        for ref, row, near in ((low_ref, 0, 0), (high_ref, ROWS - 2, ROWS - 1)):
            for r in range(2):
                for s in range(lay.eights):
                    at = pl.ds(ROWS * ROWS * s + row + r, ROWS, stride=ROWS)
                    ref[tile(r * lay.eights + s), :] = m_ref[at, :]
            ref[pl.ds(lay.delta, lay.pad), :] = jnp.zeros((lay.pad, LANES), F32)
            for p in range(lay.packs):
                ref[pl.ds(lay.delta + p, 1), :] = delta_ref[pl.ds(ROWS * p + near, 1), :]

    even = Place().b_even
    pl.when(even)(lambda: fill(two_ref, one_ref))
    pl.when(jnp.logical_not(even))(lambda: fill(one_ref, two_ref))


def cross_kernel(m_ref, one_ref, two_ref, cross_ref):
    lay = Layout(m_ref.shape[0] // ROWS)
    at = Place()
    row = iota(0)
    count = lay.flow // ROWS

    def beyond(take, c):
        where = [pl.ds(c * lay.flow + n * ROWS, ROWS) for n in range(count)]
        return [take(one_ref[w, :], two_ref[w, :]) for w in where]

    above, below = [[beyond(take, c) for c in range(2)] for take in (at.from_up, at.from_down)]
    top, bottom = [[level_rows(m_ref, c, r) for c in (2, 3)] for r in (0, ROWS - 1)]

    def total(flow, carried):
        return 0.5 * jnp.sum(sum(x * y for x, y in zip(flow, carried)), axis=0, keepdims=True)

    out = jnp.zeros((ROWS, LANES), F32)
    for f in range(2):
        sums = (total(above[0], top[f]), -total(top[0], above[f]), total(bottom[0], below[f]), -total(below[0], bottom[f]))
        for k in range(4):
            out = jnp.where(row == 4 * f + k, sums[k], out)
    cross_ref[...] = out


def moment_kernel(
    flat_ref, own_ref, near_ref, cross_ref, flow_one_ref, flow_two_ref, one_ref, two_ref, done_ref, basis_ref, send_ref, wide_ref, *, levels
):
    lay = Layout(levels * COMPS)
    at = Place()
    row, lane = iota(0), iota(1)
    outside = (lane < STRIP // 2) | (lane >= LANES - STRIP // 2)
    rows = 3 * ROWS

    def neighbours(where, first_ref=one_ref, second_ref=two_ref):
        first, second = first_ref[where, :], second_ref[where, :]
        return at.from_up(first, second), at.from_down(first, second)

    def around(where, own, *refs):
        up, down = neighbours(where, *refs)
        return up, own, down

    strips = around(pl.ds(lay.strip, ROWS), own_ref[0:ROWS, :])
    inners = around(pl.ds(lay.inner, ROWS), own_ref[ROWS : 2 * ROWS, :])
    border = (lane == 0) | (lane == LANES - 1)
    for f in range(FLAT):
        fields = around(pl.ds(lay.flat + f * ROWS, ROWS), flat_ref[tile(f), :], flow_one_ref, flow_two_ref)
        for k in range(3):
            to = pl.ds(f * rows + k * ROWS, ROWS)
            value = fields[k]
            if 2 <= f <= 3:
                value = value + jnp.where(border, unpack(inners[k], f), 0.0)
            wide_ref[to, 0:LANES] = value
            side = roll(strips[k], -(STRIP * f + STRIP // 2), 1)
            wide_ref[to, LANES : 2 * LANES] = jnp.where(outside, side, 0.0)

    above, below = neighbours(pl.ds(lay.edge, lay.pad))
    top, bottom = near_ref[0 : lay.pad, :], near_ref[lay.pad :, :]

    def flow_packed(x):
        return roll(x, -SLOT, 1)

    def corner(a, b):
        x = jnp.where(packed_comp(a.shape) == 3, flow_packed(a), a) * b
        return 0.5 * fold(jnp.sum(x, axis=0, keepdims=True))

    corners = [corner(above, top), -corner(top, above), corner(bottom, below), -corner(below, bottom)]
    border = (iota(1, 1) < SLOT // 2) | (iota(1, 1) >= LANES - SLOT // 2)
    for f in (2, 3):
        for k, at_row in enumerate((ROWS - 1, ROWS, 2 * ROWS - 1, 2 * ROWS)):
            to = pl.ds(f * rows + at_row, 1)
            wide_ref[to, 0:LANES] = wide_ref[to, 0:LANES] + cross_ref[4 * (f - 2) + k : 4 * (f - 2) + k + 1, :]
            side = unpack(corners[k], f)
            wide_ref[to, LANES : 2 * LANES] = wide_ref[to, LANES : 2 * LANES] + jnp.where(border, side, 0.0)

    sum_u, sum_v, adv_u, adv_v, forcing, diagonal = [wide_ref[pl.ds(f * rows, rows), :] for f in range(FLAT)]
    sea = jnp.where(diagonal > 0.0, 1.0, 0.0)
    shape = (rows, 2 * LANES)
    i = iota(0, *shape) - ROWS + at.b * ROWS
    j = iota(1, *shape)
    j = jnp.where(j < LANES + LANES // 2, j, j - 2 * LANES) + at.g * LANES
    total_rows, total_cols = at.nb * ROWS, at.ng * LANES
    edges = (
        jnp.where(i == 0, 1.0, 0.0)
        + jnp.where(i == total_rows - 1, 1.0, 0.0)
        + jnp.where(j == 0, 1.0, 0.0)
        + jnp.where(j == total_cols - 1, 1.0, 0.0)
    )
    coriolis = rotation * (2.0 * (j.astype(F32) + 0.5) / total_cols - 1.0)

    def both(x, n, axis):
        return roll(x, n, axis) + roll(x, -n, axis)

    def transport(x, turn, adv):
        near = both(x, 1, 0)
        linear = (
            (1.0 - hyper_visc * (20.0 - edges)) * x
            + 8.0 * hyper_visc * near
            - hyper_visc * (both(x, 2, 0) + both(x, 2, 1))
            + both(8.0 * hyper_visc * x - 2.0 * hyper_visc * near, 1, 1)
        )
        return sea * (linear + time_step * (turn - adv)) / lay.levels

    east = transport(sum_u, coriolis * sum_v, adv_u)
    north = transport(sum_v, -coriolis * sum_u, adv_v)
    divergence = 0.5 * (roll(east, -1, 0) - roll(east, 1, 0) + roll(north, -1, 1) - roll(north, 1, 1))
    v = [forcing - gravity * sea * divergence]
    own_diagonal = diagonal - SHIFT
    for _ in range(ITERS):
        x = v[-1]
        v.append(own_diagonal * x - sea * (both(x, 1, 0) + both(x, 1, 1)))
    v = [x[ROWS : 2 * ROWS, 0:LANES] for x in v]

    def over_rows(x, y):
        return jnp.sum(x * y, axis=0, keepdims=True)

    norm, slope = [jnp.sum(over_rows(v[0], x), axis=1, keepdims=True) for x in v[:2]]
    theta = jnp.where(norm > 0.0, jnp.clip(slope / jnp.where(norm > 0.0, norm, 1.0), -SHIFT, SHIFT), 0.0)
    q = [v[0]] + [v[k] - theta * v[k - 1] for k in range(1, ITERS + 1)]
    for k in range(ITERS):
        basis_ref[tile(k), :] = q[k]
    basis_ref[tile(ITERS), :] = jnp.broadcast_to(theta, (ROWS, LANES))
    row, lane = iota(0, 2 * ROWS), iota(1, 2 * ROWS)
    line = jnp.zeros((2 * ROWS, LANES), F32)
    for k, (i, j) in enumerate(PAIRS):
        line = jnp.where(row == k, over_rows(q[i], q[j]), line)
    line = jnp.sum(line, axis=1, keepdims=True)
    line = jnp.where(row == len(PAIRS), theta, line)
    line = jnp.sum(jnp.where(row == lane, line, 0.0), axis=0, keepdims=True)
    send_ref[...] = jnp.broadcast_to(line, send_ref.shape)


def solve_kernel(
    got_ref, basis_ref, m_ref, one_ref, two_ref, mask_ref, part_ref, state_hbm, surface_hbm, state_ref, surface_ref, sems
):
    lay = Layout(state_ref.shape[0] // ROWS)
    at = Place()
    place = pl.ds(lay.delta, lay.pad)
    in_slot = lax.rem(iota(1, lay.pad), SLOT)
    comp = lax.rem(iota(0), COMPS)
    border = (iota(1) < SLOT // 2) | (iota(1) >= LANES - SLOT // 2)
    near = (in_slot == SLOT // 2 - 1) | (in_slot == SLOT // 2)
    sea = mask_ref[...].astype(F32)
    sides = ((at.from_up, 1, 0, 0, 1, 0.5 * time_step), (at.from_down, 0, 1, ROWS - 1, ROWS - 2, -0.5 * time_step))
    fixes = [across(-2.0 * hyper_visc * side[0](one_ref[place, :], two_ref[place, :])) for side in sides]
    fixes = [jnp.where(near, x, 0.0) for x in fixes]
    writes = []
    for s in range(lay.eights):
        group = pl.ds(ROWS * ROWS * s, ROWS * ROWS)
        state_ref[group, :] = part_ref[group, :]
        for (take, first, second, row, inner, slope), fix in zip(sides, fixes):
            x1, x2 = [take(one_ref[w, :], two_ref[w, :]) for w in (tile(n * lay.eights + s) for n in (first, second))]
            flow = m_ref[pl.ds(ROWS * ROWS * s + row, ROWS, stride=ROWS), :]
            u = flow
            for c in (0, 1, 3):
                u = jnp.where(comp == c, roll(flow, c - 2, 0), u)
            p, q = divmod(s * ROWS, PER)
            corner = jnp.broadcast_to(fix[p : p + 1], (ROWS, LANES))
            corner = pltpu.roll(corner, SLOT * q + SLOT // 2, 1, stride=SLOT, stride_axis=0)
            more = (
                hyper_visc * (8.0 * x1 - x2 - 2.0 * (roll(x1, 1, 1) + roll(x1, -1, 1)))
                + slope * u * x1
                + jnp.where(border, corner, 0.0)
            )
            to = pl.ds(ROWS * ROWS * s + row, ROWS, stride=ROWS)
            state_ref[to, :] = state_ref[to, :] + sea[row : row + 1] * more
            to = pl.ds(ROWS * ROWS * s + inner, ROWS, stride=ROWS)
            state_ref[to, :] = state_ref[to, :] - (hyper_visc * sea[inner : inner + 1]) * x1
        if s + 1 in (lay.eights // 2, lay.eights):
            start = len(writes) * (lay.eights // 2) * ROWS * ROWS
            part = pl.ds(start, (s + 1) * ROWS * ROWS - start)
            writes.append(pltpu.make_async_copy(state_ref.at[part], state_hbm.at[part], sems.at[len(writes)]))
            writes[-1].start()

    got = got_ref[...]
    gram = {pair: jnp.broadcast_to(got[:, k : k + 1], got.shape) for k, pair in enumerate(PAIRS)}
    theta = jnp.broadcast_to(got[:, len(PAIRS) : len(PAIRS) + 1], got.shape)

    def local(a, theta):
        out = [a[-1]]
        for x in a[-2::-1]:
            out.insert(0, x + theta * out[0])
        return out

    def dot(a, b):
        total = None
        for i, x in enumerate(local(a, theta)):
            part = None
            for j, y in enumerate(local(b, theta)):
                term = y * gram[min(i, j), max(i, j)]
                part = term if part is None else part + term
            total = x * part if total is None else total + x * part
        return jnp.sum(total, axis=0, keepdims=True)

    def add(a, scale, b):
        out = list(a) + [jnp.zeros_like(one)] * (len(b) - len(a))
        return [x + scale * b[n] if n < len(b) else x for n, x in enumerate(out)]

    def image(a):
        return [SHIFT * a[0]] + [SHIFT * a[n] + a[n - 1] for n in range(1, len(a))] + [a[-1]]

    one = jnp.ones((1, LANES), F32)
    residual, direction, surface = [one], [one], []
    norm = dot(residual, residual)
    for iteration in range(ITERS):
        applied = image(direction)
        alpha = norm / dot(direction, applied)
        if iteration:
            alpha = jnp.where(norm > 0.0, alpha, 0.0)
        surface = add(surface, alpha, direction)
        if iteration + 1 < ITERS:
            residual = add(residual, -alpha, applied)
            following = dot(residual, residual)
            ratio = following / norm
            if iteration:
                ratio = jnp.where(norm > 0.0, ratio, 0.0)
            direction = add(residual, ratio, direction)
            norm = following
    out = jnp.zeros((ROWS, LANES), F32)
    for k, x in enumerate(local(surface, basis_ref[tile(ITERS), :])):
        out = out + x * basis_ref[tile(k), :]
    surface_ref[...] = out
    writes.append(pltpu.make_async_copy(surface_ref, surface_hbm, sems.at[len(writes)]))
    writes[-1].start()
    for write in writes:
        write.wait()


def inner_kernel(m_ref, mask_ref, new_ref, done_ref):
    lay = Layout(m_ref.shape[0] // ROWS)
    at = Place()
    row, lane = iota(0), iota(1)
    sea = mask_ref[...].astype(F32)
    done_ref[...] = sea
    edges = (
        jnp.where((row == 0) & (at.b == 0), 1.0, 0.0)
        + jnp.where((row == ROWS - 1) & (at.b == at.nb - 1), 1.0, 0.0)
        + jnp.where((lane == 0) & (at.g == 0), 1.0, 0.0)
        + jnp.where((lane == LANES - 1) & (at.g == at.ng - 1), 1.0, 0.0)
    )
    centre = 1.0 - 2.0 * mixing - hyper_visc * (20.0 - edges)
    col = (lane + at.g * LANES).astype(F32)
    coriolis = time_step * rotation * (2.0 * (col + 0.5) / (at.ng * LANES) - 1.0)

    def own(level, c):
        return m_ref[tile(COMPS * min(max(level, 0), lay.levels - 1) + c), :]

    for k in range(lay.levels):
        u, v = own(k, 2), own(k, 3)
        half_u, half_v = 0.5 * time_step * u, 0.5 * time_step * v
        for c in range(COMPS):
            t = COMPS * k + c
            x = own(k, c)
            up1, dn1 = jnp.where(row == 0, 0.0, roll(x, 1, 0)), jnp.where(row == ROWS - 1, 0.0, roll(x, -1, 0))
            up2, dn2 = jnp.where(row < 2, 0.0, roll(x, 2, 0)), jnp.where(row >= ROWS - 2, 0.0, roll(x, -2, 0))
            left, right = roll(x, 1, 1), roll(x, -1, 1)
            near1 = up1 + dn1
            q = 8.0 * hyper_visc * x - 2.0 * hyper_visc * near1
            out = (
                centre * x
                + (roll(q, 1, 1) + roll(q, -1, 1))
                + 8.0 * hyper_visc * near1
                - hyper_visc * ((up2 + dn2) + (roll(x, 2, 1) + roll(x, -2, 1)))
                - (half_u * (dn1 - up1) + half_v * (right - left))
                + mixing * (own(k - 1, c) + own(k + 1, c))
            )
            if c == 2:
                out = out + coriolis * v
            if c == 3:
                out = out - coriolis * u
            new_ref[tile(t), :] = sea * out


def border_kernel(pack_ref, delta_ref, mask_ref, part_ref, state_ref, done_ref):
    lay = Layout(state_ref.shape[0] // ROWS)
    lane = iota(1)
    border = (lane < SLOT // 2) | (lane >= LANES - SLOT // 2)
    sea = mask_ref[...].astype(F32)
    sea = jnp.where(border, sea, 0.0)
    done_ref[...] = sea
    d = delta_ref[...]
    row, in_slot = lax.rem(iota(0, d.shape[0]), ROWS), lax.rem(iota(1, d.shape[0]), SLOT)
    mid = SLOT // 2
    near = (in_slot == mid - 1) | (in_slot == mid)
    far = (in_slot >= mid - 2) & (in_slot <= mid + 1)
    sign = jnp.where(in_slot == mid - 1, -0.5 * time_step, jnp.where(in_slot == mid, 0.5 * time_step, 0.0))
    dv = jnp.where(row == 0, 0.0, roll(d, 1, 0)) + jnp.where(row == ROWS - 1, 0.0, roll(d, -1, 0))
    second = jnp.where(in_slot < mid, roll(d, -2, 1), roll(d, 2, 1))
    fix = (
        jnp.where(far, -hyper_visc * second, 0.0)
        + jnp.where(near, across(hyper_visc * (8.0 * d - 2.0 * dv)), 0.0)
        + sign * spread(pack_ref[0 : d.shape[0], :], 3) * across(d)
    )
    for t in range(lay.tiles):
        p = t // PER
        state_ref[tile(t), :] = part_ref[tile(t), :] + sea * unpack(fix[p * ROWS : (p + 1) * ROWS], t)


def call(kernel, outs, *args, scratch=(), specs=None, out_specs=None, flops=0):
    return pl.pallas_call(
        kernel,
        out_shape=[jax.ShapeDtypeStruct(s, F32) for s in outs],
        in_specs=specs or [VMEM] * len(args),
        out_specs=out_specs or [VMEM] * len(outs),
        scratch_shapes=[pltpu.VMEM(s, F32) if isinstance(s, tuple) else s for s in scratch],
        compiler_params=pltpu.CompilerParams(vmem_limit_bytes=8 * 1024 * 1024),
        cost_estimate=pl.CostEstimate(flops=flops, bytes_accessed=0, transcendentals=0),
    )(*args)


def on_device(ocean_state, surface_height, surface_damping, land_mask, *, shape):
    nb, ng = shape
    axes = ("blocks", "group")
    state = ocean_state.reshape(-1, LANES)
    lay = Layout(state.shape[0] // ROWS)
    g_one, g_two = swap_pairs(shape, "group")
    b_one, b_two = swap_pairs(shape, "blocks")
    one_tile = (ROWS, LANES)
    packed = (lay.packs * ROWS, LANES)
    flats = (FLAT * ROWS, LANES)

    m, pack, flat = call(
        pack_kernel,
        [state.shape, (packed[0] + ROWS, LANES), flats],
        *[pltpu.with_memory_space_constraint(x, pltpu.HBM) for x in (state, land_mask, surface_height, surface_damping)],
        specs=[HBM] * 4,
        scratch=[
            state.shape,
            pltpu.VMEM(one_tile, land_mask.dtype),
            one_tile,
            one_tile,
            pltpu.SemaphoreType.DMA((3 + lay.packs,)),
        ],
    )
    first = lax.ppermute(pack, axes, g_one)
    second = lax.ppermute(pack, axes, g_two)
    flow_one, flow_two = call(flow_kernel, [(lay.early, LANES)] * 2, m, flat)
    flow_one = lax.ppermute(flow_one, axes, b_one)
    flow_two = lax.ppermute(flow_two, axes, b_two)
    part, inner_done = call(inner_kernel, [state.shape, one_tile], m, land_mask, flops=LONG)
    message = (lay.message, LANES)
    own, near, delta, one, two = call(
        edge_kernel,
        [(2 * ROWS, LANES), (2 * lay.pad, LANES), packed, message, message],
        pack,
        first,
        second,
        inner_done,
        flops=10 * LONG,
    )
    one = lax.ppermute(one, axes, b_one)
    two = lax.ppermute(two, axes, b_two)
    (cross,) = call(cross_kernel, [one_tile], m, flow_one, flow_two)
    part, done = call(border_kernel, [state.shape, one_tile], pack, delta, land_mask, part, flops=LONG)
    rest_one, rest_two = call(rest_kernel, [(lay.rest, LANES)] * 2, m, delta, cross)
    rest_one = lax.ppermute(rest_one, axes, b_one)
    rest_two = lax.ppermute(rest_two, axes, b_two)
    basis, sent = call(
        functools.partial(moment_kernel, levels=lay.levels),
        [((ITERS + 1) * ROWS, LANES), (nb * ng, LANES)],
        flat,
        own,
        near,
        cross,
        flow_one,
        flow_two,
        one,
        two,
        done,
        scratch=[(FLAT * 3 * ROWS, 2 * LANES)],
        flops=LONG,
    )
    got = lax.all_to_all(sent, axes, 0, 0, tiled=True)
    new_state, surface = call(
        solve_kernel,
        [state.shape, one_tile],
        got,
        basis,
        m,
        rest_one,
        rest_two,
        land_mask,
        part,
        scratch=[state.shape, one_tile, pltpu.SemaphoreType.DMA((3,))],
        out_specs=[HBM, HBM],
    )
    return new_state.reshape(ocean_state.shape), surface


def solution(mesh):
    placed = (
        P(None, None, "blocks", "group"),
        P("blocks", "group"),
        P("blocks", "group"),
        P("blocks", "group"),
    )
    shape = (mesh.shape["blocks"], mesh.shape["group"])

    def body(*args):
        return on_device(*args, shape=shape)

    return jax.shard_map(
        body,
        mesh=mesh,
        in_specs=placed,
        out_specs=(P(None, None, "blocks", "group"), P("blocks", "group")),
        check_vma=False,
    )
```

```python
import functools

import jax
import jax.numpy as jnp
from jax import lax
from jax.experimental import pallas as pl
from jax.experimental.pallas import tpu as pltpu
from jax.sharding import PartitionSpec as P

ITERS = 3

time_step = 0.25
hyper_visc = 0.025
mixing = 0.2
gravity = 4.0
rotation = 0.2

COMPS = 4
ROWS = 8
LANES = 128
SLOT = 8
PER = LANES // SLOT
FLAT = 6
STRIP = 16
LONG = 10**9
SHIFT = 4.5
PAIRS = [(i, j) for i in range(ITERS) for j in range(i, ITERS + 1)]
F32 = jnp.float32
VMEM = pl.BlockSpec(memory_space=pltpu.VMEM)
HBM = pl.BlockSpec(memory_space=pltpu.HBM)


def iota(axis, rows=ROWS, lanes=LANES):
    return lax.broadcasted_iota(jnp.int32, (rows, lanes), axis)


def roll(x, shift, axis):
    return pltpu.roll(x, shift % x.shape[axis], axis)


def tile(k):
    return pl.ds(k * ROWS, ROWS)


def swap_pairs(mesh_shape, along):
    nb, ng = mesh_shape
    first, second = [], []
    for b in range(nb):
        for g in range(ng):
            me = b * ng + g
            if along == "blocks":
                one = (b ^ 1, g)
                two = ((b - 1) ^ 1) + 1
                two = (two, g) if 0 <= two < nb else (b, g ^ 1)
            else:
                one = (b, g ^ 1)
                two = ((g - 1) ^ 1) + 1
                two = (b, two) if 0 <= two < ng else (b ^ 1, g)
            first.append((me, one[0] * ng + one[1]))
            second.append((me, two[0] * ng + two[1]))
    return first, second


class Layout:
    def __init__(self, tiles):
        self.tiles = tiles
        self.levels = tiles // COMPS
        self.packs = tiles // PER
        self.eights = tiles // ROWS
        self.pad = -(-self.packs // ROWS) * ROWS
        self.flow = -(-self.levels // ROWS) * ROWS
        self.flat = 2 * self.flow
        self.early = self.flat + FLAT * ROWS
        self.edge = 0
        self.strip = self.pad
        self.inner = self.strip + ROWS
        self.message = self.inner + ROWS
        self.delta = 2 * tiles
        self.rest = self.delta + self.pad


class Place:
    def __init__(self):
        self.b, self.nb = lax.axis_index("blocks"), lax.axis_size("blocks")
        self.g, self.ng = lax.axis_index("group"), lax.axis_size("group")
        self.b_even = lax.rem(self.b, 2) == 0
        self.g_even = lax.rem(self.g, 2) == 0
        self.up = (self.b > 0).astype(F32)
        self.down = (self.b < self.nb - 1).astype(F32)
        self.left = (self.g > 0).astype(F32)
        self.right = (self.g < self.ng - 1).astype(F32)

    def from_up(self, one, two):
        return jnp.where(self.b_even, two, one) * self.up

    def from_down(self, one, two):
        return jnp.where(self.b_even, one, two) * self.down


def pack_kernel(
    state_hbm, mask_hbm, height_hbm, damp_hbm, m_ref, pack_ref, flat_ref, state_ref, mask_ref, height_ref, damp_ref, sems
):
    lay = Layout(m_ref.shape[0] // ROWS)
    chunk = PER * ROWS
    small = [(mask_hbm, mask_ref), (height_hbm, height_ref), (damp_hbm, damp_ref)]
    copies = [pltpu.make_async_copy(a, b, sems.at[k]) for k, (a, b) in enumerate(small)]
    for p in range(lay.packs):
        at = pl.ds(p * chunk, chunk)
        copies.append(pltpu.make_async_copy(state_hbm.at[at], state_ref.at[at], sems.at[3 + p]))
    for copy in copies:
        copy.start()
    for copy in copies[: 3 + lay.packs // 2]:
        copy.wait()
    sea = mask_ref[...].astype(F32)
    row, lane = iota(0), iota(1)
    slot = lane // SLOT
    sum_u = sum_v = uu = uv = vu = zero = jnp.zeros((ROWS, LANES), F32)
    across_u = across_v = across_vu = zero
    for p in range(lay.packs):
        if p == lay.packs // 2:
            for copy in copies[3 + p :]:
                copy.wait()
        acc = zero
        for k in range(PER // COMPS):
            x = []
            for c in range(COMPS):
                q = COMPS * k + c
                x.append(state_ref[tile(p * PER + q), :] * sea)
                m_ref[tile(p * PER + q), :] = x[c]
                at = PER - 1 - q
                acc = jnp.where(slot == at, roll(x[c], SLOT * at + SLOT // 2, 1), acc)
            u, v = x[2:]
            below_u, below_v = roll(u, -1, 0), roll(v, -1, 0)
            right_u, right_v = roll(u, -1, 1), roll(v, -1, 1)
            sum_u, sum_v = sum_u + u, sum_v + v
            uu, uv, vu = uu + u * below_u, uv + u * below_v, vu + v * below_u
            across_u, across_v, across_vu = across_u + v * right_u, across_v + v * right_v, across_vu + u * right_v
        pack_ref[tile(p), :] = acc

    def step_down(ahead, back):
        inner = row < ROWS - 1
        return jnp.where(inner, ahead, 0.0) - roll(jnp.where(inner, back, 0.0), 1, 0)

    def step_right(ahead, back):
        inner = lane < LANES - 1
        return jnp.where(inner, ahead, 0.0) - roll(jnp.where(inner, back, 0.0), 1, 1)

    advect_u = 0.5 * (step_down(uu, uu) + step_right(across_u, across_vu))
    advect_v = 0.5 * (step_down(uv, vu) + step_right(across_v, across_v))
    damp = damp_ref[...]
    flat = [sum_u, sum_v, advect_u, advect_v, sea * damp * height_ref[...], sea * (4.0 + damp)]
    acc = jnp.zeros((ROWS, LANES), F32)
    for f in range(FLAT):
        flat_ref[tile(f), :] = flat[f]
        acc = jnp.where(lane // STRIP == f, roll(flat[f], STRIP * f + STRIP // 2, 1), acc)
    pack_ref[tile(lay.packs), :] = acc


def packed_comp(shape):
    return COMPS - 1 - lax.rem(lax.broadcasted_iota(jnp.int32, shape, 1) // SLOT, COMPS)


def unpack(x, t):
    return roll(x, -(SLOT * (PER - 1 - t % PER) + SLOT // 2), 1)


def spread(x, of):
    comp = packed_comp(x.shape)
    out = x
    for c in range(COMPS):
        if c != of:
            out = jnp.where(comp == c, roll(x, SLOT * (of - c), 1), out)
    return out


def across(x):
    half = lax.rem(lax.broadcasted_iota(jnp.int32, x.shape, 1), SLOT) < SLOT // 2
    return jnp.where(half, roll(x, -1, 1), roll(x, 1, 1))


def fold(x):
    step = SLOT * COMPS
    while step < LANES:
        x = x + roll(x, step, 1)
        step *= 2
    return x


def edge_kernel(pack_ref, first_ref, second_ref, done_ref, own_ref, near_ref, delta_ref, one_ref, two_ref):
    lay = Layout((pack_ref.shape[0] // ROWS - 1) * PER)
    at = Place()
    lane = iota(1)
    comp = packed_comp((ROWS, LANES))
    in_slot = lax.rem(lane, SLOT)
    half = in_slot < SLOT // 2
    sign = jnp.where(in_slot == SLOT // 2 - 1, 0.5, jnp.where(in_slot == SLOT // 2, -0.5, 0.0))

    def beyond(p, low):
        first, second = first_ref[tile(p), :], second_ref[tile(p), :]
        from_left = jnp.where(at.g_even, second, first) * at.left
        from_right = jnp.where(at.g_even, first, second) * at.right
        return jnp.where(low, from_left, from_right)

    def flow(x):
        return jnp.where(comp == 2, roll(x, SLOT, 1), x)

    near_ref[...] = jnp.zeros(near_ref.shape, F32)
    inner = jnp.zeros((ROWS, LANES), F32)
    outer = jnp.zeros((ROWS, LANES), F32)
    for p in range(lay.packs):
        own, far = pack_ref[tile(p), :], beyond(p, half)
        delta_ref[tile(p), :] = far - own
        near_ref[p : p + 1, :] = far[0:1]
        near_ref[lay.pad + p : lay.pad + p + 1, :] = far[ROWS - 1 : ROWS]
        inner = inner + flow(own) * across(far)
        outer = outer + flow(far) * across(own)
    inner, outer = fold(sign * inner), fold(sign * outer)
    strip = beyond(lay.packs, lax.rem(lane, STRIP) < STRIP // 2)
    for f in (2, 3):
        mid = STRIP * f + STRIP // 2
        border = (lane == mid - 1) | (lane == mid)
        strip = strip + jnp.where(border, roll(unpack(outer, f), mid, 1), 0.0)
    own_ref[0:ROWS, :] = strip
    own_ref[ROWS : 2 * ROWS, :] = inner

    low, high = near_ref[0 : lay.pad, :], near_ref[lay.pad :, :]
    one_ref[pl.ds(lay.edge, lay.pad), :] = jnp.where(at.b_even, high, low)
    two_ref[pl.ds(lay.edge, lay.pad), :] = jnp.where(at.b_even, low, high)
    for ref in (one_ref, two_ref):
        ref[pl.ds(lay.strip, ROWS), :] = strip
        ref[pl.ds(lay.inner, ROWS), :] = inner


def level_rows(m_ref, comp, row):
    lay = Layout(m_ref.shape[0] // ROWS)
    step = COMPS * ROWS
    parts = []
    for first in range(0, lay.levels, ROWS):
        start = min(first, lay.levels - ROWS)
        x = m_ref[pl.ds(start * step + comp * ROWS + row, ROWS, stride=step), :]
        parts.append(jnp.where(iota(0) < first - start, 0.0, x))
    return parts


def flow_kernel(m_ref, flat_ref, one_ref, two_ref):
    lay = Layout(m_ref.shape[0] // ROWS)

    def fill(low_ref, high_ref):
        for ref, row in ((low_ref, 0), (high_ref, ROWS - 1)):
            for c in range(2):
                for n, x in enumerate(level_rows(m_ref, 2 + c, row)):
                    ref[pl.ds(c * lay.flow + n * ROWS, ROWS), :] = x
            ref[pl.ds(lay.flat, FLAT * ROWS), :] = flat_ref[...]

    even = Place().b_even
    pl.when(even)(lambda: fill(two_ref, one_ref))
    pl.when(jnp.logical_not(even))(lambda: fill(one_ref, two_ref))


def rest_kernel(m_ref, delta_ref, after_ref, one_ref, two_ref):
    lay = Layout(m_ref.shape[0] // ROWS)

    def fill(low_ref, high_ref):
        for ref, row, near in ((low_ref, 0, 0), (high_ref, ROWS - 2, ROWS - 1)):
            for r in range(2):
                for s in range(lay.eights):
                    at = pl.ds(ROWS * ROWS * s + row + r, ROWS, stride=ROWS)
                    ref[tile(r * lay.eights + s), :] = m_ref[at, :]
            ref[pl.ds(lay.delta, lay.pad), :] = jnp.zeros((lay.pad, LANES), F32)
            for p in range(lay.packs):
                ref[pl.ds(lay.delta + p, 1), :] = delta_ref[pl.ds(ROWS * p + near, 1), :]

    even = Place().b_even
    pl.when(even)(lambda: fill(two_ref, one_ref))
    pl.when(jnp.logical_not(even))(lambda: fill(one_ref, two_ref))


def cross_kernel(m_ref, one_ref, two_ref, cross_ref):
    lay = Layout(m_ref.shape[0] // ROWS)
    at = Place()
    row = iota(0)
    count = lay.flow // ROWS

    def beyond(take, c):
        where = [pl.ds(c * lay.flow + n * ROWS, ROWS) for n in range(count)]
        return [take(one_ref[w, :], two_ref[w, :]) for w in where]

    above, below = [[beyond(take, c) for c in range(2)] for take in (at.from_up, at.from_down)]
    top, bottom = [[level_rows(m_ref, c, r) for c in (2, 3)] for r in (0, ROWS - 1)]

    def total(flow, carried):
        return 0.5 * jnp.sum(sum(x * y for x, y in zip(flow, carried)), axis=0, keepdims=True)

    out = jnp.zeros((ROWS, LANES), F32)
    for f in range(2):
        sums = (total(above[0], top[f]), -total(top[0], above[f]), total(bottom[0], below[f]), -total(below[0], bottom[f]))
        for k in range(4):
            out = jnp.where(row == 4 * f + k, sums[k], out)
    cross_ref[...] = out


def moment_kernel(
    flat_ref, own_ref, near_ref, cross_ref, flow_one_ref, flow_two_ref, one_ref, two_ref, done_ref, basis_ref, send_ref, wide_ref, *, levels
):
    lay = Layout(levels * COMPS)
    at = Place()
    row, lane = iota(0), iota(1)
    outside = (lane < STRIP // 2) | (lane >= LANES - STRIP // 2)
    rows = 3 * ROWS

    def neighbours(where, first_ref=one_ref, second_ref=two_ref):
        first, second = first_ref[where, :], second_ref[where, :]
        return at.from_up(first, second), at.from_down(first, second)

    def around(where, own, *refs):
        up, down = neighbours(where, *refs)
        return up, own, down

    strips = around(pl.ds(lay.strip, ROWS), own_ref[0:ROWS, :])
    inners = around(pl.ds(lay.inner, ROWS), own_ref[ROWS : 2 * ROWS, :])
    border = (lane == 0) | (lane == LANES - 1)
    for f in range(FLAT):
        fields = around(pl.ds(lay.flat + f * ROWS, ROWS), flat_ref[tile(f), :], flow_one_ref, flow_two_ref)
        for k in range(3):
            to = pl.ds(f * rows + k * ROWS, ROWS)
            value = fields[k]
            if 2 <= f <= 3:
                value = value + jnp.where(border, unpack(inners[k], f), 0.0)
            wide_ref[to, 0:LANES] = value
            side = roll(strips[k], -(STRIP * f + STRIP // 2), 1)
            wide_ref[to, LANES : 2 * LANES] = jnp.where(outside, side, 0.0)

    above, below = neighbours(pl.ds(lay.edge, lay.pad))
    top, bottom = near_ref[0 : lay.pad, :], near_ref[lay.pad :, :]

    def flow_packed(x):
        return roll(x, -SLOT, 1)

    def corner(a, b):
        x = jnp.where(packed_comp(a.shape) == 3, flow_packed(a), a) * b
        return 0.5 * fold(jnp.sum(x, axis=0, keepdims=True))

    corners = [corner(above, top), -corner(top, above), corner(bottom, below), -corner(below, bottom)]
    border = (iota(1, 1) < SLOT // 2) | (iota(1, 1) >= LANES - SLOT // 2)
    for f in (2, 3):
        for k, at_row in enumerate((ROWS - 1, ROWS, 2 * ROWS - 1, 2 * ROWS)):
            to = pl.ds(f * rows + at_row, 1)
            wide_ref[to, 0:LANES] = wide_ref[to, 0:LANES] + cross_ref[4 * (f - 2) + k : 4 * (f - 2) + k + 1, :]
            side = unpack(corners[k], f)
            wide_ref[to, LANES : 2 * LANES] = wide_ref[to, LANES : 2 * LANES] + jnp.where(border, side, 0.0)

    sum_u, sum_v, adv_u, adv_v, forcing, diagonal = [wide_ref[pl.ds(f * rows, rows), :] for f in range(FLAT)]
    sea = jnp.where(diagonal > 0.0, 1.0, 0.0)
    shape = (rows, 2 * LANES)
    i = iota(0, *shape) - ROWS + at.b * ROWS
    j = iota(1, *shape)
    j = jnp.where(j < LANES + LANES // 2, j, j - 2 * LANES) + at.g * LANES
    total_rows, total_cols = at.nb * ROWS, at.ng * LANES
    edges = (
        jnp.where(i == 0, 1.0, 0.0)
        + jnp.where(i == total_rows - 1, 1.0, 0.0)
        + jnp.where(j == 0, 1.0, 0.0)
        + jnp.where(j == total_cols - 1, 1.0, 0.0)
    )
    coriolis = rotation * (2.0 * (j.astype(F32) + 0.5) / total_cols - 1.0)

    def both(x, n, axis):
        return roll(x, n, axis) + roll(x, -n, axis)

    def transport(x, turn, adv):
        near = both(x, 1, 0)
        linear = (
            (1.0 - hyper_visc * (20.0 - edges)) * x
            + 8.0 * hyper_visc * near
            - hyper_visc * (both(x, 2, 0) + both(x, 2, 1))
            + both(8.0 * hyper_visc * x - 2.0 * hyper_visc * near, 1, 1)
        )
        return sea * (linear + time_step * (turn - adv)) / lay.levels

    east = transport(sum_u, coriolis * sum_v, adv_u)
    north = transport(sum_v, -coriolis * sum_u, adv_v)
    divergence = 0.5 * (roll(east, -1, 0) - roll(east, 1, 0) + roll(north, -1, 1) - roll(north, 1, 1))
    v = [forcing - gravity * sea * divergence]
    own_diagonal = diagonal - SHIFT
    for _ in range(ITERS - 1):
        x = v[-1]
        v.append(own_diagonal * x - sea * (both(x, 1, 0) + both(x, 1, 1)))
    x, middle = v[-1], slice(ROWS, 2 * ROWS)
    beside = both(x[:, 0:LANES], 1, 0)[middle] + both(x[middle], 1, 1)[:, 0:LANES]
    v = [x[middle, 0:LANES] for x in v]
    v.append(own_diagonal[middle, 0:LANES] * v[-1] - sea[middle, 0:LANES] * beside)

    def over_rows(x, y):
        return jnp.sum(x * y, axis=0, keepdims=True)

    norm, slope = [jnp.sum(over_rows(v[0], x), axis=1, keepdims=True) for x in v[:2]]
    theta = jnp.where(norm > 0.0, jnp.clip(slope / jnp.where(norm > 0.0, norm, 1.0), -SHIFT, SHIFT), 0.0)
    q = [v[0]] + [v[k] - theta * v[k - 1] for k in range(1, ITERS + 1)]
    for k in range(ITERS):
        basis_ref[tile(k), :] = q[k]
    basis_ref[tile(ITERS), :] = jnp.broadcast_to(theta, (ROWS, LANES))
    row, lane = iota(0, 2 * ROWS), iota(1, 2 * ROWS)
    line = jnp.zeros((2 * ROWS, LANES), F32)
    for k, (i, j) in enumerate(PAIRS):
        line = jnp.where(row == k, over_rows(q[i], q[j]), line)
    line = jnp.sum(line, axis=1, keepdims=True)
    line = jnp.where(row == len(PAIRS), theta, line)
    line = jnp.sum(jnp.where(row == lane, line, 0.0), axis=0, keepdims=True)
    send_ref[...] = jnp.broadcast_to(line, send_ref.shape)


def solve_kernel(
    got_ref, basis_ref, m_ref, one_ref, two_ref, mask_ref, part_ref, state_hbm, surface_hbm, state_ref, surface_ref, sems
):
    lay = Layout(state_ref.shape[0] // ROWS)
    at = Place()
    place = pl.ds(lay.delta, lay.pad)
    in_slot = lax.rem(iota(1, lay.pad), SLOT)
    comp = lax.rem(iota(0), COMPS)
    border = (iota(1) < SLOT // 2) | (iota(1) >= LANES - SLOT // 2)
    near = (in_slot == SLOT // 2 - 1) | (in_slot == SLOT // 2)
    sea = mask_ref[...].astype(F32)
    sides = ((at.from_up, 1, 0, 0, 1, 0.5 * time_step), (at.from_down, 0, 1, ROWS - 1, ROWS - 2, -0.5 * time_step))
    fixes = [across(-2.0 * hyper_visc * side[0](one_ref[place, :], two_ref[place, :])) for side in sides]
    fixes = [jnp.where(near, x, 0.0) for x in fixes]
    writes = []
    for s in range(lay.eights):
        group = pl.ds(ROWS * ROWS * s, ROWS * ROWS)
        state_ref[group, :] = part_ref[group, :]
        for (take, first, second, row, inner, slope), fix in zip(sides, fixes):
            x1, x2 = [take(one_ref[w, :], two_ref[w, :]) for w in (tile(n * lay.eights + s) for n in (first, second))]
            flow = m_ref[pl.ds(ROWS * ROWS * s + row, ROWS, stride=ROWS), :]
            u = flow
            for c in (0, 1, 3):
                u = jnp.where(comp == c, roll(flow, c - 2, 0), u)
            p, q = divmod(s * ROWS, PER)
            corner = jnp.broadcast_to(fix[p : p + 1], (ROWS, LANES))
            corner = pltpu.roll(corner, SLOT * q + SLOT // 2, 1, stride=SLOT, stride_axis=0)
            more = (
                hyper_visc * (8.0 * x1 - x2 - 2.0 * (roll(x1, 1, 1) + roll(x1, -1, 1)))
                + slope * u * x1
                + jnp.where(border, corner, 0.0)
            )
            to = pl.ds(ROWS * ROWS * s + row, ROWS, stride=ROWS)
            state_ref[to, :] = state_ref[to, :] + sea[row : row + 1] * more
            to = pl.ds(ROWS * ROWS * s + inner, ROWS, stride=ROWS)
            state_ref[to, :] = state_ref[to, :] - (hyper_visc * sea[inner : inner + 1]) * x1
        if s + 1 in (lay.eights // 2, lay.eights):
            start = len(writes) * (lay.eights // 2) * ROWS * ROWS
            part = pl.ds(start, (s + 1) * ROWS * ROWS - start)
            writes.append(pltpu.make_async_copy(state_ref.at[part], state_hbm.at[part], sems.at[len(writes)]))
            writes[-1].start()

    got = got_ref[...]
    gram = {pair: jnp.broadcast_to(got[:, k : k + 1], got.shape) for k, pair in enumerate(PAIRS)}
    theta = jnp.broadcast_to(got[:, len(PAIRS) : len(PAIRS) + 1], got.shape)

    def local(a, theta):
        out = [a[-1]]
        for x in a[-2::-1]:
            out.insert(0, x + theta * out[0])
        return out

    def dot(a, b):
        total = None
        for i, x in enumerate(local(a, theta)):
            part = None
            for j, y in enumerate(local(b, theta)):
                term = y * gram[min(i, j), max(i, j)]
                part = term if part is None else part + term
            total = x * part if total is None else total + x * part
        return jnp.sum(total, axis=0, keepdims=True)

    def add(a, scale, b):
        out = list(a) + [jnp.zeros_like(one)] * (len(b) - len(a))
        return [x + scale * b[n] if n < len(b) else x for n, x in enumerate(out)]

    def image(a):
        return [SHIFT * a[0]] + [SHIFT * a[n] + a[n - 1] for n in range(1, len(a))] + [a[-1]]

    one = jnp.ones((1, LANES), F32)
    residual, direction, surface = [one], [one], []
    norm = dot(residual, residual)
    for iteration in range(ITERS):
        applied = image(direction)
        alpha = norm / dot(direction, applied)
        if iteration:
            alpha = jnp.where(norm > 0.0, alpha, 0.0)
        surface = add(surface, alpha, direction)
        if iteration + 1 < ITERS:
            residual = add(residual, -alpha, applied)
            following = dot(residual, residual)
            ratio = following / norm
            if iteration:
                ratio = jnp.where(norm > 0.0, ratio, 0.0)
            direction = add(residual, ratio, direction)
            norm = following
    out = jnp.zeros((ROWS, LANES), F32)
    for k, x in enumerate(local(surface, basis_ref[tile(ITERS), :])):
        out = out + x * basis_ref[tile(k), :]
    surface_ref[...] = out
    writes.append(pltpu.make_async_copy(surface_ref, surface_hbm, sems.at[len(writes)]))
    writes[-1].start()
    for write in writes:
        write.wait()


def inner_kernel(m_ref, mask_ref, new_ref, done_ref):
    lay = Layout(m_ref.shape[0] // ROWS)
    at = Place()
    row, lane = iota(0), iota(1)
    sea = mask_ref[...].astype(F32)
    done_ref[...] = sea
    edges = (
        jnp.where((row == 0) & (at.b == 0), 1.0, 0.0)
        + jnp.where((row == ROWS - 1) & (at.b == at.nb - 1), 1.0, 0.0)
        + jnp.where((lane == 0) & (at.g == 0), 1.0, 0.0)
        + jnp.where((lane == LANES - 1) & (at.g == at.ng - 1), 1.0, 0.0)
    )
    centre = 1.0 - 2.0 * mixing - hyper_visc * (20.0 - edges)
    col = (lane + at.g * LANES).astype(F32)
    coriolis = time_step * rotation * (2.0 * (col + 0.5) / (at.ng * LANES) - 1.0)

    def own(level, c):
        return m_ref[tile(COMPS * min(max(level, 0), lay.levels - 1) + c), :]

    for k in range(lay.levels):
        u, v = own(k, 2), own(k, 3)
        half_u, half_v = 0.5 * time_step * u, 0.5 * time_step * v
        for c in range(COMPS):
            t = COMPS * k + c
            x = own(k, c)
            up1, dn1 = jnp.where(row == 0, 0.0, roll(x, 1, 0)), jnp.where(row == ROWS - 1, 0.0, roll(x, -1, 0))
            up2, dn2 = jnp.where(row < 2, 0.0, roll(x, 2, 0)), jnp.where(row >= ROWS - 2, 0.0, roll(x, -2, 0))
            left, right = roll(x, 1, 1), roll(x, -1, 1)
            near1 = up1 + dn1
            q = 8.0 * hyper_visc * x - 2.0 * hyper_visc * near1
            out = (
                centre * x
                + (roll(q, 1, 1) + roll(q, -1, 1))
                + 8.0 * hyper_visc * near1
                - hyper_visc * ((up2 + dn2) + (roll(x, 2, 1) + roll(x, -2, 1)))
                - (half_u * (dn1 - up1) + half_v * (right - left))
                + mixing * (own(k - 1, c) + own(k + 1, c))
            )
            if c == 2:
                out = out + coriolis * v
            if c == 3:
                out = out - coriolis * u
            new_ref[tile(t), :] = sea * out


def border_kernel(pack_ref, delta_ref, mask_ref, part_ref, state_ref, done_ref):
    lay = Layout(state_ref.shape[0] // ROWS)
    lane = iota(1)
    border = (lane < SLOT // 2) | (lane >= LANES - SLOT // 2)
    sea = mask_ref[...].astype(F32)
    sea = jnp.where(border, sea, 0.0)
    done_ref[...] = sea
    d = delta_ref[...]
    row, in_slot = lax.rem(iota(0, d.shape[0]), ROWS), lax.rem(iota(1, d.shape[0]), SLOT)
    mid = SLOT // 2
    near = (in_slot == mid - 1) | (in_slot == mid)
    far = (in_slot >= mid - 2) & (in_slot <= mid + 1)
    sign = jnp.where(in_slot == mid - 1, -0.5 * time_step, jnp.where(in_slot == mid, 0.5 * time_step, 0.0))
    dv = jnp.where(row == 0, 0.0, roll(d, 1, 0)) + jnp.where(row == ROWS - 1, 0.0, roll(d, -1, 0))
    second = jnp.where(in_slot < mid, roll(d, -2, 1), roll(d, 2, 1))
    fix = (
        jnp.where(far, -hyper_visc * second, 0.0)
        + jnp.where(near, across(hyper_visc * (8.0 * d - 2.0 * dv)), 0.0)
        + sign * spread(pack_ref[0 : d.shape[0], :], 3) * across(d)
    )
    for t in range(lay.tiles):
        p = t // PER
        state_ref[tile(t), :] = part_ref[tile(t), :] + sea * unpack(fix[p * ROWS : (p + 1) * ROWS], t)


def call(kernel, outs, *args, scratch=(), specs=None, out_specs=None, flops=0):
    return pl.pallas_call(
        kernel,
        out_shape=[jax.ShapeDtypeStruct(s, F32) for s in outs],
        in_specs=specs or [VMEM] * len(args),
        out_specs=out_specs or [VMEM] * len(outs),
        scratch_shapes=[pltpu.VMEM(s, F32) if isinstance(s, tuple) else s for s in scratch],
        compiler_params=pltpu.CompilerParams(vmem_limit_bytes=8 * 1024 * 1024),
        cost_estimate=pl.CostEstimate(flops=flops, bytes_accessed=0, transcendentals=0),
    )(*args)


def on_device(ocean_state, surface_height, surface_damping, land_mask, *, shape):
    nb, ng = shape
    axes = ("blocks", "group")
    state = ocean_state.reshape(-1, LANES)
    lay = Layout(state.shape[0] // ROWS)
    g_one, g_two = swap_pairs(shape, "group")
    b_one, b_two = swap_pairs(shape, "blocks")
    ends = (0, nb - 1)
    f_two = [(i, j if i // ng not in ends else (nb - 1 - i // ng) * ng + i % ng) for i, j in b_two]
    one_tile = (ROWS, LANES)
    packed = (lay.packs * ROWS, LANES)
    flats = (FLAT * ROWS, LANES)

    m, pack, flat = call(
        pack_kernel,
        [state.shape, (packed[0] + ROWS, LANES), flats],
        *[pltpu.with_memory_space_constraint(x, pltpu.HBM) for x in (state, land_mask, surface_height, surface_damping)],
        specs=[HBM] * 4,
        scratch=[
            state.shape,
            pltpu.VMEM(one_tile, land_mask.dtype),
            one_tile,
            one_tile,
            pltpu.SemaphoreType.DMA((3 + lay.packs,)),
        ],
    )
    first = lax.ppermute(pack, axes, g_one)
    second = lax.ppermute(pack, axes, g_two)
    flow_one, flow_two = call(flow_kernel, [(lay.early, LANES)] * 2, m, flat)
    flow_one = lax.ppermute(flow_one, axes, b_one)
    flow_two = lax.ppermute(flow_two, axes, f_two)
    part, inner_done = call(inner_kernel, [state.shape, one_tile], m, land_mask, flops=LONG)
    message = (lay.message, LANES)
    own, near, delta, one, two = call(
        edge_kernel,
        [(2 * ROWS, LANES), (2 * lay.pad, LANES), packed, message, message],
        pack,
        first,
        second,
        inner_done,
        flops=10 * LONG,
    )
    one = lax.ppermute(one, axes, b_one)
    two = lax.ppermute(two, axes, b_two)
    (cross,) = call(cross_kernel, [one_tile], m, flow_one, flow_two)
    part, done = call(border_kernel, [state.shape, one_tile], pack, delta, land_mask, part, flops=LONG)
    rest_one, rest_two = call(rest_kernel, [(lay.rest, LANES)] * 2, m, delta, cross)
    rest_one = lax.ppermute(rest_one, axes, b_one)
    rest_two = lax.ppermute(rest_two, axes, b_two)
    basis, sent = call(
        functools.partial(moment_kernel, levels=lay.levels),
        [((ITERS + 1) * ROWS, LANES), (nb * ng, LANES)],
        flat,
        own,
        near,
        cross,
        flow_one,
        flow_two,
        one,
        two,
        done,
        scratch=[(FLAT * 3 * ROWS, 2 * LANES)],
        flops=LONG,
    )
    got = lax.all_to_all(sent, axes, 0, 0, tiled=True)
    new_state, surface = call(
        solve_kernel,
        [state.shape, one_tile],
        got,
        basis,
        m,
        rest_one,
        rest_two,
        land_mask,
        part,
        scratch=[state.shape, one_tile, pltpu.SemaphoreType.DMA((3,))],
        out_specs=[HBM, HBM],
    )
    return new_state.reshape(ocean_state.shape), surface


def solution(mesh):
    placed = (
        P(None, None, "blocks", "group"),
        P("blocks", "group"),
        P("blocks", "group"),
        P("blocks", "group"),
    )
    shape = (mesh.shape["blocks"], mesh.shape["group"])

    def body(*args):
        return on_device(*args, shape=shape)

    return jax.shard_map(
        body,
        mesh=mesh,
        in_specs=placed,
        out_specs=(P(None, None, "blocks", "group"), P("blocks", "group")),
        check_vma=False,
    )
```
